128 devices in a mesh: section: 2 (over core), tensor: 16 (over x, z), ctx: 4 (over y).
Axes of the slice: x: 4, y: 4, z: 4, core: 2. Of those that a mesh axis runs over, the one named last changes fastest.
Arguments:
- inputs: bfloat16 [2, 4, 1024, 1024], P(None, 'ctx', 'tensor'), may hold values from -6 to 6
- segments: int32 [2, 4096], replicated, may hold values from 0 to 2, as said below
- gain_one: bfloat16 [2, 1024], P('section'), may hold values from 0.5 to 1.5
- bias_one: bfloat16 [2, 1024], P('section'), may hold values from -1.1953125 to 1.1953125
- w_qkv: bfloat16 [2, 1024, 3, 1024], P('section', None, None, 'tensor'), may hold values from -0.1875 to 0.1875
- b_qv: bfloat16 [2, 2, 1024], P('section', None, 'tensor'), may hold values from -1.1953125 to 1.1953125
- w_out: bfloat16 [2, 1024, 1024], P('section', 'tensor'), may hold values from -0.75 to 0.75
- b_out: bfloat16 [2, 1024], P('section'), may hold values from -1.1953125 to 1.1953125
- gain_two: bfloat16 [2, 1024], P('section'), may hold values from 0.5 to 1.5
- bias_two: bfloat16 [2, 1024], P('section'), may hold values from -1.1953125 to 1.1953125
- w_up: bfloat16 [2, 1024, 4096], P('section', None, 'tensor'), may hold values from -0.1875 to 0.1875
- b_up: bfloat16 [2, 4096], P('section', 'tensor'), may hold values from -1.1953125 to 1.1953125
- w_down: bfloat16 [2, 4096, 1024], P('section', 'tensor'), may hold values from -0.09375 to 0.09375
- b_down: bfloat16 [2, 1024], P('section'), may hold values from -1.1953125 to 1.1953125
- cotangent: bfloat16 [2, 4, 1024, 1024], P(None, 'ctx', 'tensor'), may hold values from -6 to 6
Outputs:
- boundary: float32 [2, 2, 4, 1024, 1024], P('section', None, 'ctx', 'tensor')
- grad_gain_one: float32 [2, 1024], P('section')
- grad_bias_one: float32 [2, 1024], P('section')
- grad_w_qkv: float32 [2, 1024, 3, 1024], P('section', None, None, 'tensor')
- grad_b_qv: float32 [2, 2, 1024], P('section', None, 'tensor')
- grad_w_out: float32 [2, 1024, 1024], P('section', 'tensor')
- grad_b_out: float32 [2, 1024], P('section')
- grad_gain_two: float32 [2, 1024], P('section')
- grad_bias_two: float32 [2, 1024], P('section')
- grad_w_up: float32 [2, 1024, 4096], P('section', None, 'tensor')
- grad_b_up: float32 [2, 4096], P('section', 'tensor')
- grad_w_down: float32 [2, 4096, 1024], P('section', 'tensor')
- grad_b_down: float32 [2, 1024], P('section')
The draws below stay inside these ranges and needn't reach their ends.
Inputs may be any that keep to these rules, and one draw needn't show every extreme that they name: `segments`: in each sequence the numbers start at 0, never fall and end at 2; every document has at least 200 tokens, and document 1 begins in the first block and ends in the last.
All inputs are finite; a program needn't handle non-finite values.
Results may differ from the reference program's by a relative error of at most 0.02.
Values may be sent and summed in bfloat16 or wider, within the bound.
No kernel may reach another device: no remote copies, remote signals or barrier semaphores. Data moves between devices by JAX's collectives and lax.ppermute only.
A program may use at most 192 MiB of HBM per device.

```python
import jax
import jax.numpy as jnp
from jax import lax

D = 1024
HEADS = 16
HEAD_DIM = 64
FF = 4096
BLOCK = 1024
MICRO = 2
MIN_DOC = 200
BLOCKS = 4
LENGTH = 4096
SECTIONS = 2


def draw_segments(key, part):
    key = jax.random.fold_in(key, 11)
    head_key, tail_key = jax.random.split(key)
    first_end = jax.random.randint(head_key, (MICRO, 1), MIN_DOC, BLOCK)
    last_start = BLOCK * BLOCKS - jax.random.randint(tail_key, (MICRO, 1), MIN_DOC, BLOCK)
    places = jnp.arange(BLOCK * BLOCKS)[None, :]
    return (places >= first_end).astype(jnp.int32) + (places >= last_start).astype(jnp.int32)


def levels(key, shape, cuts, least, top_value):
    loudness, own = 1.0, jax.random.fold_in(key, 6)
    for dim, parts in cuts:
        steps = jnp.exp(jax.random.uniform(jax.random.fold_in(own, dim), (parts,), jnp.float32, least / len(cuts), top_value / len(cuts)))
        loudness = loudness * jnp.repeat(steps, shape[dim] // parts).reshape([-1 if axis == dim else 1 for axis in range(len(shape))])
    return loudness


def normal_values(key, extent, deviation, most, cuts=(), held_as=jnp.bfloat16):
    entries = deviation * jax.random.normal(key, extent, jnp.float32)
    if cuts:
        entries = entries * levels(key, extent, cuts, -0.22, 0.18)
    return jnp.clip(entries, -most, most).astype(held_as)


def setup_inputs(seed: int = 0) -> dict:
    seeds = jax.random.split(jax.random.key(seed), 16)
    inputs = normal_values(seeds[0], (MICRO, BLOCKS, BLOCK, D), 1.0, 6.0, ((1, 4), (2, 16)))
    segments = draw_segments(jax.random.fold_in(seeds[15], 71), 0)
    gain_one = jnp.clip(1.0 + 0.1 * jax.random.normal(seeds[2], (SECTIONS, D), jnp.float32), 0.5, 1.5).astype(jnp.bfloat16)
    bias_one = normal_values(seeds[3], (SECTIONS, D), 0.2, 1.1953125, ((0, 2),))
    w_qkv = normal_values(seeds[4], (SECTIONS, D, 3, D), D ** -0.5, 0.1875, ((0, 2), (3, 16)))
    b_qv = normal_values(seeds[5], (SECTIONS, 2, D), 0.2, 1.1953125, ((0, 2), (2, 16)))
    w_out = normal_values(seeds[6], (SECTIONS, D, D), (D // 16) ** -0.5, 0.75, ((0, 2), (1, 16)))
    b_out = normal_values(seeds[7], (SECTIONS, D), 0.2, 1.1953125, ((0, 2),))
    gain_two = jnp.clip(1.0 + 0.1 * jax.random.normal(seeds[8], (SECTIONS, D), jnp.float32), 0.5, 1.5).astype(jnp.bfloat16)
    bias_two = normal_values(seeds[9], (SECTIONS, D), 0.2, 1.1953125, ((0, 2),))
    w_up = normal_values(seeds[10], (SECTIONS, D, FF), D ** -0.5, 0.1875, ((0, 2), (2, 16)))
    b_up = normal_values(seeds[11], (SECTIONS, FF), 0.2, 1.1953125, ((0, 2), (1, 16)))
    w_down = normal_values(seeds[12], (SECTIONS, FF, D), FF ** -0.5, 0.09375, ((0, 2), (1, 16)))
    b_down = normal_values(seeds[13], (SECTIONS, D), 0.2, 1.1953125, ((0, 2),))
    cotangent = normal_values(seeds[14], (MICRO, BLOCKS, BLOCK, D), 1.0, 6.0, ((1, 4), (2, 16)))
    return {"inputs": inputs, "segments": segments, "gain_one": gain_one, "bias_one": bias_one, "w_qkv": w_qkv, "b_qv": b_qv, "w_out": w_out, "b_out": b_out, "gain_two": gain_two, "bias_two": bias_two, "w_up": w_up, "b_up": b_up, "w_down": w_down, "b_down": b_down, "cotangent": cotangent}


EPSILON = 1e-05
SCORE_SCALE = 0.125
MASK_FILL = -1e+30

@jax.custom_vjp
def low(v):
    return lax.optimization_barrier(v.astype(jnp.bfloat16)).astype(jnp.float32)

@jax.custom_vjp
def low_back(v):
    return v

def low_keep(v):
    return (low(v), None)

def low_pass(kept, grad):
    return (grad,)

def back_keep(v):
    return (v, None)

def back_low(kept, grad):
    return (low(grad),)
low.defvjp(low_keep, low_pass)
low_back.defvjp(back_keep, back_low)

def layer_norm(values, gain, bias):
    center = values - lax.optimization_barrier(jnp.mean(values, axis=-1, keepdims=True))
    spread = lax.optimization_barrier(jnp.mean(center * center, axis=-1, keepdims=True))
    return center * lax.rsqrt(spread + EPSILON) * gain + bias

def precise_dot(left, right):
    return jnp.dot(left, right, precision=lax.Precision.HIGHEST)

def layer(residual, segment_ids, params):
    gain_one, bias_one, w_qkv, b_qv, w_out, b_out, gain_two, bias_two, w_up, b_up, w_down, b_down = params
    length = residual.shape[0]
    normed = low(layer_norm(residual, gain_one, bias_one))
    queries = low(low_back(precise_dot(normed, w_qkv[:, 0, :]) + b_qv[0]))
    key_rows = low(low_back(precise_dot(normed, w_qkv[:, 1, :])))
    value_rows = low(low_back(precise_dot(normed, w_qkv[:, 2, :]) + b_qv[1]))
    queries = queries.reshape(length, HEADS, HEAD_DIM)
    key_rows = key_rows.reshape(length, HEADS, HEAD_DIM)
    value_rows = value_rows.reshape(length, HEADS, HEAD_DIM)
    scores = jnp.einsum('qhd,khd->hqk', queries, key_rows, precision=lax.Precision.HIGHEST) * SCORE_SCALE
    scores = low_back(scores)
    places = jnp.arange(length)
    allowed = (segment_ids[:, None] == segment_ids[None, :]) & (places[:, None] >= places[None, :])
    scores = jnp.where(allowed[None], scores, MASK_FILL)
    probs_low = low(jax.nn.softmax(scores, axis=-1))
    mixed_heads = jnp.einsum('hqk,khd->qhd', probs_low, value_rows, precision=lax.Precision.HIGHEST).reshape(length, D)
    mixed_heads = low(low_back(mixed_heads))
    attn_out = low_back(precise_dot(mixed_heads, w_out) + b_out)
    hidden = residual + attn_out
    normed_two = low(layer_norm(hidden, gain_two, bias_two))
    up_value = low_back(precise_dot(normed_two, w_up) + b_up)
    activated = low(jax.nn.gelu(up_value))
    down_value = low_back(precise_dot(activated, w_down) + b_down)
    return hidden + down_value

def reference(inputs, segments, gain_one, bias_one, w_qkv, b_qv, w_out, b_out, gain_two, bias_two, w_up, b_up, w_down, b_down, cotangent):
    weights = tuple((param.astype(jnp.float32) for param in (gain_one, bias_one, w_qkv, b_qv, w_out, b_out, gain_two, bias_two, w_up, b_up, w_down, b_down)))
    flat_inputs = inputs.astype(jnp.float32).reshape(MICRO, LENGTH, D)

    def forward(flat_values, *layer_params):

        def one_sequence(sequence):
            residual, segment_ids = sequence
            for section_number in range(SECTIONS):
                if section_number > 0:
                    residual = low(low_back(residual))
                residual = layer(residual, segment_ids, tuple((param[section_number] for param in layer_params)))
            return residual
        return lax.map(jax.checkpoint(one_sequence), (flat_values, segments))
    result, pull_back = jax.vjp(forward, flat_inputs, *weights)
    gradients = pull_back(cotangent.astype(jnp.float32).reshape(MICRO, LENGTH, D))
    boundary = jnp.stack([gradients[0], result]).reshape(SECTIONS, MICRO, BLOCKS, BLOCK, D)
    return (boundary,) + tuple(gradients[1:])
```

```python
import functools
import math

import jax
import jax.numpy as jnp
from jax import lax
from jax.experimental import pallas as pl
from jax.experimental.pallas import tpu as pltpu
from jax.sharding import PartitionSpec as P

HEAD_DIM = 64
EPSILON = 1e-05
MASK_FILL = -1e30
BASE_TWO_SCALE = 0.125 * math.log2(math.e)
SIDE = 4
TILE = 256
LOW = jnp.bfloat16
FULL = jnp.float32


def move_z(block, distance):
    route = [
        (x * SIDE + z, x * SIDE + (z + distance) % SIDE) for x in range(SIDE) for z in range(SIDE)
    ]
    return lax.ppermute(block, "tensor", route)


def move_x(block, distance):
    route = [
        (x * SIDE + z, (x + distance) % SIDE * SIDE + z) for x in range(SIDE) for z in range(SIDE)
    ]
    return lax.ppermute(block, "tensor", route)


def move_y(block, distance):
    return lax.ppermute(block, "ctx", [(y, (y + distance) % SIDE) for y in range(SIDE)])


def move_y_open(block, distance):
    route = [(y, y + distance) for y in range(SIDE) if 0 <= y + distance < SIDE]
    return lax.ppermute(block, "ctx", route)


def move_x_in(block, distance, section):
    base = section * SIDE * SIDE
    route = [
        (base + x * SIDE + z, base + (x + distance) % SIDE * SIDE + z)
        for x in range(SIDE)
        for z in range(SIDE)
    ]
    return lax.ppermute(block, ("section", "tensor"), route)


def move_y_in(block, distance, section):
    base = section * SIDE
    route = [(base + y, base + (y + distance) % SIDE) for y in range(SIDE)]
    return lax.ppermute(block, ("section", "ctx"), route)


def swap(block):
    return lax.ppermute(block, "section", [(0, 1), (1, 0)])


def send_to(block, section):
    return lax.ppermute(block, "section", [(1 - section, section)])


def gather_z(rows):
    return jnp.concatenate([rows] + [move_z(rows, d) for d in range(1, SIDE)], axis=0)


def scatter_z(rows):
    chunks = rows.reshape(SIDE, rows.shape[0] // SIDE, rows.shape[1])
    total = chunks[0].astype(FULL)
    for d in range(1, SIDE):
        total = total + move_z(chunks[d], -d).astype(FULL)
    return total


def even_sum(block, move):
    low = block.astype(FULL)
    return (low + move(block, 2).astype(FULL)) + (
        move(block, 1).astype(FULL) + move(block, 3).astype(FULL)
    )


def layer_norm(values, gain, bias):
    center = values - jnp.mean(values, axis=-1, keepdims=True)
    spread = jnp.mean(center * center, axis=-1, keepdims=True)
    return center * lax.rsqrt(spread + EPSILON) * gain + bias


def local_dot(left, right):
    return jnp.dot(left, right, preferred_element_type=FULL)


def back_dot(left, right):
    return jnp.einsum("rf,df->rd", left, right, preferred_element_type=FULL)


def outer_sum(left, right):
    return jnp.einsum("rd,rf->df", left, right, preferred_element_type=FULL)


def nt_dot(left, right):
    return lax.dot_general(left, right, (((1,), (1,)), ((), ())), preferred_element_type=FULL)


def tn_dot(left, right):
    return lax.dot_general(left, right, (((0,), (0,)), ((), ())), preferred_element_type=FULL)


def attend_kernel(
    block_ref, low_ref, high_ref, key_ref, own_ref, kv1_ref, kv2_ref, kv3_ref, out_ref, peak, total, mixed
):
    block = block_ref[0]
    rows_all = own_ref.shape[0]

    @pl.loop(0, rows_all // TILE)
    def _(index):
        rows = pl.ds(pl.multiple_of(index * TILE, TILE), TILE)
        queries = own_ref[rows, 128:256]
        low = low_ref[rows, :]
        high = high_ref[rows, :]

        def scores(key_values, shift):
            places = key_ref[...] - shift
            raw = nt_dot(queries, key_values)
            allowed = places >= low
            if shift == 0:
                allowed = allowed & (places <= high)
            return jnp.where(allowed, raw, MASK_FILL)

        own = own_ref[:, 0:128]
        raw = scores(own, 0)
        top = jnp.max(raw, axis=1, keepdims=True)
        weight = jnp.exp2((raw - top) * BASE_TWO_SCALE)
        peak[...] = top
        total[...] = jnp.sum(weight, axis=1, keepdims=True)
        mixed[...] = local_dot(weight.astype(LOW), own)
        for d, other_ref in enumerate((kv1_ref, kv2_ref, kv3_ref), 1):

            @pl.when(block >= d)
            def _(d=d, other_ref=other_ref):
                other = other_ref[...]
                raw = scores(other, d * rows_all)
                old = peak[...]
                top = jnp.maximum(old, jnp.max(raw, axis=1, keepdims=True))
                keep = jnp.exp2((old - top) * BASE_TWO_SCALE)
                weight = jnp.exp2((raw - top) * BASE_TWO_SCALE)
                peak[...] = top
                total[...] = total[...] * keep + jnp.sum(weight, axis=1, keepdims=True)
                mixed[...] = mixed[...] * keep + local_dot(weight.astype(LOW), other)

        count = total[...]
        level = peak[...] * BASE_TWO_SCALE + jnp.log2(count)
        lanes = lax.broadcasted_iota(jnp.int32, (TILE, 128), 1)
        out_ref[rows, :] = jnp.where(lanes < HEAD_DIM, level, mixed[...] / count)


def attend_back_kernel(
    block_ref,
    low_ref,
    high_ref,
    key_ref,
    own_ref,
    kv1_ref,
    kv2_ref,
    kv3_ref,
    kept_ref,
    grad_ref,
    dq_ref,
    d0_ref,
    d1_ref,
    d2_ref,
    d3_ref,
    query_sum,
    key_sum,
):
    block = block_ref[0]
    rows_all = own_ref.shape[0]
    for d, (kv_ref, out_ref) in enumerate(
        ((own_ref, d0_ref), (kv1_ref, d1_ref), (kv2_ref, d2_ref), (kv3_ref, d3_ref))
    ):

        @pl.when(block >= d)
        def _(d=d, kv_ref=kv_ref, out_ref=out_ref):
            key_sum[...] = jnp.zeros_like(key_sum)

            @pl.loop(0, rows_all // TILE)
            def _(index):
                rows = pl.ds(pl.multiple_of(index * TILE, TILE), TILE)
                key_values = kv_ref[:, 0:128]
                queries = own_ref[rows, 128:256]
                grad = grad_ref[rows, :]
                kept = kept_ref[rows, :]
                level = kept.T[0:1, :]
                meet = jnp.sum((kept * grad.astype(FULL)).T, axis=0, keepdims=True)
                places = key_ref[...] - d * rows_all
                allowed = places >= low_ref[index]
                if d == 0:
                    allowed = allowed & (places <= high_ref[index])
                raw = nt_dot(key_values, queries)
                probs = jnp.where(allowed, jnp.exp2(raw * BASE_TWO_SCALE - level), 0.0)
                grad_scores = (probs * (nt_dot(key_values, grad) - meet)).astype(LOW)
                key_sum[...] += local_dot(grad_scores, queries) * 0.125 + local_dot(
                    probs.astype(LOW), grad
                )
                part = tn_dot(grad_scores, key_values) * 0.125
                if d == 0:
                    query_sum[rows, :] = part
                else:
                    query_sum[rows, :] += part

            out_ref[...] = key_sum[...].astype(LOW)

        if d > 0:

            @pl.when(block < d)
            def _(out_ref=out_ref):
                out_ref[...] = jnp.zeros_like(out_ref)

    lanes = lax.broadcasted_iota(jnp.int32, dq_ref.shape, 1)
    dq_ref[...] = jnp.where(lanes < HEAD_DIM, query_sum[...], 0.0).astype(LOW)


VMEM_SPEC = pl.BlockSpec(memory_space=pltpu.VMEM)
SMEM_SPEC = pl.BlockSpec(memory_space=pltpu.SMEM)


def attend(spots, own, others):
    rows = own.shape[0]
    return pl.pallas_call(
        attend_kernel,
        out_shape=jax.ShapeDtypeStruct((rows, 128), FULL),
        in_specs=[SMEM_SPEC] + [VMEM_SPEC] * 7,
        out_specs=VMEM_SPEC,
        scratch_shapes=[
            pltpu.VMEM((TILE, 1), FULL),
            pltpu.VMEM((TILE, 1), FULL),
            pltpu.VMEM((TILE, 128), FULL),
        ],
        compiler_params=pltpu.CompilerParams(vmem_limit_bytes=40 << 20),
        cost_estimate=pl.CostEstimate(
            flops=4 * rows * 2 * rows * 128, bytes_accessed=4 << 20, transcendentals=rows * 2 * rows
        ),
        name="attend",
    )(
        spots["block"],
        spots["low"].reshape(rows, 1),
        spots["place"].reshape(rows, 1),
        spots["place"].reshape(1, rows),
        own,
        *others,
    )


def attend_back(spots, own, others, kept, grad):
    rows = own.shape[0]
    tiles = rows // TILE
    return pl.pallas_call(
        attend_back_kernel,
        out_shape=[jax.ShapeDtypeStruct((rows, 128), LOW)] * 5,
        in_specs=[SMEM_SPEC] + [VMEM_SPEC] * 9,
        out_specs=[VMEM_SPEC] * 5,
        scratch_shapes=[pltpu.VMEM((rows, 128), FULL), pltpu.VMEM((rows, 128), FULL)],
        compiler_params=pltpu.CompilerParams(vmem_limit_bytes=40 << 20),
        cost_estimate=pl.CostEstimate(
            flops=10 * rows * 2 * rows * 128, bytes_accessed=6 << 20, transcendentals=rows * 2 * rows
        ),
        name="attend_back",
    )(
        spots["block"],
        spots["low"].reshape(tiles, 1, TILE),
        spots["place"].reshape(tiles, 1, TILE),
        spots["place"].reshape(rows, 1),
        own,
        *others,
        kept,
        grad,
    )


def layer_forward(residual, spots, params):
    (gain_one, bias_one, b_out, gain_two, bias_two, b_down), bias_qkv, b_up, w_qkv, w_out, w_up, w_down = params
    normed = layer_norm(residual, gain_one, bias_one).astype(LOW)
    normed_all = gather_z(normed)
    projected = (local_dot(normed_all, w_qkv) + bias_qkv).astype(LOW)
    width = projected.shape[1] // SIDE
    pieces = [projected[:, d * width : (d + 1) * width] for d in range(SIDE)]
    own = jnp.concatenate([pieces[0]] + [move_x(pieces[d], -d) for d in range(1, SIDE)], axis=0)
    others = [move_y_open(own[:, 0:128], d) for d in range(1, SIDE)]
    kept = attend(spots, own, others)
    lanes = lax.broadcasted_iota(jnp.int32, kept.shape, 1)
    mixed = jnp.where(lanes < HEAD_DIM, 0.0, kept).astype(LOW)
    rows = mixed.shape[0] // SIDE
    mixed_rows = jnp.concatenate(
        [mixed[0:rows]] + [move_x(mixed[d * rows : (d + 1) * rows], d) for d in range(1, SIDE)], axis=1
    )
    hidden = residual + (scatter_z(local_dot(mixed_rows, w_out).astype(LOW)) + b_out)
    normed_two_all = gather_z(layer_norm(hidden, gain_two, bias_two).astype(LOW))
    up_value = local_dot(normed_two_all, w_up) + b_up
    activated = jax.nn.gelu(up_value).astype(LOW)
    result = hidden + (scatter_z(local_dot(activated, w_down).astype(LOW)) + b_down)
    return result, (
        residual, normed_all, own, others, kept, mixed_rows, hidden, normed_two_all, up_value, activated
    )


def layer_backward(grad_out, stored, spots, params, section):
    (gain_one, bias_one, b_out, gain_two, bias_two, b_down), bias_qkv, b_up, w_qkv, w_out, w_up, w_down = params
    residual, normed_all, own, others, kept, mixed_rows, hidden, normed_two_all, up_value, activated = stored
    grad_down = grad_out.astype(LOW)
    g_b_down = jnp.sum(grad_down.astype(FULL), axis=0)
    grad_down_all = gather_z(grad_down)
    _, gelu_pull = jax.vjp(jax.nn.gelu, up_value)
    (grad_up,) = gelu_pull(back_dot(grad_down_all, w_down))
    grad_up = grad_up.astype(LOW)
    grad_normed_two = scatter_z(back_dot(grad_up, w_up).astype(LOW))
    g_w_down = outer_sum(activated, grad_down_all).astype(LOW)
    g_b_up = jnp.sum(grad_up.astype(FULL), axis=0)
    g_w_up = outer_sum(normed_two_all, grad_up).astype(LOW)
    _, norm_two_pull = jax.vjp(layer_norm, hidden, gain_two, bias_two)
    grad_hidden_part, g_gain_two, g_bias_two = norm_two_pull(grad_normed_two)
    grad_hidden = grad_out + grad_hidden_part
    grad_attn = grad_hidden.astype(LOW)
    g_b_out = jnp.sum(grad_attn.astype(FULL), axis=0)
    grad_attn_all = gather_z(grad_attn)
    grad_mixed = back_dot(grad_attn_all, w_out).astype(LOW)
    pieces = [grad_mixed[:, d * 128 : (d + 1) * 128] for d in range(SIDE)]
    grad_mixed_own = jnp.concatenate(
        [pieces[0]] + [move_x(pieces[d], -d) for d in range(1, SIDE)], axis=0
    )
    g_w_out = outer_sum(mixed_rows, grad_attn_all).astype(LOW)
    dq, dkv0, dkv1, dkv2, dkv3 = attend_back(spots, own, others, kept, grad_mixed_own)
    dkv = dkv0.astype(FULL)
    for d, part in enumerate((dkv1, dkv2, dkv3), 1):
        dkv = dkv + move_y_open(part, -d).astype(FULL)
    grad_own = jnp.concatenate([dkv.astype(LOW), dq], axis=1)
    rows = grad_own.shape[0] // SIDE
    grad_qkv = jnp.concatenate(
        [grad_own[0:rows]] + [move_x(grad_own[d * rows : (d + 1) * rows], d) for d in range(1, SIDE)],
        axis=1,
    )
    grad_normed = scatter_z(back_dot(grad_qkv, w_qkv).astype(LOW))
    g_w_qkv = outer_sum(normed_all, grad_qkv).astype(LOW)
    g_b_qkv = jnp.sum(grad_qkv.astype(FULL), axis=0)
    _, norm_one_pull = jax.vjp(layer_norm, residual, gain_one, bias_one)
    grad_residual_part, g_gain_one, g_bias_one = norm_one_pull(grad_normed)
    grad_residual = grad_hidden + grad_residual_part
    vectors = jnp.stack([g_gain_one, g_bias_one, g_b_out, g_gain_two, g_bias_two, g_b_down])
    split = jnp.concatenate([g_b_up.reshape(SIDE, TILE), g_b_qkv.reshape(SIDE, TILE)], axis=1)
    w_out_rows = g_w_out.reshape(SIDE, 2, HEAD_DIM, -1)[:, 1].reshape(SIDE * HEAD_DIM, -1)
    weights = (
        settle(g_w_qkv, 1, section),
        settle(w_out_rows, 0, section),
        settle(g_w_up, 1, section),
        settle(g_w_down, 0, section),
    )
    return grad_residual, vectors, split, weights


def settle(grads, axis, section):
    both = (grads.astype(FULL) + send_to(grads, section).astype(FULL)).astype(LOW)
    pieces = jnp.split(both, SIDE, axis=axis)
    total = pieces[0].astype(FULL)
    for d in range(1, SIDE):
        total = total + move_x_in(pieces[d], -d, section).astype(FULL)
    return even_sum(total.astype(LOW), lambda block, d: move_y_in(block, d, section))


def collect(shard, axis, section, here, pad=None):
    pieces = [shard] + [move_x_in(shard, d, section) for d in range(1, SIDE)]
    if pad is not None:
        pieces = [part for piece in pieces for part in (pad, piece)]
    whole = jnp.concatenate(pieces, axis=axis)
    return jnp.where(here == section, whole, send_to(whole, 1 - section))


def per_device(
    inputs,
    segments,
    gain_one,
    bias_one,
    w_qkv,
    b_qv,
    w_out,
    b_out,
    gain_two,
    bias_two,
    w_up,
    b_up,
    w_down,
    b_down,
    cotangent,
):
    here = lax.axis_index("section")
    block = lax.axis_index("ctx")
    spot = lax.axis_index("tensor")
    x_here, z_here = spot // SIDE, spot % SIDE
    row_count, model_width = inputs.shape[2], inputs.shape[3]
    block_rows = row_count * SIDE * SIDE

    sequence = lax.dynamic_index_in_dim(inputs, here, 0, False)[0].astype(FULL)
    grad_last = lax.dynamic_index_in_dim(cotangent, here, 0, False)[0].astype(FULL)
    segment_ids = lax.dynamic_index_in_dim(segments, here, 0, False)
    start_one = jnp.sum((segment_ids < 1).astype(jnp.int32))
    start_two = jnp.sum((segment_ids < 2).astype(jnp.int32))
    order = jnp.arange(block_rows)
    from_x = (x_here + order // (block_rows // SIDE)) % SIDE
    from_z = (z_here - order // row_count % SIDE) % SIDE
    place = block * block_rows + (from_x * SIDE + from_z) * row_count + order % row_count
    low = jnp.where(place >= start_two, start_two, jnp.where(place >= start_one, start_one, 0))
    spots = {
        "block": block.reshape(1).astype(jnp.int32),
        "place": place.astype(jnp.int32),
        "low": low.astype(jnp.int32),
    }

    gap = jnp.zeros((HEAD_DIM,), LOW)
    small = jnp.concatenate(
        [gain_one, bias_one, b_out, gain_two, bias_two, b_down]
        + [
            jnp.concatenate(
                [b_up[0], gap, b_qv[0, 1], b_qv[0, 0], gap, jnp.zeros((model_width - 512,), LOW)]
            )[None],
            jnp.zeros((1, model_width), LOW),
        ],
        axis=0,
    )
    small_other = swap(small)
    smalls = (
        jnp.where(here == 0, small, small_other),
        jnp.where(here == 0, small_other, small),
    )
    split_own = jnp.stack([smalls[0][6, :512], smalls[1][6, :512]])
    split_all = [split_own] + [move_x(split_own, d) for d in range(1, SIDE)]
    w_kvq = jnp.concatenate(
        [w_qkv[0, :, 1], w_qkv[0, :, 2], w_qkv[0, :, 0], jnp.zeros((model_width, HEAD_DIM), LOW)],
        axis=1,
    )
    gap_rows = jnp.zeros((HEAD_DIM, model_width), LOW)
    params = []
    for section in range(2):
        vectors = tuple(smalls[section][row].astype(FULL) for row in range(6))
        bias_up = jnp.concatenate([part[section, 0:256] for part in split_all]).astype(FULL)
        bias_qkv = jnp.concatenate([part[section, 256:512] for part in split_all]).astype(FULL)
        params.append(
            (
                vectors,
                bias_qkv,
                bias_up,
                collect(w_kvq, 1, section, here),
                collect(w_out[0], 0, section, here, gap_rows),
                collect(w_up[0], 1, section, here),
                collect(w_down[0], 0, section, here),
            )
        )

    middle, stored_first = layer_forward(sequence, spots, params[0])
    result, stored_last = layer_forward(middle.astype(LOW).astype(FULL), spots, params[1])
    grad_middle, vectors_last, split_last, weights_last = layer_backward(
        grad_last, stored_last, spots, params[1], 1
    )
    grad_first, vectors_first, split_first, weights_first = layer_backward(
        grad_middle.astype(LOW).astype(FULL), stored_first, spots, params[0], 0
    )

    passed = swap(jnp.where(here == 0, result, grad_first))
    kept = jnp.where(here == 0, grad_first, result)
    boundary = jnp.where(here == 0, jnp.stack([kept, passed]), jnp.stack([passed, kept]))
    boundary = boundary.reshape(1, 2, 1, row_count, model_width)

    pad = jnp.zeros((2, model_width), FULL)
    mine = jnp.where(here == 0, vectors_first, vectors_last)
    theirs = jnp.where(here == 0, vectors_last, vectors_first)
    split_mine = jnp.where(here == 0, split_first, split_last)
    split_theirs = jnp.where(here == 0, split_last, split_first)
    sent = jnp.concatenate([theirs, split_theirs.reshape(2, -1)], axis=0)
    arrived = swap(sent)
    vectors = mine + arrived[:6]
    split = split_mine + arrived[6:].reshape(split_mine.shape)
    vectors = even_sum(vectors, move_z)
    packs = [
        jnp.concatenate(
            [vectors, jnp.pad(split[d], (0, model_width - 512))[None], jnp.zeros((1, model_width), FULL)],
            axis=0,
        )
        for d in range(SIDE)
    ]
    pack = (packs[0] + move_x(packs[2], -2)) + (move_x(packs[1], -1) + move_x(packs[3], -3))
    pack = even_sum(pack, move_y)

    def pick(index):
        return jnp.where(here == 0, weights_first[index], weights_last[index])

    g_kvq = pick(0)
    g_w_qkv = jnp.stack([g_kvq[:, 128:192], g_kvq[:, 0:64], g_kvq[:, 64:128]], axis=1)
    g_b_qv = jnp.stack([pack[6, 384:448], pack[6, 320:384]])
    return (
        boundary,
        pack[0:1],
        pack[1:2],
        g_w_qkv[None],
        g_b_qv[None],
        pick(1)[None],
        pack[2:3],
        pack[3:4],
        pack[4:5],
        pick(2)[None],
        pack[6:7, 0:256],
        pick(3)[None],
        pack[5:6],
    )


def solution(mesh):
    return jax.shard_map(
        per_device,
        mesh=mesh,
        in_specs=(
            P(None, "ctx", "tensor", None),
            P(),
            P("section", None),
            P("section", None),
            P("section", None, None, "tensor"),
            P("section", None, "tensor"),
            P("section", "tensor", None),
            P("section", None),
            P("section", None),
            P("section", None),
            P("section", None, "tensor"),
            P("section", "tensor"),
            P("section", "tensor", None),
            P("section", None),
            P(None, "ctx", "tensor", None),
        ),
        out_specs=(
            P("section", None, "ctx", "tensor", None),
            P("section", None),
            P("section", None),
            P("section", None, None, "tensor"),
            P("section", None, "tensor"),
            P("section", "tensor", None),
            P("section", None),
            P("section", None),
            P("section", None),
            P("section", None, "tensor"),
            P("section", "tensor"),
            P("section", "tensor", None),
            P("section", None),
        ),
        check_vma=False,
    )
```

```python
import functools
import math

import jax
import jax.numpy as jnp
from jax import lax
from jax.experimental import pallas as pl
from jax.experimental.pallas import tpu as pltpu
from jax.sharding import PartitionSpec as P

HEAD_DIM = 64
EPSILON = 1e-05
MASK_FILL = -1e30
BASE_TWO_SCALE = 0.125 * math.log2(math.e)
SIDE = 4
TILE = 256
LN_TWO = math.log(2.0)
LOW = jnp.bfloat16
FULL = jnp.float32


def move_z(block, distance):
    route = [
        (x * SIDE + z, x * SIDE + (z + distance) % SIDE) for x in range(SIDE) for z in range(SIDE)
    ]
    return lax.ppermute(block, "tensor", route)


def move_x(block, distance):
    route = [
        (x * SIDE + z, (x + distance) % SIDE * SIDE + z) for x in range(SIDE) for z in range(SIDE)
    ]
    return lax.ppermute(block, "tensor", route)


def move_y(block, distance):
    return lax.ppermute(block, "ctx", [(y, (y + distance) % SIDE) for y in range(SIDE)])


def move_y_open(block, distance):
    route = [(y, y + distance) for y in range(SIDE) if 0 <= y + distance < SIDE]
    return lax.ppermute(block, "ctx", route)


def move_x_in(block, distance, section):
    base = section * SIDE * SIDE
    route = [
        (base + x * SIDE + z, base + (x + distance) % SIDE * SIDE + z)
        for x in range(SIDE)
        for z in range(SIDE)
    ]
    return lax.ppermute(block, ("section", "tensor"), route)


def move_y_in(block, distance, section):
    base = section * SIDE
    route = [(base + y, base + (y + distance) % SIDE) for y in range(SIDE)]
    return lax.ppermute(block, ("section", "ctx"), route)


def swap(block):
    return lax.ppermute(block, "section", [(0, 1), (1, 0)])


def send_to(block, section):
    return lax.ppermute(block, "section", [(1 - section, section)])


def gather_z(rows):
    return jnp.concatenate([rows] + [move_z(rows, d) for d in range(1, SIDE)], axis=0)


def scatter_z(rows):
    chunks = rows.reshape(SIDE, rows.shape[0] // SIDE, rows.shape[1])
    total = chunks[0].astype(FULL)
    for d in range(1, SIDE):
        total = total + move_z(chunks[d], -d).astype(FULL)
    return total


def even_sum(block, move):
    low = block.astype(FULL)
    return (low + move(block, 2).astype(FULL)) + (
        move(block, 1).astype(FULL) + move(block, 3).astype(FULL)
    )


def even_pairs(blocks, move):
    return (blocks[0].astype(FULL) + move(blocks[2], -2).astype(FULL)) + (
        move(blocks[1], -1).astype(FULL) + move(blocks[3], -3).astype(FULL)
    )


def layer_norm(values, gain, bias):
    center = values - jnp.mean(values, axis=-1, keepdims=True)
    spread = jnp.mean(center * center, axis=-1, keepdims=True)
    return center * lax.rsqrt(spread + EPSILON) * gain + bias


def local_dot(left, right):
    return jnp.dot(left, right, preferred_element_type=FULL)


def back_dot(left, right):
    return jnp.einsum("rf,df->rd", left, right, preferred_element_type=FULL)


def outer_sum(left, right):
    return jnp.einsum("rd,rf->df", left, right, preferred_element_type=FULL)


def nt_dot(left, right):
    return lax.dot_general(left, right, (((1,), (1,)), ((), ())), preferred_element_type=FULL)


def tn_dot(left, right):
    return lax.dot_general(left, right, (((0,), (0,)), ((), ())), preferred_element_type=FULL)


def attend_kernel(
    scalar_ref, low_ref, high_ref, key_ref, own_ref, kv1_ref, kv2_ref, kv3_ref, out_ref,
    peak, mixed, held, arrived,
):
    block = scalar_ref[0]
    rows_all = own_ref.shape[0]
    tiles = rows_all // TILE
    copies = [
        pltpu.make_async_copy(ref, held.at[d], arrived.at[d])
        for d, ref in enumerate((kv1_ref, kv2_ref, kv3_ref))
    ]
    for copy in copies:
        copy.start()
    peak[...] = jnp.full_like(peak, MASK_FILL)
    mixed[...] = jnp.zeros_like(mixed)
    for d in range(SIDE):
        if d > 0:
            copies[d - 1].wait()
        start = (block - d) * rows_all

        @pl.loop(0, tiles)
        def _(index, d=d, start=start):
            rows = pl.ds(pl.multiple_of(index * TILE, TILE), TILE)
            least, most = scalar_ref[1 + index], scalar_ref[1 + tiles + index]

            def step(masked):
                key_values = own_ref[:, 0:128] if d == 0 else held[d - 1]
                raw = nt_dot(key_values, own_ref[rows, 128:256])
                if masked:
                    places = key_ref[...] - d * rows_all
                    allowed = places >= low_ref[index]
                    if d == 0:
                        allowed = allowed & (places <= high_ref[index])
                    raw = jnp.where(allowed, raw, MASK_FILL)
                old = peak[index]
                top = jnp.maximum(old, jnp.max(raw, axis=0, keepdims=True))
                weight = jnp.exp2(raw - top).astype(LOW)
                lanes = lax.broadcasted_iota(jnp.int32, key_values.shape, 1)
                ones_values = jnp.where(lanes < HEAD_DIM, jnp.ones_like(key_values), key_values)
                peak[index] = top
                mixed[index] = mixed[index] * jnp.exp2(old - top) + tn_dot(ones_values, weight)

            if d == 0:
                step(True)
            else:
                reached = (block >= d) & (least < start + rows_all)
                pl.when(reached & (most <= start))(lambda: step(False))
                pl.when(reached & (most > start))(lambda: step(True))

    @pl.loop(0, tiles)
    def _(index):
        rows = pl.ds(pl.multiple_of(index * TILE, TILE), TILE)
        sums = mixed[index]
        count = sums[0:1, :]
        level = peak[index] + jnp.log2(count)
        lines = lax.broadcasted_iota(jnp.int32, sums.shape, 0)
        out_ref[rows, :] = jnp.where(lines < HEAD_DIM, level, sums / count).T


def attend_back_kernel(
    scalar_ref, low_ref, high_ref, key_ref, own_ref, kv1_ref, kv2_ref, kv3_ref, kept_ref, grad_ref,
    dq_ref, d0_ref, d1_ref, d2_ref, d3_ref,
    query_sum, key_sum, held, arrived,
):
    block = scalar_ref[0]
    rows_all = own_ref.shape[0]
    tiles = rows_all // TILE
    copies = [
        pltpu.make_async_copy(ref, held.at[d], arrived.at[d])
        for d, ref in enumerate((kv1_ref, kv2_ref, kv3_ref))
    ]
    for copy in copies:
        copy.start()
    query_sum[...] = jnp.zeros_like(query_sum)
    for d, out_ref in enumerate((d0_ref, d1_ref, d2_ref, d3_ref)):
        if d > 0:
            copies[d - 1].wait()

        @pl.when(block >= d)
        def _(d=d, out_ref=out_ref):
            start = (block - d) * rows_all
            key_sum[...] = jnp.zeros_like(key_sum)

            @pl.loop(0, tiles)
            def _(index):
                rows = pl.ds(pl.multiple_of(index * TILE, TILE), TILE)
                least, most = scalar_ref[1 + index], scalar_ref[1 + tiles + index]

                def step(masked):
                    queries = own_ref[rows, 128:256]
                    grad = grad_ref[rows, :]
                    kept = kept_ref[rows, :]
                    level = kept.T[0:1, :]
                    meet = jnp.sum((kept * grad.astype(FULL)).T, axis=0, keepdims=True)
                    key_values = own_ref[:, 0:128] if d == 0 else held[d - 1]
                    probs = jnp.exp2(nt_dot(key_values, queries) - level)
                    if masked:
                        places = key_ref[...] - d * rows_all
                        allowed = places >= low_ref[index]
                        if d == 0:
                            allowed = allowed & (places <= high_ref[index])
                        probs = jnp.where(allowed, probs, 0.0)
                    grad_scores = (probs * (nt_dot(key_values, grad) - meet)).astype(LOW)
                    key_sum[...] += local_dot(grad_scores, queries) * LN_TWO + local_dot(
                        probs.astype(LOW), grad
                    )
                    query_sum[rows, :] += tn_dot(grad_scores, key_values)

                if d == 0:
                    step(True)
                else:
                    pl.when(most <= start)(lambda: step(False))
                    pl.when((most > start) & (least < start + rows_all))(lambda: step(True))

            out_ref[...] = key_sum[...].astype(LOW)

        if d > 0:

            @pl.when(block < d)
            def _(out_ref=out_ref):
                out_ref[...] = jnp.zeros_like(out_ref)

    lanes = lax.broadcasted_iota(jnp.int32, dq_ref.shape, 1)
    dq_ref[...] = jnp.where(lanes < HEAD_DIM, query_sum[...] * 0.125, 0.0).astype(LOW)


VMEM_SPEC = pl.BlockSpec(memory_space=pltpu.VMEM)
SMEM_SPEC = pl.BlockSpec(memory_space=pltpu.SMEM)
ANY_SPEC = pl.BlockSpec(memory_space=pl.ANY)


def attend(spots, own, others):
    rows = own.shape[0]
    return pl.pallas_call(
        attend_kernel,
        out_shape=jax.ShapeDtypeStruct((rows, 128), FULL),
        in_specs=[SMEM_SPEC] + [VMEM_SPEC] * 4 + [ANY_SPEC] * 3,
        out_specs=VMEM_SPEC,
        scratch_shapes=[
            pltpu.VMEM((rows // TILE, 1, TILE), FULL),
            pltpu.VMEM((rows // TILE, 128, TILE), FULL),
            pltpu.VMEM((3, rows, 128), LOW),
            pltpu.SemaphoreType.DMA((3,)),
        ],
        compiler_params=pltpu.CompilerParams(vmem_limit_bytes=40 << 20),
        cost_estimate=pl.CostEstimate(
            flops=4 * rows * 2 * rows * 128, bytes_accessed=4 << 20, transcendentals=rows * 2 * rows
        ),
        name="attend",
    )(spots["scalars"], spots["low"], spots["high"], spots["keys"], own, *others)


def attend_back(spots, own, others, kept, grad):
    rows = own.shape[0]
    return pl.pallas_call(
        attend_back_kernel,
        out_shape=[jax.ShapeDtypeStruct((rows, 128), LOW)] * 5,
        in_specs=[SMEM_SPEC] + [VMEM_SPEC] * 4 + [ANY_SPEC] * 3 + [VMEM_SPEC] * 2,
        out_specs=[VMEM_SPEC] * 5,
        scratch_shapes=[
            pltpu.VMEM((rows, 128), FULL),
            pltpu.VMEM((rows, 128), FULL),
            pltpu.VMEM((3, rows, 128), LOW),
            pltpu.SemaphoreType.DMA((3,)),
        ],
        compiler_params=pltpu.CompilerParams(vmem_limit_bytes=40 << 20),
        cost_estimate=pl.CostEstimate(
            flops=10 * rows * 2 * rows * 128, bytes_accessed=6 << 20, transcendentals=rows * 2 * rows
        ),
        name="attend_back",
    )(spots["scalars"], spots["low"], spots["high"], spots["keys"], own, *others, kept, grad)


def tie(first, *rest):
    return lax.optimization_barrier((first, *rest))


X_GROUPS = [[x * SIDE + z for x in range(SIDE)] for z in range(SIDE)]


def forward_attention(residual, normed_all, spots, vectors, bias_qkv, w_heads, w_back):
    b_out = vectors[2]
    projected = ((nt_dot(normed_all, w_heads) + bias_qkv) * spots["scale"]).astype(LOW)
    width = projected.shape[1] // SIDE
    pieces = [projected[:, d * width : (d + 1) * width] for d in range(SIDE)]
    own = jnp.concatenate([pieces[0]] + [move_x(pieces[d], -d) for d in range(1, SIDE)], axis=0)
    others = [move_y_open(own[:, 0:128], d) for d in range(1, SIDE)]
    kept = attend(spots, own, others)
    lanes = lax.broadcasted_iota(jnp.int32, kept.shape, 1)
    mixed = jnp.where(lanes < HEAD_DIM, 0.0, kept).astype(LOW)
    rows = mixed.shape[0] // SIDE
    mixed_rows = jnp.concatenate(
        [mixed[0:rows]] + [move_x(mixed[d * rows : (d + 1) * rows], d) for d in range(1, SIDE)], axis=1
    )
    hidden = residual + (scatter_z(local_dot(mixed_rows, w_back).astype(LOW)) + b_out)
    return hidden, (residual, normed_all, own, others, kept, mixed_rows)


def forward_hidden_units(hidden, vectors, b_up, w_up, w_down):
    gain_two, bias_two, b_down = vectors[3:6]
    normed_two_all = gather_z(layer_norm(hidden, gain_two, bias_two).astype(LOW))
    up_value = nt_dot(normed_two_all, w_up) + b_up
    activated = jax.nn.gelu(up_value).astype(LOW)
    result = hidden + (scatter_z(local_dot(activated, w_down).astype(LOW)) + b_down)
    return result, (hidden, normed_two_all, up_value, activated)


def backward_hidden_units(grad_out, grad_down_all, stored, vectors, w_up, w_down):
    hidden, normed_two_all, up_value, activated = stored
    gain_two, bias_two = vectors[3:5]
    grad_down = grad_out.astype(LOW)
    g_b_down = jnp.sum(grad_down.astype(FULL), axis=0, keepdims=True)
    _, gelu_pull = jax.vjp(jax.nn.gelu, up_value)
    (grad_up,) = gelu_pull(nt_dot(grad_down_all, w_down))
    grad_up = grad_up.astype(LOW)
    grad_normed_two = scatter_z(local_dot(grad_up, w_up).astype(LOW))
    g_w_down = tn_dot(activated, grad_down_all).astype(LOW)
    g_b_up = jnp.sum(grad_up.astype(FULL), axis=0)
    g_w_up = tn_dot(grad_up, normed_two_all).astype(LOW)
    _, norm_two_pull = jax.vjp(layer_norm, hidden, gain_two, bias_two)
    grad_hidden_part, g_gain_two, g_bias_two = norm_two_pull(grad_normed_two)
    grad_hidden = grad_out + grad_hidden_part
    return grad_hidden, (g_gain_two, g_bias_two, g_b_down), g_b_up, g_w_up, g_w_down


def backward_mixed(grad_hidden, stored, w_back, spots):
    mixed_rows = stored[5]
    grad_attn = grad_hidden.astype(LOW)
    g_b_out = jnp.sum(grad_attn.astype(FULL), axis=0, keepdims=True)
    grad_attn_all = gather_z(grad_attn)
    grad_mixed = (nt_dot(grad_attn_all, w_back) * spots["upper"]).astype(LOW)
    pieces = [grad_mixed[:, d * 128 : (d + 1) * 128] for d in range(SIDE)]
    grad_own = jnp.concatenate(
        [pieces[0]] + [move_x(pieces[d], -d) for d in range(1, SIDE)], axis=0
    )
    g_w_out = tn_dot(mixed_rows, grad_attn_all)
    return grad_own, g_b_out, g_w_out


def backward_heads(grad_mixed_own, stored, spots):
    _, _, own, others, kept, _ = stored
    dq, dkv0, dkv1, dkv2, dkv3 = attend_back(spots, own, others, kept, grad_mixed_own)
    dkv = dkv0.astype(FULL)
    for d, part in enumerate((dkv1, dkv2, dkv3), 1):
        dkv = dkv + move_y_open(part, -d).astype(FULL)
    grad_own = jnp.concatenate([dkv.astype(LOW), dq], axis=1)
    rows = grad_own.shape[0] // SIDE
    return jnp.concatenate(
        [grad_own[0:rows]] + [move_x(grad_own[d * rows : (d + 1) * rows], d) for d in range(1, SIDE)],
        axis=1,
    )


def backward_entry(grad_qkv, grad_hidden, stored, vectors, w_heads):
    residual, normed_all = stored[0:2]
    gain_one, bias_one = vectors[0:2]
    grad_normed = scatter_z(local_dot(grad_qkv, w_heads).astype(LOW))
    g_w_heads = tn_dot(grad_qkv, normed_all)
    g_b_qkv = jnp.sum(grad_qkv.astype(FULL), axis=0)
    _, norm_one_pull = jax.vjp(layer_norm, residual, gain_one, bias_one)
    grad_residual_part, g_gain_one, g_bias_one = norm_one_pull(grad_normed)
    return grad_hidden + grad_residual_part, (g_gain_one, g_bias_one), g_b_qkv, g_w_heads


def per_device(
    inputs,
    segments,
    gain_one,
    bias_one,
    w_qkv,
    b_qv,
    w_out,
    b_out,
    gain_two,
    bias_two,
    w_up,
    b_up,
    w_down,
    b_down,
    cotangent,
):
    here = lax.axis_index("section")
    block = lax.axis_index("ctx")
    spot = lax.axis_index("tensor")
    x_here, z_here = spot // SIDE, spot % SIDE
    row_count, model_width = inputs.shape[2], inputs.shape[3]
    block_rows = row_count * SIDE * SIDE

    def owner(layer, yes, no):
        return jnp.where(here == layer, yes, no)

    sequence = lax.dynamic_index_in_dim(inputs, here, 0, False)[0].astype(FULL)
    grad_last = lax.dynamic_index_in_dim(cotangent, here, 0, False)[0].astype(FULL)
    grad_last_all = lax.dynamic_index_in_dim(cotangent, here, 0, False)[0]

    heads_kv = jnp.concatenate([w_qkv[0, :, 1].T, w_qkv[0, :, 2].T], axis=0)
    heads_qo = jnp.concatenate([w_qkv[0, :, 0].T, w_out[0]], axis=0)
    heads_qo_other = swap(heads_qo)
    gap = jnp.zeros((HEAD_DIM,), LOW)
    small = jnp.concatenate(
        [gain_one, bias_one, b_out, gain_two, bias_two, b_down]
        + [
            jnp.concatenate(
                [b_up[0], gap, b_qv[0, 1], b_qv[0, 0], gap, jnp.zeros((model_width - 512,), LOW)]
            )[None],
            jnp.zeros((1, model_width), LOW),
        ],
        axis=0,
    )
    small_other = swap(small)
    up_own, down_other = w_up[0].T, swap(w_down[0])

    def gather_heads(layer, after=None):
        half = owner(layer, heads_kv, heads_qo_other)
        if after is not None:
            half, _ = tie(half, after)
        mine = jnp.stack([half] + [move_x(half, d) for d in range(1, SIDE)])
        return mine, swap(mine)

    def join_heads(layer, mine, theirs):
        key_value, query_out = owner(layer, mine, theirs), owner(layer, theirs, mine)
        whole = jnp.concatenate([key_value, query_out], axis=1).reshape(SIDE * TILE, model_width)
        return whole, query_out.reshape(SIDE * 128, model_width)

    def gather_units(layer, after=None):
        half = owner(layer, up_own, down_other)
        if after is not None:
            half, _ = tie(half, after)
        return lax.all_gather(half, "tensor", axis=0, tiled=True, axis_index_groups=X_GROUPS)

    def join_units(layer, mine):
        theirs = swap(mine)
        return owner(layer, mine, theirs), owner(layer, theirs, mine)

    smalls = (owner(0, small, small_other), owner(0, small_other, small))
    vectors = [
        tuple(smalls[layer][row : row + 1].astype(FULL) for row in range(6)) for layer in range(2)
    ]
    normed = layer_norm(sequence, *vectors[0][0:2]).astype(LOW)
    heads_first = join_heads(0, *gather_heads(0, normed))
    units_first = gather_units(0)
    normed_all = gather_z(normed)
    normed_all, segments = tie(normed_all, segments)
    segment_ids = lax.dynamic_index_in_dim(segments, here, 0, False)
    start_one = jnp.sum((segment_ids < 1).astype(jnp.int32))
    start_two = jnp.sum((segment_ids < 2).astype(jnp.int32))

    def first_of(place):
        return jnp.where(place >= start_two, start_two, jnp.where(place >= start_one, start_one, 0))

    order = jnp.arange(block_rows)
    from_x = (x_here + order // TILE) % SIDE
    from_z = (z_here - order // row_count % SIDE) % SIDE
    place = block * block_rows + (from_x * SIDE + from_z) * row_count + order % row_count
    tile_first = block * block_rows + (x_here + jnp.arange(SIDE)) % SIDE * TILE
    lane = jnp.arange(SIDE * TILE) % TILE
    spots = {
        "scalars": jnp.concatenate(
            [block[None], first_of(tile_first), first_of(tile_first + TILE - 1)]
        ).astype(jnp.int32),
        "high": place.astype(jnp.int32).reshape(SIDE, 1, TILE),
        "low": first_of(place).astype(jnp.int32).reshape(SIDE, 1, TILE),
        "keys": place.astype(jnp.int32).reshape(block_rows, 1),
        "scale": jnp.where(lane < 128, 1.0, jnp.where(lane < 192, BASE_TWO_SCALE, 0.0)).astype(FULL),
        "upper": (jnp.arange(SIDE * 128) % 128 >= HEAD_DIM).astype(FULL),
    }

    split_own = jnp.concatenate([smalls[0][6:7, :512], smalls[1][6:7, :512]], axis=0)
    split_all = [split_own] + [move_x(split_own, d) for d in range(1, SIDE)]
    bias_heads = [
        jnp.concatenate([part[layer : layer + 1, 256:512] for part in split_all], axis=1).astype(FULL)
        for layer in range(2)
    ]
    turn = ((x_here - jnp.arange(SIDE)) % SIDE)[None, :] == jnp.arange(SIDE)[:, None]
    bias_up = [
        jnp.sum(
            jnp.where(
                turn[:, :, None], jnp.stack([part[layer, 0:256] for part in split_all]).astype(FULL)[None], 0.0
            ),
            axis=1,
        ).reshape(1, -1)
        for layer in range(2)
    ]

    hidden, kept_heads_first = forward_attention(sequence, normed_all, spots, vectors[0], bias_heads[0], *heads_first)
    heads_last = gather_heads(1, kept_heads_first[4])
    units_first = join_units(0, units_first)
    units_last = gather_units(1, kept_heads_first[4])
    hidden, grad_last_all = tie(hidden, gather_z(grad_last_all))
    middle, kept_units_first = forward_hidden_units(hidden, vectors[0], bias_up[0], *units_first)
    middle, *heads_last = tie(middle, *heads_last)
    heads_last = join_heads(1, *heads_last)
    middle = middle.astype(LOW).astype(FULL)
    normed_all = gather_z(layer_norm(middle, *vectors[1][0:2]).astype(LOW))
    hidden, kept_heads_last = forward_attention(
        middle, normed_all, spots, vectors[1], bias_heads[1], *heads_last
    )
    units_last = join_units(1, units_last)
    result, kept_units_last = forward_hidden_units(hidden, vectors[1], bias_up[1], *units_last)

    def swap_grads(layer, first, second):
        return owner(layer, first, second), swap(owner(layer, second, first))

    def add_grads(kept, arrived):
        return (kept.astype(FULL) + arrived.astype(FULL)).astype(LOW)

    def scatter_units(grads):
        return lax.psum_scatter(
            grads, "tensor", scatter_dimension=0, tiled=True, axis_index_groups=X_GROUPS
        )

    def split_heads(g_w_heads, g_w_out):
        heads = g_w_heads.reshape(SIDE, TILE, model_width)
        key_value = heads[:, 0:128].astype(LOW)
        return key_value, (heads[:, 128:256] + g_w_out.reshape(SIDE, 128, model_width)).astype(LOW)

    def scatter_heads(grads):
        total = grads[0].astype(FULL)
        for d in range(1, SIDE):
            total = total + move_x(grads[d], -d).astype(FULL)
        return total.astype(LOW)

    def pack_vectors(heads, units, g_b_out, g_b_up, g_b_qkv):
        by_turn = jnp.sum(
            jnp.where(turn[:, :, None], g_b_up.reshape(SIDE, 1, TILE), 0.0), axis=0
        )
        return jnp.concatenate(
            [
                *heads, g_b_out, *units,
                jnp.concatenate([by_turn, g_b_qkv.reshape(SIDE, TILE)], axis=1).reshape(2, -1),
            ],
            axis=0,
        )

    grad_hidden, vec_units_last, g_b_up_last, g_up, g_down = backward_hidden_units(
        grad_last, grad_last_all, kept_units_last, vectors[1], *units_last
    )
    units_kept, units_arrived = swap_grads(1, g_up, g_down)
    grad_mixed, g_b_out_last, g_out = backward_mixed(grad_hidden, kept_heads_last, heads_last[1], spots)
    grad_mixed, units_kept, units_arrived = tie(grad_mixed, units_kept, units_arrived)
    units_sum_last = scatter_units(add_grads(units_kept, units_arrived))
    grad_qkv = backward_heads(grad_mixed, kept_heads_last, spots)
    grad_middle, vec_heads_last, g_b_qkv_last, g_heads = backward_entry(
        grad_qkv, grad_hidden, kept_heads_last, vectors[1], heads_last[0]
    )
    heads_kept, heads_arrived = swap_grads(1, *split_heads(g_heads, g_out))

    grad_middle = grad_middle.astype(LOW).astype(FULL)
    grad_middle, units_sum_last = tie(grad_middle, units_sum_last)
    units_sum_last = lax.psum(units_sum_last, "ctx")
    grad_hidden, vec_units_first, g_b_up_first, g_up, g_down = backward_hidden_units(
        grad_middle, gather_z(grad_middle.astype(LOW)), kept_units_first, vectors[0], *units_first
    )
    units_kept, units_arrived = swap_grads(0, g_up, g_down)
    grad_hidden, heads_kept, heads_arrived = tie(grad_hidden, heads_kept, heads_arrived)
    heads_sum_last = scatter_heads(add_grads(heads_kept, heads_arrived))
    grad_mixed, g_b_out_first, g_out = backward_mixed(grad_hidden, kept_heads_first, heads_first[1], spots)
    grad_mixed, units_kept, units_arrived, heads_sum_last, units_sum_last = tie(
        grad_mixed, units_kept, units_arrived, heads_sum_last, units_sum_last
    )
    units_sum_first = scatter_units(add_grads(units_kept, units_arrived))
    grad_qkv = backward_heads(grad_mixed, kept_heads_first, spots)
    grad_qkv, units_sum_first = tie(grad_qkv, units_sum_first)
    units_sum_first, heads_sum_last = lax.psum((units_sum_first, heads_sum_last), "ctx")
    gain_one, bias_one = vectors[0][0:2]
    residual, normed_all = kept_heads_first[0:2]
    grad_normed = local_dot(grad_qkv, heads_first[0])
    g_bias_one = jnp.sum(grad_normed, axis=0, keepdims=True)
    g_gain_one = jnp.sum(grad_normed * ((normed_all.astype(FULL) - bias_one) / gain_one), axis=0, keepdims=True)
    g_b_qkv_first = jnp.sum(grad_qkv.astype(FULL), axis=0)
    sums_first = pack_vectors(
        (g_gain_one, g_bias_one), vec_units_first, g_b_out_first, g_b_up_first, g_b_qkv_first
    )
    sums_last = pack_vectors(vec_heads_last, vec_units_last, g_b_out_last, g_b_up_last, g_b_qkv_last)
    sums = owner(0, sums_first, sums_last) + swap(owner(0, sums_last, sums_first))
    common = jnp.pad(sums[:6], ((0, 10), (0, 0))).astype(LOW)
    chunks = grad_normed.astype(LOW).reshape(SIDE, row_count, model_width)
    chunks = [jnp.concatenate([chunks[d], common], axis=0) for d in range(SIDE)]
    chunks = even_pairs(chunks, move_z)
    heads_kept, heads_arrived = swap_grads(0, *split_heads(tn_dot(grad_qkv, normed_all), g_out))
    halves = add_grads(heads_kept, heads_arrived)
    common = chunks[row_count : row_count + 6].astype(LOW)
    split = sums[6:].reshape(SIDE, 1, 512).astype(LOW)
    packs = [
        jnp.concatenate(
            [
                halves[d],
                common,
                jnp.pad(split[d], ((0, 0), (0, model_width - 512))),
                jnp.zeros((9, model_width), LOW),
            ],
            axis=0,
        )
        for d in range(SIDE)
    ]
    pack = even_sum(even_pairs(packs, move_x).astype(LOW), move_y)
    heads_sum_first, pack = pack[:128], pack[128:]
    _, norm_one_pull = jax.vjp(lambda rows: layer_norm(rows, gain_one, bias_one), residual)
    grad_first = grad_hidden + norm_one_pull(chunks[:row_count])[0]

    passed = swap(owner(0, result, grad_first))
    kept = owner(0, grad_first, result)
    boundary = owner(0, jnp.stack([kept, passed]), jnp.stack([passed, kept]))
    boundary = boundary.reshape(1, 2, 1, row_count, model_width)

    units_sum = owner(0, units_sum_first, units_sum_last)
    heads_sum = owner(0, heads_sum_first, heads_sum_last)
    units_theirs = swap(owner(0, units_sum_last, units_sum_first))
    heads_theirs = swap(owner(0, heads_sum_last, heads_sum_first).astype(LOW))
    g_key_value = heads_sum.astype(FULL)
    g_query_out = heads_theirs.astype(FULL)
    g_w_qkv = jnp.stack([g_query_out[0:64].T, g_key_value[0:64].T, g_key_value[64:128].T], axis=1)
    g_b_qv = jnp.stack([pack[6, 384:448], pack[6, 320:384]])
    return (
        boundary,
        pack[0:1],
        pack[1:2],
        g_w_qkv[None],
        g_b_qv[None],
        g_query_out[64:128][None],
        pack[2:3],
        pack[3:4],
        pack[4:5],
        units_sum.astype(FULL).T[None],
        pack[6:7, 0:256],
        units_theirs.astype(FULL)[None],
        pack[5:6],
    )


def solution(mesh):
    return jax.shard_map(
        per_device,
        mesh=mesh,
        in_specs=(
            P(None, "ctx", "tensor", None),
            P(),
            P("section", None),
            P("section", None),
            P("section", None, None, "tensor"),
            P("section", None, "tensor"),
            P("section", "tensor", None),
            P("section", None),
            P("section", None),
            P("section", None),
            P("section", None, "tensor"),
            P("section", "tensor"),
            P("section", "tensor", None),
            P("section", None),
            P(None, "ctx", "tensor", None),
        ),
        out_specs=(
            P("section", None, "ctx", "tensor", None),
            P("section", None),
            P("section", None),
            P("section", None, None, "tensor"),
            P("section", None, "tensor"),
            P("section", "tensor", None),
            P("section", None),
            P("section", None),
            P("section", None),
            P("section", None, "tensor"),
            P("section", "tensor"),
            P("section", "tensor", None),
            P("section", None),
        ),
        check_vma=False,
    )
```

```python
import functools
import math

import jax
import jax.numpy as jnp
from jax import lax
from jax.experimental import pallas as pl
from jax.experimental.pallas import tpu as pltpu
from jax.sharding import PartitionSpec as P

HEAD_DIM = 64
EPSILON = 1e-05
MASK_FILL = -1e30
BASE_TWO_SCALE = 0.125 * math.log2(math.e)
SIDE = 4
TILE = 256
LN_TWO = math.log(2.0)
LOW = jnp.bfloat16
FULL = jnp.float32


def move_z(block, distance):
    route = [
        (x * SIDE + z, x * SIDE + (z + distance) % SIDE) for x in range(SIDE) for z in range(SIDE)
    ]
    return lax.ppermute(block, "tensor", route)


def move_x(block, distance):
    route = [
        (x * SIDE + z, (x + distance) % SIDE * SIDE + z) for x in range(SIDE) for z in range(SIDE)
    ]
    return lax.ppermute(block, "tensor", route)


def move_y(block, distance):
    return lax.ppermute(block, "ctx", [(y, (y + distance) % SIDE) for y in range(SIDE)])


def move_y_open(block, distance):
    route = [(y, y + distance) for y in range(SIDE) if 0 <= y + distance < SIDE]
    return lax.ppermute(block, "ctx", route)


def move_x_in(block, distance, section):
    base = section * SIDE * SIDE
    route = [
        (base + x * SIDE + z, base + (x + distance) % SIDE * SIDE + z)
        for x in range(SIDE)
        for z in range(SIDE)
    ]
    return lax.ppermute(block, ("section", "tensor"), route)


def move_y_in(block, distance, section):
    base = section * SIDE
    route = [(base + y, base + (y + distance) % SIDE) for y in range(SIDE)]
    return lax.ppermute(block, ("section", "ctx"), route)


def swap(block):
    return lax.ppermute(block, "section", [(0, 1), (1, 0)])


def send_to(block, section):
    return lax.ppermute(block, "section", [(1 - section, section)])


def gather_z(rows):
    return jnp.concatenate([rows] + [move_z(rows, d) for d in range(1, SIDE)], axis=0)


def scatter_z(rows):
    chunks = rows.reshape(SIDE, rows.shape[0] // SIDE, rows.shape[1])
    total = chunks[0].astype(FULL)
    for d in range(1, SIDE):
        total = total + move_z(chunks[d], -d).astype(FULL)
    return total


def even_sum(block, move):
    low = block.astype(FULL)
    return (low + move(block, 2).astype(FULL)) + (
        move(block, 1).astype(FULL) + move(block, 3).astype(FULL)
    )


def even_pairs(blocks, move):
    return (blocks[0].astype(FULL) + move(blocks[2], -2).astype(FULL)) + (
        move(blocks[1], -1).astype(FULL) + move(blocks[3], -3).astype(FULL)
    )


def layer_norm(values, gain, bias):
    center = values - jnp.mean(values, axis=-1, keepdims=True)
    spread = jnp.mean(center * center, axis=-1, keepdims=True)
    return center * lax.rsqrt(spread + EPSILON) * gain + bias


def local_dot(left, right):
    return jnp.dot(left, right, preferred_element_type=FULL)


def back_dot(left, right):
    return jnp.einsum("rf,df->rd", left, right, preferred_element_type=FULL)


def outer_sum(left, right):
    return jnp.einsum("rd,rf->df", left, right, preferred_element_type=FULL)


def nt_dot(left, right):
    return lax.dot_general(left, right, (((1,), (1,)), ((), ())), preferred_element_type=FULL)


def tn_dot(left, right):
    return lax.dot_general(left, right, (((0,), (0,)), ((), ())), preferred_element_type=FULL)


def attend_kernel(
    scalar_ref, low_ref, high_ref, key_ref, own_ref, kv1_ref, kv2_ref, kv3_ref, out_ref,
    peak, mixed, held, arrived,
):
    block = scalar_ref[0]
    rows_all = own_ref.shape[0]
    tiles = rows_all // TILE
    copies = [
        pltpu.make_async_copy(ref, held.at[d], arrived.at[d])
        for d, ref in enumerate((kv1_ref, kv2_ref, kv3_ref))
    ]
    for copy in copies:
        copy.start()
    peak[...] = jnp.full_like(peak, MASK_FILL)
    mixed[...] = jnp.zeros_like(mixed)
    for d in range(SIDE):
        if d > 0:
            copies[d - 1].wait()
        start = (block - d) * rows_all

        @pl.loop(0, tiles)
        def _(index, d=d, start=start):
            rows = pl.ds(pl.multiple_of(index * TILE, TILE), TILE)
            least, most = scalar_ref[1 + index], scalar_ref[1 + tiles + index]

            def step(masked):
                key_values = own_ref[:, 0:128] if d == 0 else held[d - 1]
                raw = nt_dot(key_values, own_ref[rows, 128:256])
                if masked:
                    places = key_ref[...] - d * rows_all
                    allowed = places >= low_ref[index]
                    if d == 0:
                        allowed = allowed & (places <= high_ref[index])
                    raw = jnp.where(allowed, raw, MASK_FILL)
                old = peak[index]
                top = jnp.maximum(old, jnp.max(raw, axis=0, keepdims=True))
                weight = jnp.exp2(raw - top).astype(LOW)
                lanes = lax.broadcasted_iota(jnp.int32, key_values.shape, 1)
                ones_values = jnp.where(lanes < HEAD_DIM, jnp.ones_like(key_values), key_values)
                peak[index] = top
                mixed[index] = mixed[index] * jnp.exp2(old - top) + tn_dot(ones_values, weight)

            if d == 0:
                step(True)
            else:
                reached = (block >= d) & (least < start + rows_all)
                pl.when(reached & (most <= start))(lambda: step(False))
                pl.when(reached & (most > start))(lambda: step(True))

    @pl.loop(0, tiles)
    def _(index):
        rows = pl.ds(pl.multiple_of(index * TILE, TILE), TILE)
        sums = mixed[index]
        count = sums[0:1, :]
        level = peak[index] + jnp.log2(count)
        lines = lax.broadcasted_iota(jnp.int32, sums.shape, 0)
        out_ref[rows, :] = jnp.where(lines < HEAD_DIM, level, sums / count).T


def attend_back_kernel(
    scalar_ref, low_ref, high_ref, key_ref, own_ref, kv1_ref, kv2_ref, kv3_ref, kept_ref, grad_ref,
    dq_ref, d0_ref, d1_ref, d2_ref, d3_ref,
    query_sum, key_sum, held, arrived,
):
    block = scalar_ref[0]
    rows_all = own_ref.shape[0]
    tiles = rows_all // TILE
    copies = [
        pltpu.make_async_copy(ref, held.at[d], arrived.at[d])
        for d, ref in enumerate((kv1_ref, kv2_ref, kv3_ref))
    ]
    for copy in copies:
        copy.start()
    query_sum[...] = jnp.zeros_like(query_sum)
    for d, out_ref in enumerate((d0_ref, d1_ref, d2_ref, d3_ref)):
        if d > 0:
            copies[d - 1].wait()

        @pl.when(block >= d)
        def _(d=d, out_ref=out_ref):
            start = (block - d) * rows_all
            key_sum[...] = jnp.zeros_like(key_sum)

            @pl.loop(0, tiles)
            def _(index):
                rows = pl.ds(pl.multiple_of(index * TILE, TILE), TILE)
                least, most = scalar_ref[1 + index], scalar_ref[1 + tiles + index]

                def step(masked):
                    queries = own_ref[rows, 128:256]
                    grad = grad_ref[rows, :]
                    kept = kept_ref[rows, :]
                    level = kept.T[0:1, :]
                    meet = jnp.sum((kept * grad.astype(FULL)).T, axis=0, keepdims=True)
                    key_values = own_ref[:, 0:128] if d == 0 else held[d - 1]
                    probs = jnp.exp2(nt_dot(key_values, queries) - level)
                    if masked:
                        places = key_ref[...] - d * rows_all
                        allowed = places >= low_ref[index]
                        if d == 0:
                            allowed = allowed & (places <= high_ref[index])
                        probs = jnp.where(allowed, probs, 0.0)
                    grad_scores = (probs * (nt_dot(key_values, grad) - meet)).astype(LOW)
                    key_sum[...] += local_dot(grad_scores, queries) * LN_TWO + local_dot(
                        probs.astype(LOW), grad
                    )
                    query_sum[rows, :] += tn_dot(grad_scores, key_values)

                if d == 0:
                    step(True)
                else:
                    pl.when(most <= start)(lambda: step(False))
                    pl.when((most > start) & (least < start + rows_all))(lambda: step(True))

            out_ref[...] = key_sum[...].astype(LOW)

        if d > 0:

            @pl.when(block < d)
            def _(out_ref=out_ref):
                out_ref[...] = jnp.zeros_like(out_ref)

    lanes = lax.broadcasted_iota(jnp.int32, dq_ref.shape, 1)
    dq_ref[...] = jnp.where(lanes < HEAD_DIM, query_sum[...] * 0.125, 0.0).astype(LOW)


VMEM_SPEC = pl.BlockSpec(memory_space=pltpu.VMEM)
SMEM_SPEC = pl.BlockSpec(memory_space=pltpu.SMEM)
ANY_SPEC = pl.BlockSpec(memory_space=pl.ANY)


def attend(spots, own, others):
    rows = own.shape[0]
    return pl.pallas_call(
        attend_kernel,
        out_shape=jax.ShapeDtypeStruct((rows, 128), FULL),
        in_specs=[SMEM_SPEC] + [VMEM_SPEC] * 4 + [ANY_SPEC] * 3,
        out_specs=VMEM_SPEC,
        scratch_shapes=[
            pltpu.VMEM((rows // TILE, 1, TILE), FULL),
            pltpu.VMEM((rows // TILE, 128, TILE), FULL),
            pltpu.VMEM((3, rows, 128), LOW),
            pltpu.SemaphoreType.DMA((3,)),
        ],
        compiler_params=pltpu.CompilerParams(vmem_limit_bytes=60 << 20),
        cost_estimate=pl.CostEstimate(
            flops=4 * rows * 2 * rows * 128, bytes_accessed=4 << 20, transcendentals=rows * 2 * rows
        ),
        name="attend",
    )(spots["scalars"], spots["low"], spots["high"], spots["keys"], own, *others)


def attend_back(spots, own, others, kept, grad):
    rows = own.shape[0]
    return pl.pallas_call(
        attend_back_kernel,
        out_shape=[jax.ShapeDtypeStruct((rows, 128), LOW)] * 5,
        in_specs=[SMEM_SPEC] + [VMEM_SPEC] * 4 + [ANY_SPEC] * 3 + [VMEM_SPEC] * 2,
        out_specs=[VMEM_SPEC] * 5,
        scratch_shapes=[
            pltpu.VMEM((rows, 128), FULL),
            pltpu.VMEM((rows, 128), FULL),
            pltpu.VMEM((3, rows, 128), LOW),
            pltpu.SemaphoreType.DMA((3,)),
        ],
        compiler_params=pltpu.CompilerParams(vmem_limit_bytes=60 << 20),
        cost_estimate=pl.CostEstimate(
            flops=10 * rows * 2 * rows * 128, bytes_accessed=6 << 20, transcendentals=rows * 2 * rows
        ),
        name="attend_back",
    )(spots["scalars"], spots["low"], spots["high"], spots["keys"], own, *others, kept, grad)


def tie(first, *rest):
    return lax.optimization_barrier((first, *rest))


X_GROUPS = [[x * SIDE + z for x in range(SIDE)] for z in range(SIDE)]


def forward_attention(residual, normed_all, spots, vectors, bias_qkv, w_heads, w_back):
    b_out = vectors[2]
    projected = ((nt_dot(normed_all, w_heads) + bias_qkv) * spots["scale"]).astype(LOW)
    width = projected.shape[1] // SIDE
    pieces = [projected[:, d * width : (d + 1) * width] for d in range(SIDE)]
    own = jnp.concatenate([pieces[0]] + [move_x(pieces[d], -d) for d in range(1, SIDE)], axis=0)
    others = [move_y_open(own[:, 0:128], d) for d in range(1, SIDE)]
    kept = attend(spots, own, others)
    lanes = lax.broadcasted_iota(jnp.int32, kept.shape, 1)
    mixed = jnp.where(lanes < HEAD_DIM, 0.0, kept).astype(LOW)
    rows = mixed.shape[0] // SIDE
    mixed_rows = jnp.concatenate(
        [mixed[0:rows]] + [move_x(mixed[d * rows : (d + 1) * rows], d) for d in range(1, SIDE)], axis=1
    )
    hidden = residual + (scatter_z(local_dot(mixed_rows, w_back).astype(LOW)) + b_out)
    return hidden, (residual, normed_all, own, others, kept, mixed_rows)


def forward_hidden_units(hidden, vectors, b_up, w_up, w_down):
    gain_two, bias_two, b_down = vectors[3:6]
    normed_two_all = gather_z(layer_norm(hidden, gain_two, bias_two).astype(LOW))
    up_value = nt_dot(normed_two_all, w_up) + b_up
    activated = jax.nn.gelu(up_value).astype(LOW)
    result = hidden + (scatter_z(local_dot(activated, w_down).astype(LOW)) + b_down)
    return result, (hidden, normed_two_all, up_value, activated)


def backward_hidden_units(grad_out, grad_down_all, stored, vectors, w_up, w_down):
    hidden, normed_two_all, up_value, activated = stored
    gain_two, bias_two = vectors[3:5]
    grad_down = grad_out.astype(LOW)
    g_b_down = jnp.sum(grad_down.astype(FULL), axis=0, keepdims=True)
    _, gelu_pull = jax.vjp(jax.nn.gelu, up_value)
    (grad_up,) = gelu_pull(nt_dot(grad_down_all, w_down))
    grad_up = grad_up.astype(LOW)
    grad_normed_two = scatter_z(local_dot(grad_up, w_up).astype(LOW))
    g_w_down = tn_dot(activated, grad_down_all).astype(LOW)
    g_b_up = jnp.sum(grad_up.astype(FULL), axis=0)
    g_w_up = tn_dot(grad_up, normed_two_all).astype(LOW)
    _, norm_two_pull = jax.vjp(layer_norm, hidden, gain_two, bias_two)
    grad_hidden_part, g_gain_two, g_bias_two = norm_two_pull(grad_normed_two)
    grad_hidden = grad_out + grad_hidden_part
    return grad_hidden, (g_gain_two, g_bias_two, g_b_down), g_b_up, g_w_up, g_w_down


def backward_mixed(grad_hidden, stored, w_back, spots):
    mixed_rows = stored[5]
    grad_attn = grad_hidden.astype(LOW)
    g_b_out = jnp.sum(grad_attn.astype(FULL), axis=0, keepdims=True)
    grad_attn_all = gather_z(grad_attn)
    grad_mixed = (nt_dot(grad_attn_all, w_back) * spots["upper"]).astype(LOW)
    pieces = [grad_mixed[:, d * 128 : (d + 1) * 128] for d in range(SIDE)]
    grad_own = jnp.concatenate(
        [pieces[0]] + [move_x(pieces[d], -d) for d in range(1, SIDE)], axis=0
    )
    g_w_out = tn_dot(mixed_rows, grad_attn_all).astype(LOW)
    return grad_own, g_b_out, g_w_out


def backward_heads(parts):
    dq, dkv0, dkv1, dkv2, dkv3 = parts
    dkv = dkv0.astype(FULL)
    for d, part in enumerate((dkv1, dkv2, dkv3), 1):
        dkv = dkv + move_y_open(part, -d).astype(FULL)
    grad_own = jnp.concatenate([dkv.astype(LOW), dq], axis=1)
    rows = grad_own.shape[0] // SIDE
    return jnp.concatenate(
        [grad_own[0:rows]] + [move_x(grad_own[d * rows : (d + 1) * rows], d) for d in range(1, SIDE)],
        axis=1,
    )


def backward_entry(grad_qkv, grad_hidden, stored, vectors, w_heads):
    residual, normed_all = stored[0:2]
    gain_one, bias_one = vectors[0:2]
    grad_normed = scatter_z(local_dot(grad_qkv, w_heads).astype(LOW))
    g_w_heads = tn_dot(grad_qkv, normed_all).astype(LOW)
    g_b_qkv = jnp.sum(grad_qkv.astype(FULL), axis=0)
    _, norm_one_pull = jax.vjp(layer_norm, residual, gain_one, bias_one)
    grad_residual_part, g_gain_one, g_bias_one = norm_one_pull(grad_normed)
    return grad_hidden + grad_residual_part, (g_gain_one, g_bias_one), g_b_qkv, g_w_heads


def per_device(
    inputs,
    segments,
    gain_one,
    bias_one,
    w_qkv,
    b_qv,
    w_out,
    b_out,
    gain_two,
    bias_two,
    w_up,
    b_up,
    w_down,
    b_down,
    cotangent,
):
    here = lax.axis_index("section")
    block = lax.axis_index("ctx")
    spot = lax.axis_index("tensor")
    x_here, z_here = spot // SIDE, spot % SIDE
    row_count, model_width = inputs.shape[2], inputs.shape[3]
    block_rows = row_count * SIDE * SIDE

    def owner(layer, yes, no):
        return jnp.where(here == layer, yes, no)

    sequence = lax.dynamic_index_in_dim(inputs, here, 0, False)[0].astype(FULL)
    grad_last = lax.dynamic_index_in_dim(cotangent, here, 0, False)[0].astype(FULL)
    grad_last_all = lax.dynamic_index_in_dim(cotangent, here, 0, False)[0]

    gap = jnp.zeros((HEAD_DIM,), LOW)
    biases = jnp.concatenate(
        [b_up[0], gap, b_qv[0, 1], b_qv[0, 0], gap, jnp.zeros((model_width - 512,), LOW)]
    )[None]
    heads_kv = jnp.concatenate(
        [w_qkv[0, :, 1].T, w_qkv[0, :, 2].T, biases, jnp.zeros((15, model_width), LOW)], axis=0
    )
    heads_qo = jnp.concatenate(
        [w_qkv[0, :, 0].T, w_out[0], jnp.zeros((16, model_width), LOW)], axis=0
    )
    heads_qo_other = swap(heads_qo)
    small = jnp.concatenate(
        [gain_one, bias_one, b_out, gain_two, bias_two, b_down, jnp.zeros((2, model_width), LOW)],
        axis=0,
    )
    small_other = swap(small)
    up_own, down_other = w_up[0].T, swap(w_down[0])
    downward = [(x_here - d) % SIDE for d in range(SIDE)]

    def reorder(pieces):
        return [lax.dynamic_index_in_dim(pieces, place, 0, False) for place in downward]

    def half_heads(layer):
        return owner(layer, heads_kv, heads_qo_other)

    def join_heads(layer, mine, theirs):
        key_value, query_out = owner(layer, mine, theirs), owner(layer, theirs, mine)
        whole = jnp.concatenate([key_value[:, :128], query_out[:, :128]], axis=1)
        back = query_out[:, :128].reshape(SIDE * 128, model_width)
        rows = key_value[:, 128, :512].astype(FULL)
        bias_heads = rows[:, 256:].reshape(1, SIDE * TILE)
        bias_up = jnp.concatenate(reorder(rows[:, :256])).reshape(1, SIDE * TILE)
        return (whole.reshape(SIDE * TILE, model_width), back), bias_heads, bias_up

    def gather_whole(half):
        return lax.all_gather(half, "tensor", axis=0, tiled=True, axis_index_groups=X_GROUPS)

    def gather_units(layer):
        return gather_whole(owner(layer, up_own, down_other))

    def join_units(layer, mine):
        theirs = swap(mine)
        return owner(layer, mine, theirs), owner(layer, theirs, mine)

    smalls = (owner(0, small, small_other), owner(0, small_other, small))
    vectors = [
        tuple(smalls[layer][row : row + 1].astype(FULL) for row in range(6)) for layer in range(2)
    ]
    normed = layer_norm(sequence, *vectors[0][0:2]).astype(LOW)
    half, normed = tie(half_heads(0), normed)
    mine = jnp.stack([half] + [move_x(half, d) for d in range(1, SIDE)])
    normed_all, mine = tie(gather_z(normed), mine)
    heads_first, bias_heads_first, bias_up_first = join_heads(0, mine, swap(mine))
    units_first = gather_units(0)
    heads_last = gather_whole(half_heads(1)).reshape(SIDE, -1, model_width)
    units_last = gather_units(1)
    normed_all, segments = tie(normed_all, segments)
    segment_ids = lax.dynamic_index_in_dim(segments, here, 0, False)
    start_one = jnp.sum((segment_ids < 1).astype(jnp.int32))
    start_two = jnp.sum((segment_ids < 2).astype(jnp.int32))

    def first_of(place):
        return jnp.where(place >= start_two, start_two, jnp.where(place >= start_one, start_one, 0))

    order = jnp.arange(block_rows)
    from_x = (x_here + order // TILE) % SIDE
    from_z = (z_here - order // row_count % SIDE) % SIDE
    place = block * block_rows + (from_x * SIDE + from_z) * row_count + order % row_count
    tile_first = block * block_rows + (x_here + jnp.arange(SIDE)) % SIDE * TILE
    lane = jnp.arange(SIDE * TILE) % TILE
    spots = {
        "scalars": jnp.concatenate(
            [block[None], first_of(tile_first), first_of(tile_first + TILE - 1)]
        ).astype(jnp.int32),
        "high": place.astype(jnp.int32).reshape(SIDE, 1, TILE),
        "low": first_of(place).astype(jnp.int32).reshape(SIDE, 1, TILE),
        "keys": place.astype(jnp.int32).reshape(block_rows, 1),
        "scale": jnp.where(lane < 128, 1.0, jnp.where(lane < 192, BASE_TWO_SCALE, 0.0)).astype(FULL),
        "upper": (jnp.arange(SIDE * 128) % 128 >= HEAD_DIM).astype(FULL),
    }

    hidden, kept_heads_first = forward_attention(sequence, normed_all, spots, vectors[0], bias_heads_first, *heads_first)
    units_first = join_units(0, units_first)
    hidden, grad_last_all = tie(hidden, gather_z(grad_last_all))
    middle, kept_units_first = forward_hidden_units(hidden, vectors[0], bias_up_first, *units_first)
    mine = jnp.stack(reorder(heads_last))
    middle, mine, theirs = tie(middle, mine, swap(mine))
    heads_last, bias_heads_last, bias_up_last = join_heads(1, mine, theirs)
    middle = middle.astype(LOW).astype(FULL)
    normed_all = gather_z(layer_norm(middle, *vectors[1][0:2]).astype(LOW))
    hidden, kept_heads_last = forward_attention(
        middle, normed_all, spots, vectors[1], bias_heads_last, *heads_last
    )
    units_last = join_units(1, units_last)
    result, kept_units_last = forward_hidden_units(hidden, vectors[1], bias_up_last, *units_last)

    def swap_grads(layer, first, second):
        return owner(layer, first, second), swap(owner(layer, second, first))

    def add_grads(kept, arrived):
        return (kept.astype(FULL) + arrived.astype(FULL)).astype(LOW)

    def scatter_whole(grads):
        return lax.psum_scatter(
            grads, "tensor", scatter_dimension=0, tiled=True, axis_index_groups=X_GROUPS
        )

    def split_heads(g_w_heads, g_w_out):
        heads = g_w_heads.reshape(SIDE, TILE, model_width)
        return heads[:, 0:128], heads[:, 128:256] + g_w_out.reshape(SIDE, 128, model_width)

    turn = jnp.stack(downward)[None, :] == jnp.arange(SIDE)[:, None]

    def pack_vectors(heads, units, g_b_out, g_b_up, g_b_qkv):
        by_turn = jnp.sum(
            jnp.where(turn[:, :, None], g_b_up.reshape(SIDE, 1, TILE), 0.0), axis=0
        )
        return jnp.concatenate(
            [
                *heads, g_b_out, *units,
                jnp.concatenate([by_turn, g_b_qkv.reshape(SIDE, TILE)], axis=1).reshape(2, -1),
            ],
            axis=0,
        )

    grad_hidden, vec_units_last, g_b_up_last, g_up, g_down = backward_hidden_units(
        grad_last, grad_last_all, kept_units_last, vectors[1], *units_last
    )
    grad_hidden, units_kept, units_arrived = tie(grad_hidden, *swap_grads(1, g_up, g_down))
    units_sum_last = scatter_whole(add_grads(units_kept, units_arrived))
    grad_mixed, g_b_out_last, g_out = backward_mixed(grad_hidden, kept_heads_last, heads_last[1], spots)
    grad_qkv = backward_heads(attend_back(spots, *kept_heads_last[2:5], grad_mixed))
    grad_middle, vec_heads_last, g_b_qkv_last, g_heads = backward_entry(
        grad_qkv, grad_hidden, kept_heads_last, vectors[1], heads_last[0]
    )
    heads_kept, heads_arrived = swap_grads(1, *split_heads(g_heads, g_out))

    grad_middle = grad_middle.astype(LOW).astype(FULL)
    grad_down_all, heads_kept, heads_arrived = tie(
        gather_z(grad_middle.astype(LOW)), heads_kept, heads_arrived
    )
    heads_sum_last = scatter_whole(
        jnp.concatenate(reorder(add_grads(heads_kept, heads_arrived)), axis=0)
    )
    grad_hidden, vec_units_first, g_b_up_first, g_up, g_down = backward_hidden_units(
        grad_middle, grad_down_all, kept_units_first, vectors[0], *units_first
    )
    grad_hidden, units_kept, units_arrived, units_sum_last = tie(
        grad_hidden, *swap_grads(0, g_up, g_down), units_sum_last
    )
    units_sum_first = scatter_whole(add_grads(units_kept, units_arrived))
    grad_mixed, g_b_out_first, g_out = backward_mixed(grad_hidden, kept_heads_first, heads_first[1], spots)
    parts = attend_back(spots, *kept_heads_first[2:5], grad_mixed)
    parts, units_sum_first, heads_sum_last = tie(parts, units_sum_first, heads_sum_last)
    units_sum_first, units_sum_last, heads_sum_last = lax.psum(
        (units_sum_first, units_sum_last, heads_sum_last), "ctx"
    )
    grad_qkv = backward_heads(parts)

    gain_one, bias_one = vectors[0][0:2]
    residual, normed_all = kept_heads_first[0:2]
    grad_normed = local_dot(grad_qkv, heads_first[0])
    g_bias_one = jnp.sum(grad_normed, axis=0, keepdims=True)
    g_gain_one = jnp.sum(grad_normed * ((normed_all.astype(FULL) - bias_one) / gain_one), axis=0, keepdims=True)
    g_b_qkv_first = jnp.sum(grad_qkv.astype(FULL), axis=0)
    sums_first = pack_vectors(
        (g_gain_one, g_bias_one), vec_units_first, g_b_out_first, g_b_up_first, g_b_qkv_first
    )
    sums_last = pack_vectors(vec_heads_last, vec_units_last, g_b_out_last, g_b_up_last, g_b_qkv_last)
    common = jnp.pad(jnp.concatenate([sums_first[:6], sums_last[:6]]), ((0, 4), (0, 0))).astype(LOW)
    chunks = grad_normed.astype(LOW).reshape(SIDE, row_count, model_width)
    chunks = even_pairs([jnp.concatenate([chunks[d], common], axis=0) for d in range(SIDE)], move_z)
    heads_kept, heads_arrived = swap_grads(0, *split_heads(tn_dot(grad_qkv, normed_all).astype(LOW), g_out))
    halves = add_grads(heads_kept, heads_arrived)
    sums_first = jnp.concatenate([chunks[row_count : row_count + 6], sums_first[6:]])
    sums_last = jnp.concatenate([chunks[row_count + 6 : row_count + 12], sums_last[6:]])
    sums = owner(0, sums_first, sums_last) + swap(owner(0, sums_last, sums_first))
    common = sums[:6].astype(LOW)
    split = sums[6:].reshape(SIDE, 1, 512).astype(LOW)
    packs = [
        jnp.concatenate(
            [
                halves[d],
                common,
                jnp.pad(split[d], ((0, 0), (0, model_width - 512))),
                jnp.zeros((9, model_width), LOW),
            ],
            axis=0,
        )
        for d in range(SIDE)
    ]
    pack = even_sum(even_pairs(packs, move_x).astype(LOW), move_y)
    pack, units_sum_first, units_sum_last, heads_sum_last = tie(
        pack, units_sum_first, units_sum_last, heads_sum_last
    )
    heads_sum_first, pack = pack[:128], pack[128:]
    _, norm_one_pull = jax.vjp(lambda rows: layer_norm(rows, gain_one, bias_one), residual)
    grad_first = grad_hidden + norm_one_pull(chunks[:row_count])[0]

    passed = swap(owner(0, result, grad_first))
    kept = owner(0, grad_first, result)
    boundary = owner(0, jnp.stack([kept, passed]), jnp.stack([passed, kept]))
    boundary = boundary.reshape(1, 2, 1, row_count, model_width)

    units_sum = owner(0, units_sum_first, units_sum_last)
    heads_sum = owner(0, heads_sum_first, heads_sum_last)
    units_theirs = swap(owner(0, units_sum_last, units_sum_first))
    heads_theirs = swap(owner(0, heads_sum_last, heads_sum_first).astype(LOW))
    g_key_value = heads_sum.astype(FULL)
    g_query_out = heads_theirs.astype(FULL)
    g_w_qkv = jnp.stack([g_query_out[0:64].T, g_key_value[0:64].T, g_key_value[64:128].T], axis=1)
    g_b_qv = jnp.stack([pack[6, 384:448], pack[6, 320:384]])
    return (
        boundary,
        pack[0:1],
        pack[1:2],
        g_w_qkv[None],
        g_b_qv[None],
        g_query_out[64:128][None],
        pack[2:3],
        pack[3:4],
        pack[4:5],
        units_sum.astype(FULL).T[None],
        pack[6:7, 0:256],
        units_theirs.astype(FULL)[None],
        pack[5:6],
    )


def solution(mesh):
    return jax.shard_map(
        per_device,
        mesh=mesh,
        in_specs=(
            P(None, "ctx", "tensor", None),
            P(),
            P("section", None),
            P("section", None),
            P("section", None, None, "tensor"),
            P("section", None, "tensor"),
            P("section", "tensor", None),
            P("section", None),
            P("section", None),
            P("section", None),
            P("section", None, "tensor"),
            P("section", "tensor"),
            P("section", "tensor", None),
            P("section", None),
            P(None, "ctx", "tensor", None),
        ),
        out_specs=(
            P("section", None, "ctx", "tensor", None),
            P("section", None),
            P("section", None),
            P("section", None, None, "tensor"),
            P("section", None, "tensor"),
            P("section", "tensor", None),
            P("section", None),
            P("section", None),
            P("section", None),
            P("section", None, "tensor"),
            P("section", "tensor"),
            P("section", "tensor", None),
            P("section", None),
        ),
        check_vma=False,
    )
```

```python
import functools
import math

import jax
import jax.numpy as jnp
from jax import lax
from jax.experimental import pallas as pl
from jax.experimental.pallas import tpu as pltpu
from jax.sharding import PartitionSpec as P

HEAD_DIM = 64
EPSILON = 1e-05
MASK_FILL = -1e30
BASE_TWO_SCALE = 0.125 * math.log2(math.e)
SIDE = 4
TILE = 256
LN_TWO = math.log(2.0)
LOW = jnp.bfloat16
FULL = jnp.float32


def move_z(block, distance):
    route = [
        (x * SIDE + z, x * SIDE + (z + distance) % SIDE) for x in range(SIDE) for z in range(SIDE)
    ]
    return lax.ppermute(block, "tensor", route)


def move_x(block, distance):
    route = [
        (x * SIDE + z, (x + distance) % SIDE * SIDE + z) for x in range(SIDE) for z in range(SIDE)
    ]
    return lax.ppermute(block, "tensor", route)


def move_y(block, distance):
    return lax.ppermute(block, "ctx", [(y, (y + distance) % SIDE) for y in range(SIDE)])


def move_y_open(block, distance):
    route = [(y, y + distance) for y in range(SIDE) if 0 <= y + distance < SIDE]
    return lax.ppermute(block, "ctx", route)


def move_x_in(block, distance, section):
    base = section * SIDE * SIDE
    route = [
        (base + x * SIDE + z, base + (x + distance) % SIDE * SIDE + z)
        for x in range(SIDE)
        for z in range(SIDE)
    ]
    return lax.ppermute(block, ("section", "tensor"), route)


def move_y_in(block, distance, section):
    base = section * SIDE
    route = [(base + y, base + (y + distance) % SIDE) for y in range(SIDE)]
    return lax.ppermute(block, ("section", "ctx"), route)


def swap(block):
    return lax.ppermute(block, "section", [(0, 1), (1, 0)])


def send_to(block, section):
    return lax.ppermute(block, "section", [(1 - section, section)])


def gather_z(rows):
    return jnp.concatenate([rows] + [move_z(rows, d) for d in range(1, SIDE)], axis=0)


def scatter_z(rows):
    chunks = rows.reshape(SIDE, rows.shape[0] // SIDE, rows.shape[1])
    total = chunks[0].astype(FULL)
    for d in range(1, SIDE):
        total = total + move_z(chunks[d], -d).astype(FULL)
    return total


def even_sum(block, move):
    low = block.astype(FULL)
    return (low + move(block, 2).astype(FULL)) + (
        move(block, 1).astype(FULL) + move(block, 3).astype(FULL)
    )


def even_pairs(blocks, move):
    return (blocks[0].astype(FULL) + move(blocks[2], -2).astype(FULL)) + (
        move(blocks[1], -1).astype(FULL) + move(blocks[3], -3).astype(FULL)
    )


def layer_norm(values, gain, bias):
    center = values - jnp.mean(values, axis=-1, keepdims=True)
    spread = jnp.mean(center * center, axis=-1, keepdims=True)
    return center * lax.rsqrt(spread + EPSILON) * gain + bias


def layer_norm_back(grad, values, gain):
    center = values - jnp.mean(values, axis=-1, keepdims=True)
    scale = lax.rsqrt(jnp.mean(center * center, axis=-1, keepdims=True) + EPSILON)
    unit = center * scale
    part = grad * gain
    back = scale * (
        part
        - jnp.mean(part, axis=-1, keepdims=True)
        - unit * jnp.mean(part * unit, axis=-1, keepdims=True)
    )
    return back, jnp.sum(grad * unit, axis=0, keepdims=True), jnp.sum(grad, axis=0, keepdims=True)


def local_dot(left, right):
    return jnp.dot(left, right, preferred_element_type=FULL)


def back_dot(left, right):
    return jnp.einsum("rf,df->rd", left, right, preferred_element_type=FULL)


def outer_sum(left, right):
    return jnp.einsum("rd,rf->df", left, right, preferred_element_type=FULL)


def nt_dot(left, right):
    return lax.dot_general(left, right, (((1,), (1,)), ((), ())), preferred_element_type=FULL)


def tn_dot(left, right):
    return lax.dot_general(left, right, (((0,), (0,)), ((), ())), preferred_element_type=FULL)


def place_in_block(order, x_here, z_here):
    from_x = (x_here + (order >> 8)) & 3
    from_z = (z_here - ((order >> 6) & 3)) & 3
    return (from_x << 8) + (from_z << 6) + (order & 63)


def first_of_document(place, start_one, start_two):
    return jnp.where(place >= start_two, start_two, jnp.where(place >= start_one, start_one, 0))


def tile_bounds(scalar_ref, pair, rows_all):
    block, x_here, _, start_one, start_two = [scalar_ref[i] for i in range(5)]
    least, most = [], []
    for part in range(2):
        place = block * rows_all + ((x_here + pair * 2 + part) & 3) * TILE
        least.append(first_of_document(place, start_one, start_two))
        most.append(first_of_document(place + TILE - 1, start_one, start_two))
    return jnp.minimum(*least), jnp.maximum(*most)


def tile_limits(scalar_ref, index, rows_all):
    block, x_here, z_here, start_one, start_two = [scalar_ref[i] for i in range(5)]
    order = lax.broadcasted_iota(jnp.int32, (1, TILE), 1) + index * TILE
    high = block * rows_all + place_in_block(order, x_here, z_here)
    return first_of_document(high, start_one, start_two), high


def attend_kernel(
    scalar_ref, own_ref, kv1_ref, kv2_ref, kv3_ref, out_ref, peak, mixed, held, keys, arrived
):
    block = scalar_ref[0]
    rows_all = own_ref.shape[0]
    tiles = rows_all // TILE
    copies = [
        pltpu.make_async_copy(ref, held.at[d], arrived.at[d])
        for d, ref in enumerate((kv1_ref, kv2_ref, kv3_ref))
    ]
    for copy in copies:
        copy.start()
    peak[...] = jnp.full_like(peak, MASK_FILL)
    mixed[...] = jnp.zeros_like(mixed)
    keys[...] = place_in_block(
        lax.broadcasted_iota(jnp.int32, keys.shape, 0), scalar_ref[1], scalar_ref[2]
    )
    for d in range(SIDE):
        if d > 0:
            copies[d - 1].wait()
        start = (block - d) * rows_all

        @pl.loop(0, tiles // 2)
        def _(pair, d=d, start=start):
            least, most = tile_bounds(scalar_ref, pair, rows_all)
            indices = [pair * 2, pair * 2 + 1]

            def step(masked):
                key_values = own_ref[:, 0:128] if d == 0 else held[d - 1]
                lanes = lax.broadcasted_iota(jnp.int32, key_values.shape, 1)
                ones_values = jnp.where(lanes < HEAD_DIM, jnp.ones_like(key_values), key_values)
                raws = []
                for index in indices:
                    rows = pl.ds(pl.multiple_of(index * TILE, TILE), TILE)
                    raws.append(nt_dot(key_values, own_ref[rows, 128:256]))
                for index, raw in zip(indices, raws):
                    if masked:
                        low, high = tile_limits(scalar_ref, index, rows_all)
                        allowed = keys[...] >= low - start
                        if d == 0:
                            allowed = allowed & (keys[...] <= high - start)
                        raw = jnp.where(allowed, raw, MASK_FILL)
                    old = peak[index]
                    top = jnp.maximum(old, jnp.max(raw, axis=0, keepdims=True))
                    weight = jnp.exp2(raw - top).astype(LOW)
                    peak[index] = top
                    mixed[index] = mixed[index] * jnp.exp2(old - top) + tn_dot(ones_values, weight)

            if d == 0:
                step(True)
            else:
                reached = (block >= d) & (least < start + rows_all)
                pl.when(reached & (most <= start))(lambda: step(False))
                pl.when(reached & (most > start))(lambda: step(True))

    @pl.loop(0, tiles)
    def _(index):
        rows = pl.ds(pl.multiple_of(index * TILE, TILE), TILE)
        sums = mixed[index]
        count = sums[0:1, :]
        level = peak[index] + jnp.log2(count)
        lines = lax.broadcasted_iota(jnp.int32, sums.shape, 0)
        out_ref[rows, :] = jnp.where(lines < HEAD_DIM, level, sums / count).T


def attend_back_kernel(
    scalar_ref, own_ref, kv1_ref, kv2_ref, kv3_ref, kept_ref, grad_ref,
    dq_ref, d0_ref, d1_ref, d2_ref, d3_ref,
    query_sum, key_sum, held, keys, stats, arrived,
):
    block = scalar_ref[0]
    rows_all = own_ref.shape[0]
    tiles = rows_all // TILE
    copies = [
        pltpu.make_async_copy(ref, held.at[d], arrived.at[d])
        for d, ref in enumerate((kv1_ref, kv2_ref, kv3_ref))
    ]
    for copy in copies:
        copy.start()
    query_sum[...] = jnp.zeros_like(query_sum)
    keys[...] = place_in_block(
        lax.broadcasted_iota(jnp.int32, keys.shape, 0), scalar_ref[1], scalar_ref[2]
    )

    @pl.loop(0, tiles)
    def _(index):
        rows = pl.ds(pl.multiple_of(index * TILE, TILE), TILE)
        kept = kept_ref[rows, :]
        stats[index, 0:1, :] = kept.T[0:1, :]
        stats[index, 1:2, :] = jnp.sum((kept * grad_ref[rows, :].astype(FULL)).T, axis=0, keepdims=True)

    for d, out_ref in enumerate((d0_ref, d1_ref, d2_ref, d3_ref)):
        if d > 0:
            copies[d - 1].wait()

        @pl.when(block >= d)
        def _(d=d, out_ref=out_ref):
            start = (block - d) * rows_all
            key_sum[...] = jnp.zeros_like(key_sum)

            @pl.loop(0, tiles // 2)
            def _(pair):
                least, most = tile_bounds(scalar_ref, pair, rows_all)
                indices = [pair * 2, pair * 2 + 1]

                def step(masked):
                    key_values = own_ref[:, 0:128] if d == 0 else held[d - 1]
                    spans = [pl.ds(pl.multiple_of(index * TILE, TILE), TILE) for index in indices]
                    raws = [nt_dot(key_values, own_ref[rows, 128:256]) for rows in spans]
                    meets = [nt_dot(key_values, grad_ref[rows, :]) for rows in spans]
                    for index, rows, raw, meet in zip(indices, spans, raws, meets):
                        probs = jnp.exp2(raw - stats[index, 0:1, :])
                        if masked:
                            low, high = tile_limits(scalar_ref, index, rows_all)
                            allowed = keys[...] >= low - start
                            if d == 0:
                                allowed = allowed & (keys[...] <= high - start)
                            probs = jnp.where(allowed, probs, 0.0)
                        grad_scores = (probs * (meet - stats[index, 1:2, :])).astype(LOW)
                        key_sum[...] += local_dot(grad_scores, own_ref[rows, 128:256]) * LN_TWO + local_dot(
                            probs.astype(LOW), grad_ref[rows, :]
                        )
                        query_sum[rows, :] += tn_dot(grad_scores, key_values)

                if d == 0:
                    step(True)
                else:
                    pl.when(most <= start)(lambda: step(False))
                    pl.when((most > start) & (least < start + rows_all))(lambda: step(True))

            out_ref[...] = key_sum[...].astype(LOW)

        if d > 0:

            @pl.when(block < d)
            def _(out_ref=out_ref):
                out_ref[...] = jnp.zeros_like(out_ref)

    lanes = lax.broadcasted_iota(jnp.int32, dq_ref.shape, 1)
    dq_ref[...] = jnp.where(lanes < HEAD_DIM, query_sum[...] * 0.125, 0.0).astype(LOW)


VMEM_SPEC = pl.BlockSpec(memory_space=pltpu.VMEM)
SMEM_SPEC = pl.BlockSpec(memory_space=pltpu.SMEM)
FAR_SPEC = pl.BlockSpec(memory_space=pltpu.HBM)


def attend(spots, own, others):
    rows = own.shape[0]
    return pl.pallas_call(
        attend_kernel,
        out_shape=jax.ShapeDtypeStruct((rows, 128), FULL),
        in_specs=[SMEM_SPEC, VMEM_SPEC] + [FAR_SPEC] * 3,
        out_specs=VMEM_SPEC,
        scratch_shapes=[
            pltpu.VMEM((rows // TILE, 1, TILE), FULL),
            pltpu.VMEM((rows // TILE, 128, TILE), FULL),
            pltpu.VMEM((3, rows, 128), LOW),
            pltpu.VMEM((rows, 1), jnp.int32),
            pltpu.SemaphoreType.DMA((3,)),
        ],
        compiler_params=pltpu.CompilerParams(vmem_limit_bytes=40 << 20),
        cost_estimate=pl.CostEstimate(
            flops=4 * rows * 2 * rows * 128, bytes_accessed=4 << 20, transcendentals=rows * 2 * rows
        ),
        name="attend",
    )(spots["scalars"], own, *others)


def attend_back(spots, own, others, kept, grad):
    rows = own.shape[0]
    return pl.pallas_call(
        attend_back_kernel,
        out_shape=[jax.ShapeDtypeStruct((rows, 128), LOW)] * 5,
        in_specs=[SMEM_SPEC, VMEM_SPEC] + [FAR_SPEC] * 3 + [VMEM_SPEC] * 2,
        out_specs=[VMEM_SPEC] * 5,
        scratch_shapes=[
            pltpu.VMEM((rows, 128), FULL),
            pltpu.VMEM((rows, 128), FULL),
            pltpu.VMEM((3, rows, 128), LOW),
            pltpu.VMEM((rows, 1), jnp.int32),
            pltpu.VMEM((rows // TILE, 8, TILE), FULL),
            pltpu.SemaphoreType.DMA((3,)),
        ],
        compiler_params=pltpu.CompilerParams(vmem_limit_bytes=40 << 20),
        cost_estimate=pl.CostEstimate(
            flops=10 * rows * 2 * rows * 128, bytes_accessed=6 << 20, transcendentals=rows * 2 * rows
        ),
        name="attend_back",
    )(spots["scalars"], own, *others, kept, grad)


def tie(first, *rest):
    return lax.optimization_barrier((first, *rest))


X_GROUPS = [[x * SIDE + z for x in range(SIDE)] for z in range(SIDE)]


def forward_attention(residual, normed_all, spots, vectors, bias_qkv, w_heads, w_back, early=None):
    b_out = vectors[2]
    projected = ((nt_dot(normed_all, w_heads) + bias_qkv) * spots["scale"]).astype(LOW)
    width = projected.shape[1] // SIDE
    pieces = [projected[:, d * width : (d + 1) * width] for d in range(SIDE)]
    own = jnp.concatenate([pieces[0]] + [move_x(pieces[d], -d) for d in range(1, SIDE)], axis=0)
    if early is not None:
        own, early = tie(own, early)
    others = [move_y_open(own[:, 0:128], d) for d in range(1, SIDE)]
    kept = attend(spots, own, others)
    if early is not None:
        kept, early = tie(kept, gather_z(early))
    lanes = lax.broadcasted_iota(jnp.int32, kept.shape, 1)
    mixed = jnp.where(lanes < HEAD_DIM, 0.0, kept).astype(LOW)
    rows = mixed.shape[0] // SIDE
    mixed_rows = jnp.concatenate(
        [mixed[0:rows]] + [move_x(mixed[d * rows : (d + 1) * rows], d) for d in range(1, SIDE)], axis=1
    )
    hidden = residual + (scatter_z(local_dot(mixed_rows, w_back).astype(LOW)) + b_out)
    return hidden, (residual, normed_all, own, others, kept, mixed_rows), early


def forward_hidden_units(hidden, vectors, b_up, w_up, w_down):
    gain_two, bias_two, b_down = vectors[3:6]
    normed_two_all = gather_z(layer_norm(hidden, gain_two, bias_two).astype(LOW))
    up_value = nt_dot(normed_two_all, w_up) + b_up
    activated = jax.nn.gelu(up_value).astype(LOW)
    result = hidden + (scatter_z(local_dot(activated, w_down).astype(LOW)) + b_down)
    return result, (hidden, normed_two_all, up_value, activated)


def backward_hidden_units(grad_out, grad_down_all, stored, vectors, w_up, w_down):
    hidden, normed_two_all, up_value, activated = stored
    gain_two = vectors[3]
    grad_down = grad_out.astype(LOW)
    g_b_down = jnp.sum(grad_down.astype(FULL), axis=0, keepdims=True)
    _, gelu_pull = jax.vjp(jax.nn.gelu, up_value)
    (grad_up,) = gelu_pull(nt_dot(grad_down_all, w_down))
    grad_up = grad_up.astype(LOW)
    grad_normed_two = scatter_z(local_dot(grad_up, w_up).astype(LOW))
    g_w_down = tn_dot(activated, grad_down_all).astype(LOW)
    g_b_up = jnp.sum(grad_up.astype(FULL), axis=0)
    g_w_up = tn_dot(grad_up, normed_two_all).astype(LOW)
    grad_hidden_part, g_gain_two, g_bias_two = layer_norm_back(grad_normed_two, hidden, gain_two)
    grad_hidden = grad_out + grad_hidden_part
    return grad_hidden, (g_gain_two, g_bias_two, g_b_down), g_b_up, g_w_up, g_w_down


def backward_mixed(grad_hidden, stored, w_back, spots):
    mixed_rows = stored[5]
    grad_attn = grad_hidden.astype(LOW)
    g_b_out = jnp.sum(grad_attn.astype(FULL), axis=0, keepdims=True)
    grad_attn_all = gather_z(grad_attn)
    grad_mixed = (nt_dot(grad_attn_all, w_back) * spots["upper"]).astype(LOW)
    pieces = [grad_mixed[:, d * 128 : (d + 1) * 128] for d in range(SIDE)]
    grad_own = jnp.concatenate(
        [pieces[0]] + [move_x(pieces[d], -d) for d in range(1, SIDE)], axis=0
    )
    g_w_out = tn_dot(mixed_rows, grad_attn_all).astype(LOW)
    return grad_own, g_b_out, g_w_out


def backward_heads(parts):
    dq, dkv0, dkv1, dkv2, dkv3 = parts
    dkv = dkv0.astype(FULL)
    for d, part in enumerate((dkv1, dkv2, dkv3), 1):
        dkv = dkv + move_y_open(part, -d).astype(FULL)
    grad_own = jnp.concatenate([dkv.astype(LOW), dq], axis=1)
    rows = grad_own.shape[0] // SIDE
    return jnp.concatenate(
        [grad_own[0:rows]] + [move_x(grad_own[d * rows : (d + 1) * rows], d) for d in range(1, SIDE)],
        axis=1,
    )


def backward_entry(grad_qkv, grad_hidden, stored, vectors, w_heads):
    residual, normed_all = stored[0:2]
    gain_one = vectors[0]
    grad_normed = scatter_z(local_dot(grad_qkv, w_heads).astype(LOW))
    g_w_heads = tn_dot(grad_qkv, normed_all).astype(LOW)
    g_b_qkv = jnp.sum(grad_qkv.astype(FULL), axis=0)
    grad_residual_part, g_gain_one, g_bias_one = layer_norm_back(grad_normed, residual, gain_one)
    return grad_hidden + grad_residual_part, (g_gain_one, g_bias_one), g_b_qkv, g_w_heads


def per_device(
    inputs,
    segments,
    gain_one,
    bias_one,
    w_qkv,
    b_qv,
    w_out,
    b_out,
    gain_two,
    bias_two,
    w_up,
    b_up,
    w_down,
    b_down,
    cotangent,
):
    here = lax.axis_index("section")
    block = lax.axis_index("ctx")
    spot = lax.axis_index("tensor")
    x_here, z_here = spot // SIDE, spot % SIDE
    row_count, model_width = inputs.shape[2], inputs.shape[3]

    def owner(layer, yes, no):
        return jnp.where(here == layer, yes, no)

    sequence = lax.dynamic_index_in_dim(inputs, here, 0, False)[0].astype(FULL)
    grad_last = lax.dynamic_index_in_dim(cotangent, here, 0, False)[0].astype(FULL)
    grad_last_all = lax.dynamic_index_in_dim(cotangent, here, 0, False)[0]

    gap = jnp.zeros((HEAD_DIM,), LOW)
    biases = jnp.concatenate(
        [b_up[0], gap, b_qv[0, 1], b_qv[0, 0], gap, jnp.zeros((model_width - 512,), LOW)]
    )[None]
    heads_kv = jnp.concatenate(
        [w_qkv[0, :, 1].T, w_qkv[0, :, 2].T, biases, jnp.zeros((15, model_width), LOW)], axis=0
    )
    heads_qo = jnp.concatenate(
        [w_qkv[0, :, 0].T, w_out[0], jnp.zeros((16, model_width), LOW)], axis=0
    )
    heads_qo_other = swap(heads_qo)
    small = jnp.concatenate(
        [gain_one, bias_one, b_out, gain_two, bias_two, b_down, jnp.zeros((2, model_width), LOW)],
        axis=0,
    )
    small_other = swap(small)
    up_own, down_other = w_up[0].T, swap(w_down[0])
    downward = [(x_here - d) % SIDE for d in range(SIDE)]

    def reorder(pieces):
        return [lax.dynamic_index_in_dim(pieces, place, 0, False) for place in downward]

    def half_heads(layer):
        return owner(layer, heads_kv, heads_qo_other)

    def join_heads(layer, mine, theirs):
        key_value, query_out = owner(layer, mine, theirs), owner(layer, theirs, mine)
        whole = jnp.concatenate([key_value[:, :128], query_out[:, :128]], axis=1)
        back = query_out[:, :128].reshape(SIDE * 128, model_width)
        rows = key_value[:, 128, :512].astype(FULL)
        bias_heads = rows[:, 256:].reshape(1, SIDE * TILE)
        bias_up = jnp.concatenate(reorder(rows[:, :256])).reshape(1, SIDE * TILE)
        return (whole.reshape(SIDE * TILE, model_width), back), bias_heads, bias_up

    def gather_whole(half):
        return lax.all_gather(half, "tensor", axis=0, tiled=True, axis_index_groups=X_GROUPS)

    def join_units(layer, mine):
        theirs = swap(mine)
        return owner(layer, mine, theirs), owner(layer, theirs, mine)

    smalls = (owner(0, small, small_other), owner(0, small_other, small))
    vectors = [
        tuple(smalls[layer][row : row + 1].astype(FULL) for row in range(6)) for layer in range(2)
    ]
    normed = layer_norm(sequence, *vectors[0][0:2]).astype(LOW)
    half, normed = tie(half_heads(0), normed)
    mine = jnp.stack([half] + [move_x(half, d) for d in range(1, SIDE)])
    half = owner(0, up_own, down_other)
    normed_all, mine, half = tie(gather_z(normed), mine, half)
    heads_first, bias_heads_first, bias_up_first = join_heads(0, mine, swap(mine))
    units_first = gather_whole(half)
    heads_last = gather_whole(half_heads(1)).reshape(SIDE, -1, model_width)
    units_last = gather_whole(owner(1, up_own, down_other))
    normed_all, segments = tie(normed_all, segments)
    segment_ids = lax.dynamic_index_in_dim(segments, here, 0, False)
    start_one = jnp.sum((segment_ids < 1).astype(jnp.int32))
    start_two = jnp.sum((segment_ids < 2).astype(jnp.int32))

    lane = jnp.arange(SIDE * TILE) % TILE
    spots = {
        "scalars": jnp.stack([block, x_here, z_here, start_one, start_two]).astype(jnp.int32),
        "scale": jnp.where(lane < 128, 1.0, jnp.where(lane < 192, BASE_TWO_SCALE, 0.0)).astype(FULL),
        "upper": (jnp.arange(SIDE * 128) % 128 >= HEAD_DIM).astype(FULL),
    }

    hidden, kept_heads_first, grad_last_all = forward_attention(
        sequence, normed_all, spots, vectors[0], bias_heads_first, *heads_first, grad_last_all
    )
    units_first = join_units(0, units_first)
    middle, kept_units_first = forward_hidden_units(hidden, vectors[0], bias_up_first, *units_first)
    mine = jnp.stack(reorder(heads_last))
    middle, mine, theirs = tie(middle, mine, swap(mine))
    heads_last, bias_heads_last, bias_up_last = join_heads(1, mine, theirs)
    middle = middle.astype(LOW).astype(FULL)
    normed_all = gather_z(layer_norm(middle, *vectors[1][0:2]).astype(LOW))
    hidden, kept_heads_last, _ = forward_attention(
        middle, normed_all, spots, vectors[1], bias_heads_last, *heads_last
    )
    units_last = join_units(1, units_last)
    result, kept_units_last = forward_hidden_units(hidden, vectors[1], bias_up_last, *units_last)

    def swap_grads(layer, first, second):
        return owner(layer, first, second), swap(owner(layer, second, first))

    def add_grads(kept, arrived):
        return (kept.astype(FULL) + arrived.astype(FULL)).astype(LOW)

    def scatter_whole(grads):
        return lax.psum_scatter(
            grads, "tensor", scatter_dimension=0, tiled=True, axis_index_groups=X_GROUPS
        )

    def split_heads(g_w_heads, g_w_out):
        heads = g_w_heads.reshape(SIDE, TILE, model_width)
        return heads[:, 0:128], heads[:, 128:256] + g_w_out.reshape(SIDE, 128, model_width)

    turn = jnp.stack(downward)[None, :] == jnp.arange(SIDE)[:, None]

    def pack_vectors(heads, units, g_b_out, g_b_up, g_b_qkv):
        by_turn = jnp.sum(
            jnp.where(turn[:, :, None], g_b_up.reshape(SIDE, 1, TILE), 0.0), axis=0
        )
        return jnp.concatenate(
            [
                *heads, g_b_out, *units,
                jnp.concatenate([by_turn, g_b_qkv.reshape(SIDE, TILE)], axis=1).reshape(2, -1),
            ],
            axis=0,
        )

    grad_hidden, vec_units_last, g_b_up_last, g_up, g_down = backward_hidden_units(
        grad_last, grad_last_all, kept_units_last, vectors[1], *units_last
    )
    grad_hidden, units_kept, units_arrived = tie(grad_hidden, *swap_grads(1, g_up, g_down))
    units_sum_last = scatter_whole(add_grads(units_kept, units_arrived))
    grad_mixed, g_b_out_last, g_out = backward_mixed(grad_hidden, kept_heads_last, heads_last[1], spots)
    grad_qkv = backward_heads(attend_back(spots, *kept_heads_last[2:5], grad_mixed))
    grad_middle, vec_heads_last, g_b_qkv_last, g_heads = backward_entry(
        grad_qkv, grad_hidden, kept_heads_last, vectors[1], heads_last[0]
    )
    heads_kept, heads_arrived = swap_grads(1, *split_heads(g_heads, g_out))

    grad_middle = grad_middle.astype(LOW).astype(FULL)
    grad_down_all, heads_kept, heads_arrived = tie(
        gather_z(grad_middle.astype(LOW)), heads_kept, heads_arrived
    )
    heads_sum_last = scatter_whole(
        jnp.concatenate(reorder(add_grads(heads_kept, heads_arrived)), axis=0)
    )
    grad_hidden, vec_units_first, g_b_up_first, g_up, g_down = backward_hidden_units(
        grad_middle, grad_down_all, kept_units_first, vectors[0], *units_first
    )
    grad_hidden, units_kept, units_arrived, units_sum_last = tie(
        grad_hidden, *swap_grads(0, g_up, g_down), units_sum_last
    )
    units_sum_first = scatter_whole(add_grads(units_kept, units_arrived))
    grad_mixed, g_b_out_first, g_out = backward_mixed(grad_hidden, kept_heads_first, heads_first[1], spots)
    parts = attend_back(spots, *kept_heads_first[2:5], grad_mixed)
    parts, units_sum_first, heads_sum_last = tie(parts, units_sum_first, heads_sum_last)
    units_sum_first, units_sum_last, heads_sum_last = lax.psum(
        (units_sum_first, units_sum_last, heads_sum_last), "ctx"
    )
    grad_qkv = backward_heads(parts)

    gain_one, bias_one = vectors[0][0:2]
    residual, normed_all = kept_heads_first[0:2]
    grad_normed = local_dot(grad_qkv, heads_first[0])
    g_bias_one = jnp.sum(grad_normed, axis=0, keepdims=True)
    g_gain_one = jnp.sum(grad_normed * ((normed_all.astype(FULL) - bias_one) / gain_one), axis=0, keepdims=True)
    g_b_qkv_first = jnp.sum(grad_qkv.astype(FULL), axis=0)
    sums_first = pack_vectors(
        (g_gain_one, g_bias_one), vec_units_first, g_b_out_first, g_b_up_first, g_b_qkv_first
    )
    sums_last = pack_vectors(vec_heads_last, vec_units_last, g_b_out_last, g_b_up_last, g_b_qkv_last)
    common = jnp.pad(jnp.concatenate([sums_first[:6], sums_last[:6]]), ((0, 4), (0, 0))).astype(LOW)
    chunks = grad_normed.astype(LOW).reshape(SIDE, row_count, model_width)
    chunks = even_pairs([jnp.concatenate([chunks[d], common], axis=0) for d in range(SIDE)], move_z)
    heads_kept, heads_arrived = swap_grads(0, *split_heads(tn_dot(grad_qkv, normed_all).astype(LOW), g_out))
    halves = add_grads(heads_kept, heads_arrived)
    sums_first = jnp.concatenate([chunks[row_count : row_count + 6], sums_first[6:]])
    sums_last = jnp.concatenate([chunks[row_count + 6 : row_count + 12], sums_last[6:]])
    sums = owner(0, sums_first, sums_last) + swap(owner(0, sums_last, sums_first))
    common = sums[:6].astype(LOW)
    split = sums[6:].reshape(SIDE, 1, 512).astype(LOW)
    packs = [
        jnp.concatenate(
            [
                common,
                jnp.pad(split[d], ((0, 0), (0, model_width - 512))),
                jnp.zeros((9, model_width), LOW),
            ],
            axis=0,
        )
        for d in range(SIDE)
    ]
    pack = jnp.concatenate([even_pairs(halves, move_x), even_pairs(packs, move_x)], axis=0)
    pack = even_sum(pack.astype(LOW), move_y)
    pack, units_sum_first, units_sum_last, heads_sum_last = tie(
        pack, units_sum_first, units_sum_last, heads_sum_last
    )
    heads_sum_first, pack = pack[:128], pack[128:]
    grad_first = grad_hidden + layer_norm_back(chunks[:row_count], residual, gain_one)[0]

    passed = swap(owner(0, result, grad_first))
    kept = owner(0, grad_first, result)
    boundary = owner(0, jnp.stack([kept, passed]), jnp.stack([passed, kept]))
    boundary = boundary.reshape(1, 2, 1, row_count, model_width)

    units_sum = owner(0, units_sum_first, units_sum_last)
    heads_sum = owner(0, heads_sum_first, heads_sum_last)
    units_theirs = swap(owner(0, units_sum_last, units_sum_first))
    heads_theirs = swap(owner(0, heads_sum_last, heads_sum_first).astype(LOW))
    g_key_value = heads_sum.astype(FULL)
    g_query_out = heads_theirs.astype(FULL)
    g_w_qkv = jnp.stack([g_query_out[0:64].T, g_key_value[0:64].T, g_key_value[64:128].T], axis=1)
    g_b_qv = jnp.stack([pack[6, 384:448], pack[6, 320:384]])
    return (
        boundary,
        pack[0:1],
        pack[1:2],
        g_w_qkv[None],
        g_b_qv[None],
        g_query_out[64:128][None],
        pack[2:3],
        pack[3:4],
        pack[4:5],
        units_sum.astype(FULL).T[None],
        pack[6:7, 0:256],
        units_theirs.astype(FULL)[None],
        pack[5:6],
    )


def solution(mesh):
    return jax.shard_map(
        per_device,
        mesh=mesh,
        in_specs=(
            P(None, "ctx", "tensor", None),
            P(),
            P("section", None),
            P("section", None),
            P("section", None, None, "tensor"),
            P("section", None, "tensor"),
            P("section", "tensor", None),
            P("section", None),
            P("section", None),
            P("section", None),
            P("section", None, "tensor"),
            P("section", "tensor"),
            P("section", "tensor", None),
            P("section", None),
            P(None, "ctx", "tensor", None),
        ),
        out_specs=(
            P("section", None, "ctx", "tensor", None),
            P("section", None),
            P("section", None),
            P("section", None, None, "tensor"),
            P("section", None, "tensor"),
            P("section", "tensor", None),
            P("section", None),
            P("section", None),
            P("section", None),
            P("section", None, "tensor"),
            P("section", "tensor"),
            P("section", "tensor", None),
            P("section", None),
        ),
        check_vma=False,
    )
```

```python
import functools
import math

import jax
import jax.numpy as jnp
from jax import lax
from jax.experimental import pallas as pl
from jax.experimental.pallas import tpu as pltpu
from jax.sharding import PartitionSpec as P

HEAD_DIM = 64
EPSILON = 1e-05
MASK_FILL = -1e30
BASE_TWO_SCALE = 0.125 * math.log2(math.e)
SIDE = 4
TILE = 256
LN_TWO = math.log(2.0)
LOW = jnp.bfloat16
FULL = jnp.float32


def move_z(block, distance):
    route = [
        (x * SIDE + z, x * SIDE + (z + distance) % SIDE) for x in range(SIDE) for z in range(SIDE)
    ]
    return lax.ppermute(block, "tensor", route)


def move_x(block, distance):
    route = [
        (x * SIDE + z, (x + distance) % SIDE * SIDE + z) for x in range(SIDE) for z in range(SIDE)
    ]
    return lax.ppermute(block, "tensor", route)


def move_y(block, distance):
    return lax.ppermute(block, "ctx", [(y, (y + distance) % SIDE) for y in range(SIDE)])


def move_y_open(block, distance):
    route = [(y, y + distance) for y in range(SIDE) if 0 <= y + distance < SIDE]
    return lax.ppermute(block, "ctx", route)


def move_x_in(block, distance, section):
    base = section * SIDE * SIDE
    route = [
        (base + x * SIDE + z, base + (x + distance) % SIDE * SIDE + z)
        for x in range(SIDE)
        for z in range(SIDE)
    ]
    return lax.ppermute(block, ("section", "tensor"), route)


def move_y_in(block, distance, section):
    base = section * SIDE
    route = [(base + y, base + (y + distance) % SIDE) for y in range(SIDE)]
    return lax.ppermute(block, ("section", "ctx"), route)


def swap(block):
    return lax.ppermute(block, "section", [(0, 1), (1, 0)])


def send_to(block, section):
    return lax.ppermute(block, "section", [(1 - section, section)])


def gather_z(rows):
    return jnp.concatenate([rows] + [move_z(rows, d) for d in range(1, SIDE)], axis=0)


def scatter_z(rows):
    chunks = rows.reshape(SIDE, rows.shape[0] // SIDE, rows.shape[1])
    total = chunks[0].astype(FULL)
    for d in range(1, SIDE):
        total = total + move_z(chunks[d], -d).astype(FULL)
    return total


def even_sum(block, move):
    low = block.astype(FULL)
    return (low + move(block, 2).astype(FULL)) + (
        move(block, 1).astype(FULL) + move(block, 3).astype(FULL)
    )


def even_pairs(blocks, move):
    return (blocks[0].astype(FULL) + move(blocks[2], -2).astype(FULL)) + (
        move(blocks[1], -1).astype(FULL) + move(blocks[3], -3).astype(FULL)
    )


def layer_norm(values, gain, bias):
    center = values - jnp.mean(values, axis=-1, keepdims=True)
    spread = jnp.mean(center * center, axis=-1, keepdims=True)
    return center * lax.rsqrt(spread + EPSILON) * gain + bias


def column_sum(rows):
    ones = jnp.ones((8, rows.shape[0]), rows.dtype)
    return jnp.dot(
        ones, rows, precision=lax.Precision.HIGHEST, preferred_element_type=FULL
    )[0:1]


def layer_norm_back(grad, values, gain):
    center = values - jnp.mean(values, axis=-1, keepdims=True)
    scale = lax.rsqrt(jnp.mean(center * center, axis=-1, keepdims=True) + EPSILON)
    unit = center * scale
    part = grad * gain
    back = scale * (
        part
        - jnp.mean(part, axis=-1, keepdims=True)
        - unit * jnp.mean(part * unit, axis=-1, keepdims=True)
    )
    return back, column_sum(grad * unit), column_sum(grad)


def local_dot(left, right):
    return jnp.dot(left, right, preferred_element_type=FULL)


def back_dot(left, right):
    return jnp.einsum("rf,df->rd", left, right, preferred_element_type=FULL)


def outer_sum(left, right):
    return jnp.einsum("rd,rf->df", left, right, preferred_element_type=FULL)


def nt_dot(left, right):
    return lax.dot_general(left, right, (((1,), (1,)), ((), ())), preferred_element_type=FULL)


def tn_dot(left, right):
    return lax.dot_general(left, right, (((0,), (0,)), ((), ())), preferred_element_type=FULL)


def place_in_block(order, x_here, z_here):
    from_x = (x_here + (order >> 8)) & 3
    from_z = (z_here - ((order >> 6) & 3)) & 3
    return (from_x << 8) + (from_z << 6) + (order & 63)


def first_of_document(place, start_one, start_two):
    return jnp.where(place >= start_two, start_two, jnp.where(place >= start_one, start_one, 0))


def tile_bounds(scalar_ref, indices, rows_all):
    block, x_here, _, start_one, start_two = [scalar_ref[i] for i in range(5)]
    least, most = [], []
    for index in indices:
        place = block * rows_all + ((x_here + index) & 3) * TILE
        least.append(first_of_document(place, start_one, start_two))
        most.append(first_of_document(place + TILE - 1, start_one, start_two))
    return functools.reduce(jnp.minimum, least), functools.reduce(jnp.maximum, most)


def tile_limits(scalar_ref, index, rows_all):
    block, x_here, z_here, start_one, start_two = [scalar_ref[i] for i in range(5)]
    order = lax.broadcasted_iota(jnp.int32, (1, TILE), 1) + index * TILE
    high = block * rows_all + place_in_block(order, x_here, z_here)
    return first_of_document(high, start_one, start_two), high


def attend_kernel(
    scalar_ref, own_ref, kv1_ref, kv2_ref, kv3_ref, out_ref, peak, mixed, held, keys, arrived
):
    block = scalar_ref[0]
    rows_all = own_ref.shape[0]
    tiles = rows_all // TILE
    copies = [
        pltpu.make_async_copy(ref, held.at[d], arrived.at[d])
        for d, ref in enumerate((kv1_ref, kv2_ref, kv3_ref))
    ]
    for copy in copies:
        copy.start()
    peak[...] = jnp.full_like(peak, MASK_FILL)
    mixed[...] = jnp.zeros_like(mixed)
    keys[...] = place_in_block(
        lax.broadcasted_iota(jnp.int32, keys.shape, 0), scalar_ref[1], scalar_ref[2]
    )
    for d in range(SIDE):
        if d > 0:
            copies[d - 1].wait()
        start = (block - d) * rows_all

        @pl.loop(0, tiles // 2)
        def _(pair, d=d, start=start):
            indices = [pair * 2, pair * 2 + 1]
            least, most = tile_bounds(scalar_ref, indices, rows_all)

            def step(masked):
                key_values = own_ref[:, 0:128] if d == 0 else held[d - 1]
                lanes = lax.broadcasted_iota(jnp.int32, key_values.shape, 1)
                ones_values = jnp.where(lanes < HEAD_DIM, jnp.ones_like(key_values), key_values)
                raws = []
                for index in indices:
                    rows = pl.ds(pl.multiple_of(index * TILE, TILE), TILE)
                    raws.append(nt_dot(key_values, own_ref[rows, 128:256]))
                for index, raw in zip(indices, raws):
                    if masked:
                        low, high = tile_limits(scalar_ref, index, rows_all)
                        allowed = keys[...] >= low - start
                        if d == 0:
                            allowed = allowed & (keys[...] <= high - start)
                        raw = jnp.where(allowed, raw, MASK_FILL)
                    old = peak[index]
                    top = jnp.maximum(old, jnp.max(raw, axis=0, keepdims=True))
                    weight = jnp.exp2(raw - top).astype(LOW)
                    peak[index] = top
                    mixed[index] = mixed[index] * jnp.exp2(old - top) + tn_dot(ones_values, weight)

            if d == 0:
                step(True)
            else:
                reached = (block >= d) & (least < start + rows_all)
                pl.when(reached & (most <= start))(lambda: step(False))
                pl.when(reached & (most > start))(lambda: step(True))

    @pl.loop(0, tiles)
    def _(index):
        rows = pl.ds(pl.multiple_of(index * TILE, TILE), TILE)
        sums = mixed[index]
        count = sums[0:1, :]
        level = peak[index] + jnp.log2(count)
        lines = lax.broadcasted_iota(jnp.int32, sums.shape, 0)
        out_ref[rows, :] = jnp.where(lines < HEAD_DIM, level, sums / count).T


def attend_back_kernel(
    scalar_ref, own_ref, kv1_ref, kv2_ref, kv3_ref, kept_ref, grad_ref,
    dq_ref, d0_ref, d1_ref, d2_ref, d3_ref,
    query_sum, key_sum, held, keys, stats, arrived,
):
    block = scalar_ref[0]
    rows_all = own_ref.shape[0]
    tiles = rows_all // TILE
    copies = [
        pltpu.make_async_copy(ref, held.at[d], arrived.at[d])
        for d, ref in enumerate((kv1_ref, kv2_ref, kv3_ref))
    ]
    for copy in copies:
        copy.start()
    query_sum[...] = jnp.zeros_like(query_sum)
    keys[...] = place_in_block(
        lax.broadcasted_iota(jnp.int32, keys.shape, 0), scalar_ref[1], scalar_ref[2]
    )

    @pl.loop(0, tiles)
    def _(index):
        rows = pl.ds(pl.multiple_of(index * TILE, TILE), TILE)
        kept = kept_ref[rows, :]
        stats[index, 0:1, :] = kept.T[0:1, :]
        stats[index, 1:2, :] = jnp.sum((kept * grad_ref[rows, :].astype(FULL)).T, axis=0, keepdims=True)

    for d, out_ref in enumerate((d0_ref, d1_ref, d2_ref, d3_ref)):
        if d > 0:
            copies[d - 1].wait()

        @pl.when(block >= d)
        def _(d=d, out_ref=out_ref):
            start = (block - d) * rows_all
            key_sum[...] = jnp.zeros_like(key_sum)

            @pl.loop(0, tiles)
            def _(index):
                indices = [index]
                least, most = tile_bounds(scalar_ref, indices, rows_all)

                def step(masked):
                    key_values = own_ref[:, 0:128] if d == 0 else held[d - 1]
                    spans = [pl.ds(pl.multiple_of(index * TILE, TILE), TILE) for index in indices]
                    raws = [nt_dot(key_values, own_ref[rows, 128:256]) for rows in spans]
                    meets = [nt_dot(key_values, grad_ref[rows, :]) for rows in spans]
                    for index, rows, raw, meet in zip(indices, spans, raws, meets):
                        probs = jnp.exp2(raw - stats[index, 0:1, :])
                        if masked:
                            low, high = tile_limits(scalar_ref, index, rows_all)
                            allowed = keys[...] >= low - start
                            if d == 0:
                                allowed = allowed & (keys[...] <= high - start)
                            probs = jnp.where(allowed, probs, 0.0)
                        grad_scores = (probs * (meet - stats[index, 1:2, :])).astype(LOW)
                        key_sum[...] += local_dot(grad_scores, own_ref[rows, 128:256]) * LN_TWO + local_dot(
                            probs.astype(LOW), grad_ref[rows, :]
                        )
                        query_sum[rows, :] += tn_dot(grad_scores, key_values)

                if d == 0:
                    step(True)
                else:
                    pl.when(most <= start)(lambda: step(False))
                    pl.when((most > start) & (least < start + rows_all))(lambda: step(True))

            out_ref[...] = key_sum[...].astype(LOW)

        if d > 0:

            @pl.when(block < d)
            def _(out_ref=out_ref):
                out_ref[...] = jnp.zeros_like(out_ref)

    lanes = lax.broadcasted_iota(jnp.int32, dq_ref.shape, 1)
    dq_ref[...] = jnp.where(lanes < HEAD_DIM, query_sum[...] * 0.125, 0.0).astype(LOW)


VMEM_SPEC = pl.BlockSpec(memory_space=pltpu.VMEM)
SMEM_SPEC = pl.BlockSpec(memory_space=pltpu.SMEM)
FAR_SPEC = pl.BlockSpec(memory_space=pltpu.HBM)


def attend(spots, own, others):
    rows = own.shape[0]
    return pl.pallas_call(
        attend_kernel,
        out_shape=jax.ShapeDtypeStruct((rows, 128), FULL),
        in_specs=[SMEM_SPEC, VMEM_SPEC] + [FAR_SPEC] * 3,
        out_specs=VMEM_SPEC,
        scratch_shapes=[
            pltpu.VMEM((rows // TILE, 1, TILE), FULL),
            pltpu.VMEM((rows // TILE, 128, TILE), FULL),
            pltpu.VMEM((3, rows, 128), LOW),
            pltpu.VMEM((rows, 1), jnp.int32),
            pltpu.SemaphoreType.DMA((3,)),
        ],
        compiler_params=pltpu.CompilerParams(vmem_limit_bytes=40 << 20),
        cost_estimate=pl.CostEstimate(
            flops=4 * rows * 2 * rows * 128, bytes_accessed=4 << 20, transcendentals=rows * 2 * rows
        ),
        name="attend",
    )(spots["scalars"], own, *others)


def attend_back(spots, own, others, kept, grad):
    rows = own.shape[0]
    return pl.pallas_call(
        attend_back_kernel,
        out_shape=[jax.ShapeDtypeStruct((rows, 128), LOW)] * 5,
        in_specs=[SMEM_SPEC, VMEM_SPEC] + [FAR_SPEC] * 3 + [VMEM_SPEC] * 2,
        out_specs=[VMEM_SPEC] * 5,
        scratch_shapes=[
            pltpu.VMEM((rows, 128), FULL),
            pltpu.VMEM((rows, 128), FULL),
            pltpu.VMEM((3, rows, 128), LOW),
            pltpu.VMEM((rows, 1), jnp.int32),
            pltpu.VMEM((rows // TILE, 8, TILE), FULL),
            pltpu.SemaphoreType.DMA((3,)),
        ],
        compiler_params=pltpu.CompilerParams(vmem_limit_bytes=40 << 20),
        cost_estimate=pl.CostEstimate(
            flops=10 * rows * 2 * rows * 128, bytes_accessed=6 << 20, transcendentals=rows * 2 * rows
        ),
        name="attend_back",
    )(spots["scalars"], own, *others, kept, grad)


def tie(first, *rest):
    return lax.optimization_barrier((first, *rest))


X_GROUPS = [[x * SIDE + z for x in range(SIDE)] for z in range(SIDE)]


def forward_attention(residual, normed_all, spots, vectors, bias_qkv, w_heads, w_back):
    b_out = vectors[2]
    projected = ((nt_dot(normed_all, w_heads) + bias_qkv) * spots["scale"]).astype(LOW)
    width = projected.shape[1] // SIDE
    pieces = [projected[:, d * width : (d + 1) * width] for d in range(SIDE)]
    own = jnp.concatenate([pieces[0]] + [move_x(pieces[d], -d) for d in range(1, SIDE)], axis=0)
    others = [move_y_open(own[:, 0:128], d) for d in range(1, SIDE)]
    kept = attend(spots, own, others)
    lanes = lax.broadcasted_iota(jnp.int32, kept.shape, 1)
    mixed = jnp.where(lanes < HEAD_DIM, 0.0, kept).astype(LOW)
    rows = mixed.shape[0] // SIDE
    mixed_rows = jnp.concatenate(
        [mixed[0:rows]] + [move_x(mixed[d * rows : (d + 1) * rows], d) for d in range(1, SIDE)], axis=1
    )
    hidden = residual + (scatter_z(local_dot(mixed_rows, w_back).astype(LOW)) + b_out)
    return hidden, (residual, normed_all, own, others, kept, mixed_rows)


def forward_hidden_units(hidden, vectors, b_up, w_up, w_down):
    gain_two, bias_two, b_down = vectors[3:6]
    normed_two_all = gather_z(layer_norm(hidden, gain_two, bias_two).astype(LOW))
    up_value = nt_dot(normed_two_all, w_up) + b_up
    activated = jax.nn.gelu(up_value).astype(LOW)
    result = hidden + (scatter_z(local_dot(activated, w_down).astype(LOW)) + b_down)
    return result, (hidden, normed_two_all, up_value, activated)


def backward_hidden_units(grad_out, grad_down_all, stored, vectors, w_up, w_down):
    hidden, normed_two_all, up_value, activated = stored
    gain_two = vectors[3]
    grad_down = grad_out.astype(LOW)
    g_b_down = column_sum(grad_down)
    _, gelu_pull = jax.vjp(jax.nn.gelu, up_value)
    (grad_up,) = gelu_pull(nt_dot(grad_down_all, w_down))
    grad_up = grad_up.astype(LOW)
    grad_normed_two = scatter_z(local_dot(grad_up, w_up).astype(LOW))
    g_w_down = tn_dot(activated, grad_down_all).astype(LOW)
    g_b_up = jnp.sum(grad_up.astype(FULL), axis=0)
    g_w_up = tn_dot(grad_up, normed_two_all).astype(LOW)
    grad_hidden_part, g_gain_two, g_bias_two = layer_norm_back(grad_normed_two, hidden, gain_two)
    grad_hidden = grad_out + grad_hidden_part
    return grad_hidden, (g_gain_two, g_bias_two, g_b_down), g_b_up, g_w_up, g_w_down


def backward_mixed(grad_hidden, stored, w_back, spots, side):
    mixed_rows = stored[5]
    grad_attn = grad_hidden.astype(LOW)
    g_b_out = column_sum(grad_attn)
    grad_attn_all, side = tie(gather_z(grad_attn), side)
    grad_mixed = (nt_dot(grad_attn_all, w_back) * spots["upper"]).astype(LOW)
    pieces = [grad_mixed[:, d * 128 : (d + 1) * 128] for d in range(SIDE)]
    grad_own = jnp.concatenate(
        [pieces[0]] + [move_x(pieces[d], -d) for d in range(1, SIDE)], axis=0
    )
    g_w_out = tn_dot(mixed_rows, grad_attn_all).astype(LOW)
    return grad_own, g_b_out, g_w_out, side


def backward_heads(parts, *side):
    dq, dkv0, dkv1, dkv2, dkv3 = parts
    dkv = dkv0.astype(FULL)
    for d, part in enumerate((dkv1, dkv2, dkv3), 1):
        dkv = dkv + move_y_open(part, -d).astype(FULL)
    grad_own = jnp.concatenate([dkv.astype(LOW), dq], axis=1)
    if side:
        grad_own, *side = tie(grad_own, *side)
    rows = grad_own.shape[0] // SIDE
    grad_qkv = jnp.concatenate(
        [grad_own[0:rows]] + [move_x(grad_own[d * rows : (d + 1) * rows], d) for d in range(1, SIDE)],
        axis=1,
    )
    return (grad_qkv, *side) if side else grad_qkv


def backward_entry(grad_qkv, grad_hidden, stored, vectors, w_heads):
    residual, normed_all = stored[0:2]
    gain_one = vectors[0]
    grad_normed = scatter_z(local_dot(grad_qkv, w_heads).astype(LOW))
    g_w_heads = tn_dot(grad_qkv, normed_all).astype(LOW)
    g_b_qkv = jnp.sum(grad_qkv.astype(FULL), axis=0)
    grad_residual_part, g_gain_one, g_bias_one = layer_norm_back(grad_normed, residual, gain_one)
    return grad_hidden + grad_residual_part, (g_gain_one, g_bias_one), g_b_qkv, g_w_heads


def per_device(
    inputs,
    segments,
    gain_one,
    bias_one,
    w_qkv,
    b_qv,
    w_out,
    b_out,
    gain_two,
    bias_two,
    w_up,
    b_up,
    w_down,
    b_down,
    cotangent,
):
    here = lax.axis_index("section")
    block = lax.axis_index("ctx")
    spot = lax.axis_index("tensor")
    x_here, z_here = spot // SIDE, spot % SIDE
    row_count, model_width = inputs.shape[2], inputs.shape[3]

    def owner(layer, yes, no):
        return jnp.where(here == layer, yes, no)

    sequence = lax.dynamic_index_in_dim(inputs, here, 0, False)[0].astype(FULL)
    grad_last = lax.dynamic_index_in_dim(cotangent, here, 0, False)[0].astype(FULL)
    grad_last_all = lax.dynamic_index_in_dim(cotangent, here, 0, False)[0]

    gap = jnp.zeros((HEAD_DIM,), LOW)
    biases = jnp.concatenate(
        [b_up[0], gap, b_qv[0, 1], b_qv[0, 0], gap, jnp.zeros((model_width - 512,), LOW)]
    )[None]
    heads_kv = jnp.concatenate(
        [w_qkv[0, :, 1].T, w_qkv[0, :, 2].T, biases, jnp.zeros((15, model_width), LOW)], axis=0
    )
    heads_qo = jnp.concatenate(
        [w_qkv[0, :, 0].T, w_out[0], jnp.zeros((16, model_width), LOW)], axis=0
    )
    heads_qo_other = swap(heads_qo)
    small = jnp.concatenate(
        [gain_one, bias_one, b_out, gain_two, bias_two, b_down, jnp.zeros((2, model_width), LOW)],
        axis=0,
    )
    small_other = swap(small)
    up_own, down_other = w_up[0].T, swap(w_down[0])
    downward = [(x_here - d) % SIDE for d in range(SIDE)]

    def reorder(pieces):
        return [lax.dynamic_index_in_dim(pieces, place, 0, False) for place in downward]

    def half_heads(layer):
        return owner(layer, heads_kv, heads_qo_other)

    def join_heads(layer, mine, theirs):
        key_value, query_out = owner(layer, mine, theirs), owner(layer, theirs, mine)
        whole = jnp.concatenate([key_value[:, :128], query_out[:, :128]], axis=1)
        back = query_out[:, :128].reshape(SIDE * 128, model_width)
        rows = key_value[:, 128, :512].astype(FULL)
        bias_heads = rows[:, 256:].reshape(1, SIDE * TILE)
        bias_up = jnp.concatenate(reorder(rows[:, :256])).reshape(1, SIDE * TILE)
        return (whole.reshape(SIDE * TILE, model_width), back), bias_heads, bias_up

    def gather_whole(half):
        return lax.all_gather(half, "tensor", axis=0, tiled=True, axis_index_groups=X_GROUPS)

    def join_units(layer, mine):
        theirs = swap(mine)
        return owner(layer, mine, theirs), owner(layer, theirs, mine)

    smalls = (owner(0, small, small_other), owner(0, small_other, small))
    vectors = [
        tuple(smalls[layer][row : row + 1].astype(FULL) for row in range(6)) for layer in range(2)
    ]
    normed = layer_norm(sequence, *vectors[0][0:2]).astype(LOW)
    half, normed = tie(half_heads(0), normed)
    mine = jnp.stack([half] + [move_x(half, d) for d in range(1, SIDE)])
    half = owner(0, up_own, down_other)
    normed_all, mine, half, grad_last_all = tie(gather_z(normed), mine, half, gather_z(grad_last_all))
    heads_first, bias_heads_first, bias_up_first = join_heads(0, mine, swap(mine))
    units_first = gather_whole(half)
    heads_last = gather_whole(half_heads(1)).reshape(SIDE, -1, model_width)
    units_last = gather_whole(owner(1, up_own, down_other))
    normed_all, segments = tie(normed_all, segments)
    segment_ids = lax.dynamic_index_in_dim(segments, here, 0, False)
    start_one = jnp.sum((segment_ids < 1).astype(jnp.int32))
    start_two = jnp.sum((segment_ids < 2).astype(jnp.int32))

    lane = jnp.arange(SIDE * TILE) % TILE
    spots = {
        "scalars": jnp.stack([block, x_here, z_here, start_one, start_two]).astype(jnp.int32),
        "scale": jnp.where(lane < 128, 1.0, jnp.where(lane < 192, BASE_TWO_SCALE, 0.0)).astype(FULL),
        "upper": (jnp.arange(SIDE * 128) % 128 >= HEAD_DIM).astype(FULL),
    }

    hidden, kept_heads_first = forward_attention(
        sequence, normed_all, spots, vectors[0], bias_heads_first, *heads_first
    )
    units_first = join_units(0, units_first)
    middle, kept_units_first = forward_hidden_units(hidden, vectors[0], bias_up_first, *units_first)
    mine = jnp.stack(reorder(heads_last))
    middle, mine, theirs = tie(middle, mine, swap(mine))
    heads_last, bias_heads_last, bias_up_last = join_heads(1, mine, theirs)
    middle = middle.astype(LOW).astype(FULL)
    normed_all = gather_z(layer_norm(middle, *vectors[1][0:2]).astype(LOW))
    hidden, kept_heads_last = forward_attention(
        middle, normed_all, spots, vectors[1], bias_heads_last, *heads_last
    )
    units_last = join_units(1, units_last)
    result, kept_units_last = forward_hidden_units(hidden, vectors[1], bias_up_last, *units_last)

    def choose_grads(layer, first, second):
        return owner(layer, first, second), owner(layer, second, first)

    def swap_grads(layer, first, second):
        kept, payload = choose_grads(layer, first, second)
        return kept, swap(payload)

    def add_grads(kept, arrived):
        return (kept.astype(FULL) + arrived.astype(FULL)).astype(LOW)

    def scatter_whole(grads):
        return lax.psum_scatter(
            grads, "tensor", scatter_dimension=0, tiled=True, axis_index_groups=X_GROUPS
        )

    def split_heads(g_w_heads, g_w_out):
        heads = g_w_heads.reshape(SIDE, TILE, model_width)
        return heads[:, 0:128], heads[:, 128:256] + g_w_out.reshape(SIDE, 128, model_width)

    turn = jnp.stack(downward)[None, :] == jnp.arange(SIDE)[:, None]

    def pack_vectors(heads, units, g_b_out, g_b_up, g_b_qkv):
        by_turn = jnp.sum(
            jnp.where(turn[:, :, None], g_b_up.reshape(SIDE, 1, TILE), 0.0), axis=0
        )
        return jnp.concatenate(
            [
                *heads, g_b_out, *units,
                jnp.concatenate([by_turn, g_b_qkv.reshape(SIDE, TILE)], axis=1).reshape(2, -1),
            ],
            axis=0,
        )

    grad_hidden, vec_units_last, g_b_up_last, g_up, g_down = backward_hidden_units(
        grad_last, grad_last_all, kept_units_last, vectors[1], *units_last
    )
    units_sum_last = add_grads(*swap_grads(1, g_up, g_down))
    grad_mixed, g_b_out_last, g_out, units_sum_last = backward_mixed(
        grad_hidden, kept_heads_last, heads_last[1], spots, units_sum_last
    )
    units_sum_last = scatter_whole(units_sum_last)
    grad_qkv = backward_heads(attend_back(spots, *kept_heads_last[2:5], grad_mixed))
    grad_qkv, units_sum_last = tie(grad_qkv, units_sum_last)
    units_sum_last = lax.psum(units_sum_last, "ctx")
    grad_middle, vec_heads_last, g_b_qkv_last, g_heads = backward_entry(
        grad_qkv, grad_hidden, kept_heads_last, vectors[1], heads_last[0]
    )
    heads_kept, heads_arrived = swap_grads(1, *split_heads(g_heads, g_out))

    grad_middle = grad_middle.astype(LOW).astype(FULL)
    heads_sum_last = jnp.concatenate(reorder(add_grads(heads_kept, heads_arrived)), axis=0)
    grad_down_all, heads_sum_last = tie(gather_z(grad_middle.astype(LOW)), heads_sum_last)
    heads_sum_last = scatter_whole(heads_sum_last)
    grad_hidden, vec_units_first, g_b_up_first, g_up, g_down = backward_hidden_units(
        grad_middle, grad_down_all, kept_units_first, vectors[0], *units_first
    )
    units_sum_first = add_grads(*swap_grads(0, g_up, g_down))
    grad_mixed, g_b_out_first, g_out, (units_sum_first, units_sum_last) = backward_mixed(
        grad_hidden, kept_heads_first, heads_first[1], spots, (units_sum_first, units_sum_last)
    )
    units_sum_first = scatter_whole(units_sum_first)
    grad_qkv, units_sum_first, heads_sum_last = backward_heads(
        attend_back(spots, *kept_heads_first[2:5], grad_mixed), units_sum_first, heads_sum_last
    )
    units_sum_first, heads_sum_last = lax.psum((units_sum_first, heads_sum_last), "ctx")

    gain_one, bias_one = vectors[0][0:2]
    residual, normed_all = kept_heads_first[0:2]
    heads_kept, payload = choose_grads(0, *split_heads(tn_dot(grad_qkv, normed_all).astype(LOW), g_out))
    grad_qkv, payload = tie(grad_qkv, payload)
    halves = add_grads(heads_kept, swap(payload))
    grad_normed = local_dot(grad_qkv, heads_first[0])
    g_bias_one = column_sum(grad_normed)
    g_gain_one = column_sum(grad_normed * ((normed_all.astype(FULL) - bias_one) / gain_one))
    g_b_qkv_first = jnp.sum(grad_qkv.astype(FULL), axis=0)
    sums_first = pack_vectors(
        (g_gain_one, g_bias_one), vec_units_first, g_b_out_first, g_b_up_first, g_b_qkv_first
    )
    sums_last = pack_vectors(vec_heads_last, vec_units_last, g_b_out_last, g_b_up_last, g_b_qkv_last)
    common = jnp.pad(jnp.concatenate([sums_first[:6], sums_last[:6]]), ((0, 4), (0, 0))).astype(LOW)
    chunks = grad_normed.astype(LOW).reshape(SIDE, row_count, model_width)
    chunks = even_pairs([jnp.concatenate([chunks[d], common], axis=0) for d in range(SIDE)], move_z)
    sums_first = jnp.concatenate([chunks[row_count : row_count + 6], sums_first[6:]])
    sums_last = jnp.concatenate([chunks[row_count + 6 : row_count + 12], sums_last[6:]])
    sums = owner(0, sums_first, sums_last) + swap(owner(0, sums_last, sums_first))
    common = sums[:6].astype(LOW)
    split = sums[6:].reshape(SIDE, 1, 512).astype(LOW)
    packs = [
        jnp.concatenate(
            [
                common,
                jnp.pad(split[d], ((0, 0), (0, model_width - 512))),
                jnp.zeros((9, model_width), LOW),
            ],
            axis=0,
        )
        for d in range(SIDE)
    ]
    pack = jnp.concatenate([even_pairs(halves, move_x), even_pairs(packs, move_x)], axis=0)
    pack = even_sum(pack.astype(LOW), move_y)
    pack, units_sum_first, units_sum_last, heads_sum_last = tie(
        pack, units_sum_first, units_sum_last, heads_sum_last
    )
    heads_sum_first, pack = pack[:128], pack[128:]
    grad_first = grad_hidden + layer_norm_back(chunks[:row_count], residual, gain_one)[0]

    passed = swap(owner(0, result, grad_first))
    kept = owner(0, grad_first, result)
    boundary = owner(0, jnp.stack([kept, passed]), jnp.stack([passed, kept]))
    boundary = boundary.reshape(1, 2, 1, row_count, model_width)

    units_sum = owner(0, units_sum_first, units_sum_last)
    heads_sum = owner(0, heads_sum_first, heads_sum_last)
    units_theirs = swap(owner(0, units_sum_last, units_sum_first))
    heads_theirs = swap(owner(0, heads_sum_last, heads_sum_first).astype(LOW))
    g_key_value = heads_sum.astype(FULL)
    g_query_out = heads_theirs.astype(FULL)
    g_w_qkv = jnp.stack([g_query_out[0:64].T, g_key_value[0:64].T, g_key_value[64:128].T], axis=1)
    g_b_qv = jnp.stack([pack[6, 384:448], pack[6, 320:384]])
    return (
        boundary,
        pack[0:1],
        pack[1:2],
        g_w_qkv[None],
        g_b_qv[None],
        g_query_out[64:128][None],
        pack[2:3],
        pack[3:4],
        pack[4:5],
        units_sum.astype(FULL).T[None],
        pack[6:7, 0:256],
        units_theirs.astype(FULL)[None],
        pack[5:6],
    )


def solution(mesh):
    return jax.shard_map(
        per_device,
        mesh=mesh,
        in_specs=(
            P(None, "ctx", "tensor", None),
            P(),
            P("section", None),
            P("section", None),
            P("section", None, None, "tensor"),
            P("section", None, "tensor"),
            P("section", "tensor", None),
            P("section", None),
            P("section", None),
            P("section", None),
            P("section", None, "tensor"),
            P("section", "tensor"),
            P("section", "tensor", None),
            P("section", None),
            P(None, "ctx", "tensor", None),
        ),
        out_specs=(
            P("section", None, "ctx", "tensor", None),
            P("section", None),
            P("section", None),
            P("section", None, None, "tensor"),
            P("section", None, "tensor"),
            P("section", "tensor", None),
            P("section", None),
            P("section", None),
            P("section", None),
            P("section", None, "tensor"),
            P("section", "tensor"),
            P("section", "tensor", None),
            P("section", None),
        ),
        check_vma=False,
    )
```

```python
import functools
import math

import jax
import jax.numpy as jnp
from jax import lax
from jax.experimental import pallas as pl
from jax.experimental.pallas import tpu as pltpu
from jax.sharding import PartitionSpec as P

HEAD_DIM = 64
EPSILON = 1e-05
MASK_FILL = -1e30
BASE_TWO_SCALE = 0.125 * math.log2(math.e)
SIDE = 4
TILE = 256
LN_TWO = math.log(2.0)
LOW = jnp.bfloat16
FULL = jnp.float32


def move_z(block, distance):
    route = [
        (x * SIDE + z, x * SIDE + (z + distance) % SIDE) for x in range(SIDE) for z in range(SIDE)
    ]
    return lax.ppermute(block, "tensor", route)


def move_x(block, distance):
    route = [
        (x * SIDE + z, (x + distance) % SIDE * SIDE + z) for x in range(SIDE) for z in range(SIDE)
    ]
    return lax.ppermute(block, "tensor", route)


def move_y(block, distance):
    return lax.ppermute(block, "ctx", [(y, (y + distance) % SIDE) for y in range(SIDE)])


def move_y_open(block, distance):
    route = [(y, y + distance) for y in range(SIDE) if 0 <= y + distance < SIDE]
    return lax.ppermute(block, "ctx", route)


def move_x_in(block, distance, section):
    base = section * SIDE * SIDE
    route = [
        (base + x * SIDE + z, base + (x + distance) % SIDE * SIDE + z)
        for x in range(SIDE)
        for z in range(SIDE)
    ]
    return lax.ppermute(block, ("section", "tensor"), route)


def move_y_in(block, distance, section):
    base = section * SIDE
    route = [(base + y, base + (y + distance) % SIDE) for y in range(SIDE)]
    return lax.ppermute(block, ("section", "ctx"), route)


def swap(block):
    return lax.ppermute(block, "section", [(0, 1), (1, 0)])


def send_to(block, section):
    return lax.ppermute(block, "section", [(1 - section, section)])


def gather_z(rows):
    return jnp.concatenate([rows] + [move_z(rows, d) for d in range(1, SIDE)], axis=0)


def scatter_z(rows):
    chunks = rows.reshape(SIDE, rows.shape[0] // SIDE, rows.shape[1])
    total = chunks[0].astype(FULL)
    for d in range(1, SIDE):
        total = total + move_z(chunks[d], -d).astype(FULL)
    return total


def even_sum(block, move):
    low = block.astype(FULL)
    return (low + move(block, 2).astype(FULL)) + (
        move(block, 1).astype(FULL) + move(block, 3).astype(FULL)
    )


def even_pairs(blocks, move):
    return (blocks[0].astype(FULL) + move(blocks[2], -2).astype(FULL)) + (
        move(blocks[1], -1).astype(FULL) + move(blocks[3], -3).astype(FULL)
    )


def layer_norm(values, gain, bias):
    center = values - jnp.mean(values, axis=-1, keepdims=True)
    spread = jnp.mean(center * center, axis=-1, keepdims=True)
    return center * lax.rsqrt(spread + EPSILON) * gain + bias


def column_sum(rows):
    return jnp.sum(rows.astype(FULL), axis=0)


def layer_norm_back(grad, values, gain):
    center = values - jnp.mean(values, axis=-1, keepdims=True)
    scale = lax.rsqrt(jnp.mean(center * center, axis=-1, keepdims=True) + EPSILON)
    unit = center * scale
    part = grad * gain
    back = scale * (
        part
        - jnp.mean(part, axis=-1, keepdims=True)
        - unit * jnp.mean(part * unit, axis=-1, keepdims=True)
    )
    return back, column_sum(grad * unit), column_sum(grad)


def local_dot(left, right):
    return jnp.dot(left, right, preferred_element_type=FULL)


def back_dot(left, right):
    return jnp.einsum("rf,df->rd", left, right, preferred_element_type=FULL)


def outer_sum(left, right):
    return jnp.einsum("rd,rf->df", left, right, preferred_element_type=FULL)


def nt_dot(left, right):
    return lax.dot_general(left, right, (((1,), (1,)), ((), ())), preferred_element_type=FULL)


def tn_dot(left, right):
    return lax.dot_general(left, right, (((0,), (0,)), ((), ())), preferred_element_type=FULL)


def place_in_block(order, x_here, z_here):
    from_x = (x_here + (order >> 8)) & 3
    from_z = (z_here - ((order >> 6) & 3)) & 3
    return (from_x << 8) + (from_z << 6) + (order & 63)


def first_of_document(place, start_one, start_two):
    return jnp.where(place >= start_two, start_two, jnp.where(place >= start_one, start_one, 0))


def tile_bounds(scalar_ref, indices, rows_all):
    block, x_here, _, start_one, start_two = [scalar_ref[i] for i in range(5)]
    least, most = [], []
    for index in indices:
        place = block * rows_all + ((x_here + index) & 3) * TILE
        least.append(first_of_document(place, start_one, start_two))
        most.append(first_of_document(place + TILE - 1, start_one, start_two))
    return functools.reduce(jnp.minimum, least), functools.reduce(jnp.maximum, most)


def tile_limits(scalar_ref, index, rows_all):
    block, x_here, z_here, start_one, start_two = [scalar_ref[i] for i in range(5)]
    order = lax.broadcasted_iota(jnp.int32, (1, TILE), 1) + index * TILE
    high = block * rows_all + place_in_block(order, x_here, z_here)
    return first_of_document(high, start_one, start_two), high


def attend_kernel(
    scalar_ref, own_ref, kv1_ref, kv2_ref, kv3_ref, out_ref, peak, mixed, held, keys, arrived
):
    block = scalar_ref[0]
    rows_all = own_ref.shape[0]
    tiles = rows_all // TILE
    copies = [
        pltpu.make_async_copy(ref, held.at[d], arrived.at[d])
        for d, ref in enumerate((kv1_ref, kv2_ref, kv3_ref))
    ]
    for copy in copies:
        copy.start()
    peak[...] = jnp.full_like(peak, MASK_FILL)
    mixed[...] = jnp.zeros_like(mixed)
    keys[...] = place_in_block(
        lax.broadcasted_iota(jnp.int32, keys.shape, 0), scalar_ref[1], scalar_ref[2]
    )
    for d in range(SIDE):
        if d > 0:
            copies[d - 1].wait()
        start = (block - d) * rows_all

        @pl.loop(0, tiles // 2)
        def _(pair, d=d, start=start):
            indices = [pair * 2, pair * 2 + 1]
            least, most = tile_bounds(scalar_ref, indices, rows_all)

            def step(masked):
                key_values = own_ref[:, 0:128] if d == 0 else held[d - 1]
                lanes = lax.broadcasted_iota(jnp.int32, key_values.shape, 1)
                ones_values = jnp.where(lanes < HEAD_DIM, jnp.ones_like(key_values), key_values)
                raws = []
                for index in indices:
                    rows = pl.ds(pl.multiple_of(index * TILE, TILE), TILE)
                    raws.append(nt_dot(key_values, own_ref[rows, 128:256]))
                for index, raw in zip(indices, raws):
                    if masked:
                        low, high = tile_limits(scalar_ref, index, rows_all)
                        allowed = keys[...] >= low - start
                        if d == 0:
                            allowed = allowed & (keys[...] <= high - start)
                        raw = jnp.where(allowed, raw, MASK_FILL)
                    old = peak[index]
                    top = jnp.maximum(old, jnp.max(raw, axis=0, keepdims=True))
                    weight = jnp.exp2(raw - top).astype(LOW)
                    peak[index] = top
                    mixed[index] = mixed[index] * jnp.exp2(old - top) + tn_dot(ones_values, weight)

            if d == 0:
                step(True)
            else:
                reached = (block >= d) & (least < start + rows_all)
                pl.when(reached & (most <= start))(lambda: step(False))
                pl.when(reached & (most > start))(lambda: step(True))

    @pl.loop(0, tiles)
    def _(index):
        rows = pl.ds(pl.multiple_of(index * TILE, TILE), TILE)
        sums = mixed[index]
        count = sums[0:1, :]
        level = peak[index] + jnp.log2(count)
        lines = lax.broadcasted_iota(jnp.int32, sums.shape, 0)
        out_ref[rows, :] = jnp.where(lines < HEAD_DIM, level, sums / count).T


def attend_back_kernel(
    scalar_ref, own_ref, kv1_ref, kv2_ref, kv3_ref, kept_ref, grad_ref,
    dq_ref, d0_ref, d1_ref, d2_ref, d3_ref,
    query_sum, key_sum, held, keys, stats, arrived,
):
    block = scalar_ref[0]
    rows_all = own_ref.shape[0]
    tiles = rows_all // TILE
    copies = [
        pltpu.make_async_copy(ref, held.at[d], arrived.at[d])
        for d, ref in enumerate((kv1_ref, kv2_ref, kv3_ref))
    ]
    for copy in copies:
        copy.start()
    query_sum[...] = jnp.zeros_like(query_sum)
    keys[...] = place_in_block(
        lax.broadcasted_iota(jnp.int32, keys.shape, 0), scalar_ref[1], scalar_ref[2]
    )

    @pl.loop(0, tiles)
    def _(index):
        rows = pl.ds(pl.multiple_of(index * TILE, TILE), TILE)
        kept = kept_ref[rows, :]
        stats[index, 0:1, :] = kept.T[0:1, :]
        stats[index, 1:2, :] = jnp.sum((kept * grad_ref[rows, :].astype(FULL)).T, axis=0, keepdims=True)

    for d, out_ref in enumerate((d0_ref, d1_ref, d2_ref, d3_ref)):
        if d > 0:
            copies[d - 1].wait()

        @pl.when(block >= d)
        def _(d=d, out_ref=out_ref):
            start = (block - d) * rows_all
            key_sum[...] = jnp.zeros_like(key_sum)

            @pl.loop(0, tiles)
            def _(index):
                indices = [index]
                least, most = tile_bounds(scalar_ref, indices, rows_all)

                def step(masked):
                    key_values = own_ref[:, 0:128] if d == 0 else held[d - 1]
                    spans = [pl.ds(pl.multiple_of(index * TILE, TILE), TILE) for index in indices]
                    raws = [nt_dot(key_values, own_ref[rows, 128:256]) for rows in spans]
                    meets = [nt_dot(key_values, grad_ref[rows, :]) for rows in spans]
                    for index, rows, raw, meet in zip(indices, spans, raws, meets):
                        probs = jnp.exp2(raw - stats[index, 0:1, :])
                        if masked:
                            low, high = tile_limits(scalar_ref, index, rows_all)
                            allowed = keys[...] >= low - start
                            if d == 0:
                                allowed = allowed & (keys[...] <= high - start)
                            probs = jnp.where(allowed, probs, 0.0)
                        grad_scores = (probs * (meet - stats[index, 1:2, :])).astype(LOW)
                        key_sum[...] += local_dot(grad_scores, own_ref[rows, 128:256]) * LN_TWO + local_dot(
                            probs.astype(LOW), grad_ref[rows, :]
                        )
                        query_sum[rows, :] += tn_dot(grad_scores, key_values)

                if d == 0:
                    step(True)
                else:
                    pl.when(most <= start)(lambda: step(False))
                    pl.when((most > start) & (least < start + rows_all))(lambda: step(True))

            out_ref[...] = key_sum[...].astype(LOW)

        if d > 0:

            @pl.when(block < d)
            def _(out_ref=out_ref):
                out_ref[...] = jnp.zeros_like(out_ref)

    lanes = lax.broadcasted_iota(jnp.int32, dq_ref.shape, 1)
    dq_ref[...] = jnp.where(lanes < HEAD_DIM, query_sum[...] * 0.125, 0.0).astype(LOW)


VMEM_SPEC = pl.BlockSpec(memory_space=pltpu.VMEM)
SMEM_SPEC = pl.BlockSpec(memory_space=pltpu.SMEM)
FAR_SPEC = pl.BlockSpec(memory_space=pltpu.HBM)


def attend(spots, own, others):
    rows = own.shape[0]
    return pl.pallas_call(
        attend_kernel,
        out_shape=jax.ShapeDtypeStruct((rows, 128), FULL),
        in_specs=[SMEM_SPEC, VMEM_SPEC] + [FAR_SPEC] * 3,
        out_specs=VMEM_SPEC,
        scratch_shapes=[
            pltpu.VMEM((rows // TILE, 1, TILE), FULL),
            pltpu.VMEM((rows // TILE, 128, TILE), FULL),
            pltpu.VMEM((3, rows, 128), LOW),
            pltpu.VMEM((rows, 1), jnp.int32),
            pltpu.SemaphoreType.DMA((3,)),
        ],
        compiler_params=pltpu.CompilerParams(vmem_limit_bytes=40 << 20),
        cost_estimate=pl.CostEstimate(
            flops=4 * rows * 2 * rows * 128, bytes_accessed=4 << 20, transcendentals=rows * 2 * rows
        ),
        name="attend",
    )(spots["scalars"], own, *others)


def attend_back(spots, own, others, kept, grad):
    rows = own.shape[0]
    return pl.pallas_call(
        attend_back_kernel,
        out_shape=[jax.ShapeDtypeStruct((rows, 128), LOW)] * 5,
        in_specs=[SMEM_SPEC, VMEM_SPEC] + [FAR_SPEC] * 3 + [VMEM_SPEC] * 2,
        out_specs=[VMEM_SPEC] * 5,
        scratch_shapes=[
            pltpu.VMEM((rows, 128), FULL),
            pltpu.VMEM((rows, 128), FULL),
            pltpu.VMEM((3, rows, 128), LOW),
            pltpu.VMEM((rows, 1), jnp.int32),
            pltpu.VMEM((rows // TILE, 8, TILE), FULL),
            pltpu.SemaphoreType.DMA((3,)),
        ],
        compiler_params=pltpu.CompilerParams(vmem_limit_bytes=40 << 20),
        cost_estimate=pl.CostEstimate(
            flops=10 * rows * 2 * rows * 128, bytes_accessed=6 << 20, transcendentals=rows * 2 * rows
        ),
        name="attend_back",
    )(spots["scalars"], own, *others, kept, grad)


def tie(first, *rest):
    return lax.optimization_barrier((first, *rest))


X_GROUPS = [[x * SIDE + z for x in range(SIDE)] for z in range(SIDE)]


def forward_attention(residual, normed_all, spots, vectors, bias_qkv, w_heads, w_back):
    b_out = vectors[2]
    projected = ((nt_dot(normed_all, w_heads) + bias_qkv) * spots["scale"]).astype(LOW)
    width = projected.shape[1] // SIDE
    pieces = [projected[:, d * width : (d + 1) * width] for d in range(SIDE)]
    own = jnp.concatenate([pieces[0]] + [move_x(pieces[d], -d) for d in range(1, SIDE)], axis=0)
    others = [move_y_open(own[:, 0:128], d) for d in range(1, SIDE)]
    kept = attend(spots, own, others)
    lanes = lax.broadcasted_iota(jnp.int32, kept.shape, 1)
    mixed = jnp.where(lanes < HEAD_DIM, 0.0, kept).astype(LOW)
    rows = mixed.shape[0] // SIDE
    mixed_rows = jnp.concatenate(
        [mixed[0:rows]] + [move_x(mixed[d * rows : (d + 1) * rows], d) for d in range(1, SIDE)], axis=1
    )
    hidden = residual + (scatter_z(local_dot(mixed_rows, w_back).astype(LOW)) + b_out)
    return hidden, (residual, normed_all, own, others, kept, mixed_rows)


def forward_hidden_units(hidden, vectors, b_up, w_up, w_down):
    gain_two, bias_two, b_down = vectors[3:6]
    normed_two_all = gather_z(layer_norm(hidden, gain_two, bias_two).astype(LOW))
    up_value = nt_dot(normed_two_all, w_up) + b_up
    activated = jax.nn.gelu(up_value).astype(LOW)
    result = hidden + (scatter_z(local_dot(activated, w_down).astype(LOW)) + b_down)
    return result, (hidden, normed_two_all, up_value, activated)


def backward_hidden_units(grad_out, grad_down_all, stored, vectors, w_up, w_down):
    hidden, normed_two_all, up_value, activated = stored
    gain_two = vectors[3]
    grad_down = grad_out.astype(LOW)
    g_b_down = column_sum(grad_down)
    _, gelu_pull = jax.vjp(jax.nn.gelu, up_value)
    (grad_up,) = gelu_pull(nt_dot(grad_down_all, w_down))
    grad_up = grad_up.astype(LOW)
    grad_normed_two = scatter_z(local_dot(grad_up, w_up).astype(LOW))
    g_w_down = tn_dot(activated, grad_down_all).astype(LOW)
    g_b_up = jnp.sum(grad_up.astype(FULL), axis=0)
    g_w_up = tn_dot(grad_up, normed_two_all).astype(LOW)
    grad_hidden_part, g_gain_two, g_bias_two = layer_norm_back(grad_normed_two, hidden, gain_two)
    grad_hidden = grad_out + grad_hidden_part
    return grad_hidden, (g_gain_two, g_bias_two, g_b_down), g_b_up, g_w_up, g_w_down


def backward_mixed(grad_hidden, stored, w_back, spots, side):
    mixed_rows = stored[5]
    grad_attn = grad_hidden.astype(LOW)
    g_b_out = column_sum(grad_attn)
    grad_attn_all, side = tie(gather_z(grad_attn), side)
    grad_mixed = (nt_dot(grad_attn_all, w_back) * spots["upper"]).astype(LOW)
    pieces = [grad_mixed[:, d * 128 : (d + 1) * 128] for d in range(SIDE)]
    grad_own = jnp.concatenate(
        [pieces[0]] + [move_x(pieces[d], -d) for d in range(1, SIDE)], axis=0
    )
    g_w_out = tn_dot(mixed_rows, grad_attn_all).astype(LOW)
    return grad_own, g_b_out, g_w_out, side


def backward_heads(parts, *side):
    dq, dkv0, dkv1, dkv2, dkv3 = parts
    dkv = dkv0.astype(FULL)
    for d, part in enumerate((dkv1, dkv2, dkv3), 1):
        dkv = dkv + move_y_open(part, -d).astype(FULL)
    grad_own = jnp.concatenate([dkv.astype(LOW), dq], axis=1)
    if side:
        grad_own, *side = tie(grad_own, *side)
    rows = grad_own.shape[0] // SIDE
    grad_qkv = jnp.concatenate(
        [grad_own[0:rows]] + [move_x(grad_own[d * rows : (d + 1) * rows], d) for d in range(1, SIDE)],
        axis=1,
    )
    return (grad_qkv, *side) if side else grad_qkv


def backward_entry(grad_qkv, grad_hidden, stored, vectors, w_heads):
    residual, normed_all = stored[0:2]
    gain_one = vectors[0]
    grad_normed = scatter_z(local_dot(grad_qkv, w_heads).astype(LOW))
    g_w_heads = tn_dot(grad_qkv, normed_all).astype(LOW)
    g_b_qkv = jnp.sum(grad_qkv.astype(FULL), axis=0)
    grad_residual_part, g_gain_one, g_bias_one = layer_norm_back(grad_normed, residual, gain_one)
    return grad_hidden + grad_residual_part, (g_gain_one, g_bias_one), g_b_qkv, g_w_heads


def per_device(
    inputs,
    segments,
    gain_one,
    bias_one,
    w_qkv,
    b_qv,
    w_out,
    b_out,
    gain_two,
    bias_two,
    w_up,
    b_up,
    w_down,
    b_down,
    cotangent,
):
    here = lax.axis_index("section")
    block = lax.axis_index("ctx")
    spot = lax.axis_index("tensor")
    x_here, z_here = spot // SIDE, spot % SIDE
    row_count, model_width = inputs.shape[2], inputs.shape[3]

    def owner(layer, yes, no):
        return jnp.where(here == layer, yes, no)

    sequence = lax.dynamic_index_in_dim(inputs, here, 0, False)[0].astype(FULL)
    grad_last = lax.dynamic_index_in_dim(cotangent, here, 0, False)[0].astype(FULL)
    grad_last_all = lax.dynamic_index_in_dim(cotangent, here, 0, False)[0]

    gap = jnp.zeros((HEAD_DIM,), LOW)
    biases = jnp.concatenate(
        [b_up[0], gap, b_qv[0, 1], b_qv[0, 0], gap, jnp.zeros((model_width - 512,), LOW)]
    )[None]
    heads_kv = jnp.concatenate(
        [w_qkv[0, :, 1].T, w_qkv[0, :, 2].T, biases, jnp.zeros((15, model_width), LOW)], axis=0
    )
    heads_qo = jnp.concatenate(
        [w_qkv[0, :, 0].T, w_out[0], jnp.zeros((16, model_width), LOW)], axis=0
    )
    heads_qo_other = swap(heads_qo)
    small = jnp.concatenate(
        [gain_one, bias_one, b_out, gain_two, bias_two, b_down, jnp.zeros((2, model_width), LOW)],
        axis=0,
    )
    small_other = swap(small)
    half_rows = w_down.shape[1] // 2
    units_own = jnp.concatenate(
        [w_up[0].T.reshape(2, half_rows, model_width), w_down[0].reshape(2, half_rows, model_width)], axis=1
    )
    units_other = swap(lax.dynamic_index_in_dim(units_own, 1 - here, 0, False))
    units_own = lax.dynamic_index_in_dim(units_own, here, 0, False)
    downward = [(x_here - d) % SIDE for d in range(SIDE)]

    def reorder(pieces):
        return [lax.dynamic_index_in_dim(pieces, place, 0, False) for place in downward]

    def half_heads(layer):
        return owner(layer, heads_kv, heads_qo_other)

    def join_heads(layer, mine, theirs):
        key_value, query_out = owner(layer, mine, theirs), owner(layer, theirs, mine)
        whole = jnp.concatenate([key_value[:, :128], query_out[:, :128]], axis=1)
        back = query_out[:, :128].reshape(SIDE * 128, model_width)
        rows = key_value[:, 128, :512].astype(FULL)
        bias_heads = rows[:, 256:].reshape(1, SIDE * TILE)
        bias_up = jnp.stack(reorder(rows[:, :256])).reshape(SIDE, 2, half_rows)
        bias_up = jnp.stack([bias_up[:, 0], bias_up[:, 1]])
        bias_up = owner(0, bias_up, bias_up[::-1]).reshape(1, SIDE * TILE)
        return (whole.reshape(SIDE * TILE, model_width), back), bias_heads, bias_up

    def gather_whole(half):
        return lax.all_gather(half, "tensor", axis=0, tiled=True, axis_index_groups=X_GROUPS)

    def join_units(mine):
        mine, theirs = [
            part.reshape(SIDE, 2 * half_rows, model_width) for part in (mine, swap(mine))
        ]
        return tuple(
            jnp.concatenate([mine[:, span], theirs[:, span]]).reshape(-1, model_width)
            for span in (slice(0, half_rows), slice(half_rows, 2 * half_rows))
        )

    smalls = (owner(0, small, small_other), owner(0, small_other, small))
    vectors = [
        tuple(smalls[layer][row : row + 1].astype(FULL) for row in range(6)) for layer in range(2)
    ]
    normed = layer_norm(sequence, *vectors[0][0:2]).astype(LOW)
    half, normed = tie(half_heads(0), normed)
    mine = jnp.stack([half] + [move_x(half, d) for d in range(1, SIDE)])
    half = owner(0, units_own, units_other)
    normed_all, mine, half, grad_last_all = tie(gather_z(normed), mine, half, gather_z(grad_last_all))
    heads_first, bias_heads_first, bias_up_first = join_heads(0, mine, swap(mine))
    units_first = gather_whole(half)
    heads_last = gather_whole(half_heads(1)).reshape(SIDE, -1, model_width)
    units_last = gather_whole(owner(1, units_own, units_other))
    normed_all, segments = tie(normed_all, segments)
    segment_ids = lax.dynamic_index_in_dim(segments, here, 0, False)
    start_one = jnp.sum((segment_ids < 1).astype(jnp.int32))
    start_two = jnp.sum((segment_ids < 2).astype(jnp.int32))

    lane = jnp.arange(SIDE * TILE) % TILE
    spots = {
        "scalars": jnp.stack([block, x_here, z_here, start_one, start_two]).astype(jnp.int32),
        "scale": jnp.where(lane < 128, 1.0, jnp.where(lane < 192, BASE_TWO_SCALE, 0.0)).astype(FULL),
        "upper": (jnp.arange(SIDE * 128) % 128 >= HEAD_DIM).astype(FULL),
    }

    hidden, kept_heads_first = forward_attention(
        sequence, normed_all, spots, vectors[0], bias_heads_first, *heads_first
    )
    units_first = join_units(units_first)
    middle, kept_units_first = forward_hidden_units(hidden, vectors[0], bias_up_first, *units_first)
    mine = jnp.stack(reorder(heads_last))
    middle, mine, theirs = tie(middle, mine, swap(mine))
    heads_last, bias_heads_last, bias_up_last = join_heads(1, mine, theirs)
    middle = middle.astype(LOW).astype(FULL)
    normed_all = gather_z(layer_norm(middle, *vectors[1][0:2]).astype(LOW))
    hidden, kept_heads_last = forward_attention(
        middle, normed_all, spots, vectors[1], bias_heads_last, *heads_last
    )
    units_last = join_units(units_last)
    result, kept_units_last = forward_hidden_units(hidden, vectors[1], bias_up_last, *units_last)

    def choose_grads(layer, first, second):
        return owner(layer, first, second), owner(layer, second, first)

    def swap_grads(layer, first, second):
        kept, payload = choose_grads(layer, first, second)
        return kept, swap(payload)

    def add_grads(kept, arrived):
        return (kept.astype(FULL) + arrived.astype(FULL)).astype(LOW)

    def add_units(g_up, g_down):
        parts = [g.reshape(2, SIDE, half_rows, model_width) for g in (g_up, g_down)]
        kept, payload = [
            jnp.concatenate([part[side] for part in parts], axis=1).reshape(-1, model_width)
            for side in range(2)
        ]
        return add_grads(kept, swap(payload))

    def scatter_whole(grads):
        return lax.psum_scatter(
            grads, "tensor", scatter_dimension=0, tiled=True, axis_index_groups=X_GROUPS
        )

    def split_heads(g_w_heads, g_w_out):
        heads = g_w_heads.reshape(SIDE, TILE, model_width)
        return heads[:, 0:128], heads[:, 128:256] + g_w_out.reshape(SIDE, 128, model_width)

    turn = jnp.stack(downward)[None, :] == jnp.arange(SIDE)[:, None]

    def pack_vectors(heads, units, g_b_out, g_b_up, g_b_qkv):
        halves = g_b_up.reshape(2, SIDE, half_rows)
        halves = owner(0, halves, halves[::-1])
        by_place = jnp.concatenate([halves[0], halves[1]], axis=1)
        by_turn = jnp.sum(jnp.where(turn[:, :, None], by_place[:, None], 0.0), axis=0)
        return jnp.concatenate(
            [
                jnp.stack([*heads, g_b_out, *units]),
                jnp.concatenate([by_turn, g_b_qkv.reshape(SIDE, TILE)], axis=1).reshape(2, -1),
            ],
            axis=0,
        )

    grad_hidden, vec_units_last, g_b_up_last, g_up, g_down = backward_hidden_units(
        grad_last, grad_last_all, kept_units_last, vectors[1], *units_last
    )
    units_sum_last = add_units(g_up, g_down)
    grad_mixed, g_b_out_last, g_out, units_sum_last = backward_mixed(
        grad_hidden, kept_heads_last, heads_last[1], spots, units_sum_last
    )
    units_sum_last = scatter_whole(units_sum_last)
    grad_qkv, units_sum_last = backward_heads(
        attend_back(spots, *kept_heads_last[2:5], grad_mixed), units_sum_last
    )
    units_sum_last = lax.psum(units_sum_last, "ctx")
    grad_middle, vec_heads_last, g_b_qkv_last, g_heads = backward_entry(
        grad_qkv, grad_hidden, kept_heads_last, vectors[1], heads_last[0]
    )
    heads_kept, heads_arrived = swap_grads(1, *split_heads(g_heads, g_out))

    grad_middle = grad_middle.astype(LOW).astype(FULL)
    heads_sum_last = jnp.concatenate(reorder(add_grads(heads_kept, heads_arrived)), axis=0)
    grad_down_all, heads_sum_last = tie(gather_z(grad_middle.astype(LOW)), heads_sum_last)
    heads_sum_last = scatter_whole(heads_sum_last)
    grad_hidden, vec_units_first, g_b_up_first, g_up, g_down = backward_hidden_units(
        grad_middle, grad_down_all, kept_units_first, vectors[0], *units_first
    )
    units_sum_first = add_units(g_up, g_down)
    grad_mixed, g_b_out_first, g_out, (units_sum_first, units_sum_last) = backward_mixed(
        grad_hidden, kept_heads_first, heads_first[1], spots, (units_sum_first, units_sum_last)
    )
    units_sum_first = scatter_whole(units_sum_first)
    grad_qkv, units_sum_first, heads_sum_last = backward_heads(
        attend_back(spots, *kept_heads_first[2:5], grad_mixed), units_sum_first, heads_sum_last
    )
    units_sum_first, heads_sum_last = lax.psum((units_sum_first, heads_sum_last), "ctx")

    gain_one, bias_one = vectors[0][0:2]
    residual, normed_all = kept_heads_first[0:2]
    grad_normed = local_dot(grad_qkv, heads_first[0])
    g_bias_one = column_sum(grad_normed)
    g_gain_one = column_sum(grad_normed * ((normed_all.astype(FULL) - bias_one) / gain_one))
    g_b_qkv_first = jnp.sum(grad_qkv.astype(FULL), axis=0)
    sums_first = pack_vectors(
        (g_gain_one, g_bias_one), vec_units_first, g_b_out_first, g_b_up_first, g_b_qkv_first
    )
    sums_last = pack_vectors(vec_heads_last, vec_units_last, g_b_out_last, g_b_up_last, g_b_qkv_last)
    common = jnp.pad(jnp.concatenate([sums_first[:6], sums_last[:6]]), ((0, 4), (0, 0))).astype(LOW)
    chunks = grad_normed.astype(LOW).reshape(SIDE, row_count, model_width)
    chunks = even_pairs([jnp.concatenate([chunks[d], common], axis=0) for d in range(SIDE)], move_z)
    sums_first = jnp.concatenate([chunks[row_count : row_count + 6], sums_first[6:]])
    sums_last = jnp.concatenate([chunks[row_count + 6 : row_count + 12], sums_last[6:]])
    sums = owner(0, sums_first, sums_last) + swap(owner(0, sums_last, sums_first))
    halves = add_grads(*swap_grads(0, *split_heads(tn_dot(grad_qkv, normed_all).astype(LOW), g_out)))
    common = sums[:6].astype(LOW)
    split = sums[6:].reshape(SIDE, 1, 512).astype(LOW)
    packs = [
        jnp.concatenate(
            [
                halves[d],
                common,
                jnp.pad(split[d], ((0, 0), (0, model_width - 512))),
                jnp.zeros((9, model_width), LOW),
            ],
            axis=0,
        )
        for d in range(SIDE)
    ]
    pack, units_sum_first, units_sum_last, heads_sum_last = tie(
        even_pairs(packs, move_x).astype(LOW), units_sum_first, units_sum_last, heads_sum_last
    )
    pack = even_sum(pack, move_y)
    heads_sum_first, pack = pack[:128], pack[128:]
    grad_first = grad_hidden + layer_norm_back(chunks[:row_count], residual, gain_one)[0]

    passed = swap(owner(0, result, grad_first))
    kept = owner(0, grad_first, result)
    boundary = owner(0, jnp.stack([kept, passed]), jnp.stack([passed, kept]))
    boundary = boundary.reshape(1, 2, 1, row_count, model_width)

    units_sum = owner(0, units_sum_first, units_sum_last)
    heads_sum = owner(0, heads_sum_first, heads_sum_last)
    units_theirs = swap(owner(0, units_sum_last, units_sum_first))
    heads_theirs = swap(owner(0, heads_sum_last, heads_sum_first).astype(LOW))
    low_units, high_units = owner(0, units_sum, units_theirs), owner(0, units_theirs, units_sum)
    g_key_value = heads_sum.astype(FULL)
    g_query_out = heads_theirs.astype(FULL)
    g_w_qkv = jnp.stack([g_query_out[0:64].T, g_key_value[0:64].T, g_key_value[64:128].T], axis=1)
    g_b_qv = jnp.stack([pack[6, 384:448], pack[6, 320:384]])
    return (
        boundary,
        pack[0:1],
        pack[1:2],
        g_w_qkv[None],
        g_b_qv[None],
        g_query_out[64:128][None],
        pack[2:3],
        pack[3:4],
        pack[4:5],
        jnp.concatenate([low_units[:half_rows], high_units[:half_rows]]).astype(FULL).T[None],
        pack[6:7, 0:256],
        jnp.concatenate([low_units[half_rows:], high_units[half_rows:]]).astype(FULL)[None],
        pack[5:6],
    )


def solution(mesh):
    return jax.shard_map(
        per_device,
        mesh=mesh,
        in_specs=(
            P(None, "ctx", "tensor", None),
            P(),
            P("section", None),
            P("section", None),
            P("section", None, None, "tensor"),
            P("section", None, "tensor"),
            P("section", "tensor", None),
            P("section", None),
            P("section", None),
            P("section", None),
            P("section", None, "tensor"),
            P("section", "tensor"),
            P("section", "tensor", None),
            P("section", None),
            P(None, "ctx", "tensor", None),
        ),
        out_specs=(
            P("section", None, "ctx", "tensor", None),
            P("section", None),
            P("section", None),
            P("section", None, None, "tensor"),
            P("section", None, "tensor"),
            P("section", "tensor", None),
            P("section", None),
            P("section", None),
            P("section", None),
            P("section", None, "tensor"),
            P("section", "tensor"),
            P("section", "tensor", None),
            P("section", None),
        ),
        check_vma=False,
    )
```

```python
import functools
import math

import jax
import jax.numpy as jnp
from jax import lax
from jax.experimental import pallas as pl
from jax.experimental.pallas import tpu as pltpu
from jax.sharding import PartitionSpec as P

HEAD_DIM = 64
EPSILON = 1e-05
MASK_FILL = -1e30
BASE_TWO_SCALE = 0.125 * math.log2(math.e)
SIDE = 4
TILE = 256
LN_TWO = math.log(2.0)
LOW = jnp.bfloat16
FULL = jnp.float32


def move_z(block, distance):
    route = [
        (x * SIDE + z, x * SIDE + (z + distance) % SIDE) for x in range(SIDE) for z in range(SIDE)
    ]
    return lax.ppermute(block, "tensor", route)


def move_x(block, distance):
    route = [
        (x * SIDE + z, (x + distance) % SIDE * SIDE + z) for x in range(SIDE) for z in range(SIDE)
    ]
    return lax.ppermute(block, "tensor", route)


def move_y(block, distance):
    return lax.ppermute(block, "ctx", [(y, (y + distance) % SIDE) for y in range(SIDE)])


def move_y_open(block, distance):
    route = [(y, y + distance) for y in range(SIDE) if 0 <= y + distance < SIDE]
    return lax.ppermute(block, "ctx", route)


def move_x_in(block, distance, section):
    base = section * SIDE * SIDE
    route = [
        (base + x * SIDE + z, base + (x + distance) % SIDE * SIDE + z)
        for x in range(SIDE)
        for z in range(SIDE)
    ]
    return lax.ppermute(block, ("section", "tensor"), route)


def move_y_in(block, distance, section):
    base = section * SIDE
    route = [(base + y, base + (y + distance) % SIDE) for y in range(SIDE)]
    return lax.ppermute(block, ("section", "ctx"), route)


def swap(block):
    return lax.ppermute(block, "section", [(0, 1), (1, 0)])


def send_to(block, section):
    return lax.ppermute(block, "section", [(1 - section, section)])


def gather_z(rows):
    return jnp.concatenate([rows] + [move_z(rows, d) for d in range(1, SIDE)], axis=0)


def scatter_z(rows):
    chunks = rows.reshape(SIDE, rows.shape[0] // SIDE, rows.shape[1])
    total = chunks[0].astype(FULL)
    for d in range(1, SIDE):
        total = total + move_z(chunks[d], -d).astype(FULL)
    return total


def even_sum(block, move):
    low = block.astype(FULL)
    return (low + move(block, 2).astype(FULL)) + (
        move(block, 1).astype(FULL) + move(block, 3).astype(FULL)
    )


def even_pairs(blocks, move):
    return (blocks[0].astype(FULL) + move(blocks[2], -2).astype(FULL)) + (
        move(blocks[1], -1).astype(FULL) + move(blocks[3], -3).astype(FULL)
    )


def layer_norm(values, gain, bias):
    center = values - jnp.mean(values, axis=-1, keepdims=True)
    spread = jnp.mean(center * center, axis=-1, keepdims=True)
    return center * lax.rsqrt(spread + EPSILON) * gain + bias


def layer_norm_back(grad, values, gain):
    center = values - jnp.mean(values, axis=-1, keepdims=True)
    scale = lax.rsqrt(jnp.mean(center * center, axis=-1, keepdims=True) + EPSILON)
    unit = center * scale
    part = grad * gain
    back = scale * (
        part
        - jnp.mean(part, axis=-1, keepdims=True)
        - unit * jnp.mean(part * unit, axis=-1, keepdims=True)
    )
    return back, jnp.sum(grad * unit, axis=0), jnp.sum(grad, axis=0)


def local_dot(left, right):
    return jnp.dot(left, right, preferred_element_type=FULL)


def back_dot(left, right):
    return jnp.einsum("rf,df->rd", left, right, preferred_element_type=FULL)


def outer_sum(left, right):
    return jnp.einsum("rd,rf->df", left, right, preferred_element_type=FULL)


def nt_dot(left, right):
    return lax.dot_general(left, right, (((1,), (1,)), ((), ())), preferred_element_type=FULL)


def tn_dot(left, right):
    return lax.dot_general(left, right, (((0,), (0,)), ((), ())), preferred_element_type=FULL)


def place_in_block(order, x_here, z_here):
    from_x = (x_here + (order >> 8)) & 3
    from_z = (z_here - ((order >> 6) & 3)) & 3
    return (from_x << 8) + (from_z << 6) + (order & 63)


def first_of_document(place, start_one, start_two):
    return jnp.where(place >= start_two, start_two, jnp.where(place >= start_one, start_one, 0))


def tile_bounds(scalar_ref, indices, rows_all):
    block, x_here, _, start_one, start_two = [scalar_ref[i] for i in range(5)]
    least, most = [], []
    for index in indices:
        place = block * rows_all + ((x_here + index) & 3) * TILE
        least.append(first_of_document(place, start_one, start_two))
        most.append(first_of_document(place + TILE - 1, start_one, start_two))
    return functools.reduce(jnp.minimum, least), functools.reduce(jnp.maximum, most)


def tile_limits(scalar_ref, index, rows_all):
    block, x_here, z_here, start_one, start_two = [scalar_ref[i] for i in range(5)]
    order = lax.broadcasted_iota(jnp.int32, (1, TILE), 1) + index * TILE
    high = block * rows_all + place_in_block(order, x_here, z_here)
    return first_of_document(high, start_one, start_two), high


def attend_kernel(
    scalar_ref, own_ref, kv1_ref, kv2_ref, kv3_ref, out_ref, peak, mixed, held, keys, arrived
):
    block = scalar_ref[0]
    rows_all = own_ref.shape[0]
    tiles = rows_all // TILE
    copies = [
        pltpu.make_async_copy(ref, held.at[d], arrived.at[d])
        for d, ref in enumerate((kv1_ref, kv2_ref, kv3_ref))
    ]
    for copy in copies:
        copy.start()
    peak[...] = jnp.full_like(peak, MASK_FILL)
    mixed[...] = jnp.zeros_like(mixed)
    keys[...] = place_in_block(
        lax.broadcasted_iota(jnp.int32, keys.shape, 0), scalar_ref[1], scalar_ref[2]
    )
    for d in range(SIDE):
        if d > 0:
            copies[d - 1].wait()
        start = (block - d) * rows_all

        @pl.loop(0, tiles // 2)
        def _(pair, d=d, start=start):
            indices = [pair * 2, pair * 2 + 1]
            least, most = tile_bounds(scalar_ref, indices, rows_all)

            def step(masked):
                key_values = own_ref[:, 0:128] if d == 0 else held[d - 1]
                lanes = lax.broadcasted_iota(jnp.int32, key_values.shape, 1)
                ones_values = jnp.where(lanes < HEAD_DIM, jnp.ones_like(key_values), key_values)
                raws = []
                for index in indices:
                    rows = pl.ds(pl.multiple_of(index * TILE, TILE), TILE)
                    raws.append(nt_dot(key_values, own_ref[rows, 128:256]))
                for index, raw in zip(indices, raws):
                    if masked:
                        low, high = tile_limits(scalar_ref, index, rows_all)
                        allowed = keys[...] >= low - start
                        if d == 0:
                            allowed = allowed & (keys[...] <= high - start)
                        raw = jnp.where(allowed, raw, MASK_FILL)
                    old = peak[index]
                    top = jnp.maximum(old, jnp.max(raw, axis=0, keepdims=True))
                    weight = jnp.exp2(raw - top).astype(LOW)
                    peak[index] = top
                    mixed[index] = mixed[index] * jnp.exp2(old - top) + tn_dot(ones_values, weight)

            if d == 0:
                step(True)
            else:
                reached = (block >= d) & (least < start + rows_all)
                pl.when(reached & (most <= start))(lambda: step(False))
                pl.when(reached & (most > start))(lambda: step(True))

    @pl.loop(0, tiles)
    def _(index):
        rows = pl.ds(pl.multiple_of(index * TILE, TILE), TILE)
        sums = mixed[index]
        count = sums[0:1, :]
        level = peak[index] + jnp.log2(count)
        lines = lax.broadcasted_iota(jnp.int32, sums.shape, 0)
        out_ref[rows, :] = jnp.where(lines < HEAD_DIM, level, sums / count).T


def attend_back_kernel(
    scalar_ref, own_ref, kv1_ref, kv2_ref, kv3_ref, kept_ref, grad_ref,
    dq_ref, d0_ref, d1_ref, d2_ref, d3_ref,
    query_sum, key_sum, held, keys, stats, arrived,
):
    block = scalar_ref[0]
    rows_all = own_ref.shape[0]
    tiles = rows_all // TILE
    copies = [
        pltpu.make_async_copy(ref, held.at[d], arrived.at[d])
        for d, ref in enumerate((kv1_ref, kv2_ref, kv3_ref))
    ]
    for copy in copies:
        copy.start()
    query_sum[...] = jnp.zeros_like(query_sum)
    keys[...] = place_in_block(
        lax.broadcasted_iota(jnp.int32, keys.shape, 0), scalar_ref[1], scalar_ref[2]
    )

    @pl.loop(0, tiles)
    def _(index):
        rows = pl.ds(pl.multiple_of(index * TILE, TILE), TILE)
        kept = kept_ref[rows, :]
        stats[index, 0:1, :] = kept.T[0:1, :]
        stats[index, 1:2, :] = jnp.sum((kept * grad_ref[rows, :].astype(FULL)).T, axis=0, keepdims=True)

    for d, out_ref in enumerate((d0_ref, d1_ref, d2_ref, d3_ref)):
        if d > 0:
            copies[d - 1].wait()

        @pl.when(block >= d)
        def _(d=d, out_ref=out_ref):
            start = (block - d) * rows_all
            key_sum[...] = jnp.zeros_like(key_sum)

            @pl.loop(0, tiles)
            def _(index):
                indices = [index]
                least, most = tile_bounds(scalar_ref, indices, rows_all)

                def step(masked):
                    key_values = own_ref[:, 0:128] if d == 0 else held[d - 1]
                    spans = [pl.ds(pl.multiple_of(index * TILE, TILE), TILE) for index in indices]
                    raws = [nt_dot(key_values, own_ref[rows, 128:256]) for rows in spans]
                    meets = [nt_dot(key_values, grad_ref[rows, :]) for rows in spans]
                    for index, rows, raw, meet in zip(indices, spans, raws, meets):
                        probs = jnp.exp2(raw - stats[index, 0:1, :])
                        if masked:
                            low, high = tile_limits(scalar_ref, index, rows_all)
                            allowed = keys[...] >= low - start
                            if d == 0:
                                allowed = allowed & (keys[...] <= high - start)
                            probs = jnp.where(allowed, probs, 0.0)
                        grad_scores = (probs * (meet - stats[index, 1:2, :])).astype(LOW)
                        key_sum[...] += local_dot(grad_scores, own_ref[rows, 128:256]) * LN_TWO + local_dot(
                            probs.astype(LOW), grad_ref[rows, :]
                        )
                        query_sum[rows, :] += tn_dot(grad_scores, key_values)

                if d == 0:
                    step(True)
                else:
                    pl.when(most <= start)(lambda: step(False))
                    pl.when((most > start) & (least < start + rows_all))(lambda: step(True))

            out_ref[...] = key_sum[...].astype(LOW)

        if d > 0:

            @pl.when(block < d)
            def _(out_ref=out_ref):
                out_ref[...] = jnp.zeros_like(out_ref)

    lanes = lax.broadcasted_iota(jnp.int32, dq_ref.shape, 1)
    dq_ref[...] = jnp.where(lanes < HEAD_DIM, query_sum[...] * 0.125, 0.0).astype(LOW)


VMEM_SPEC = pl.BlockSpec(memory_space=pltpu.VMEM)
SMEM_SPEC = pl.BlockSpec(memory_space=pltpu.SMEM)
FAR_SPEC = pl.BlockSpec(memory_space=pltpu.HBM)


def attend(spots, own, others):
    rows = own.shape[0]
    return pl.pallas_call(
        attend_kernel,
        out_shape=jax.ShapeDtypeStruct((rows, 128), FULL),
        in_specs=[SMEM_SPEC, VMEM_SPEC] + [FAR_SPEC] * 3,
        out_specs=VMEM_SPEC,
        scratch_shapes=[
            pltpu.VMEM((rows // TILE, 1, TILE), FULL),
            pltpu.VMEM((rows // TILE, 128, TILE), FULL),
            pltpu.VMEM((3, rows, 128), LOW),
            pltpu.VMEM((rows, 1), jnp.int32),
            pltpu.SemaphoreType.DMA((3,)),
        ],
        compiler_params=pltpu.CompilerParams(vmem_limit_bytes=40 << 20),
        cost_estimate=pl.CostEstimate(
            flops=4 * rows * 2 * rows * 128, bytes_accessed=4 << 20, transcendentals=rows * 2 * rows
        ),
        name="attend",
    )(spots["scalars"], own, *others)


def attend_back(spots, own, others, kept, grad):
    rows = own.shape[0]
    return pl.pallas_call(
        attend_back_kernel,
        out_shape=[jax.ShapeDtypeStruct((rows, 128), LOW)] * 5,
        in_specs=[SMEM_SPEC, VMEM_SPEC] + [FAR_SPEC] * 3 + [VMEM_SPEC] * 2,
        out_specs=[VMEM_SPEC] * 5,
        scratch_shapes=[
            pltpu.VMEM((rows, 128), FULL),
            pltpu.VMEM((rows, 128), FULL),
            pltpu.VMEM((3, rows, 128), LOW),
            pltpu.VMEM((rows, 1), jnp.int32),
            pltpu.VMEM((rows // TILE, 8, TILE), FULL),
            pltpu.SemaphoreType.DMA((3,)),
        ],
        compiler_params=pltpu.CompilerParams(vmem_limit_bytes=40 << 20),
        cost_estimate=pl.CostEstimate(
            flops=10 * rows * 2 * rows * 128, bytes_accessed=6 << 20, transcendentals=rows * 2 * rows
        ),
        name="attend_back",
    )(spots["scalars"], own, *others, kept, grad)


def tie(first, *rest):
    return lax.optimization_barrier((first, *rest))


X_GROUPS = [[x * SIDE + z for x in range(SIDE)] for z in range(SIDE)]


def forward_attention(residual, normed_all, spots, vectors, bias_qkv, w_heads, w_back):
    b_out = vectors[2]
    projected = ((nt_dot(normed_all, w_heads) + bias_qkv) * spots["scale"]).astype(LOW)
    width = projected.shape[1] // SIDE
    pieces = [projected[:, d * width : (d + 1) * width] for d in range(SIDE)]
    own = jnp.concatenate([pieces[0]] + [move_x(pieces[d], -d) for d in range(1, SIDE)], axis=0)
    others = [move_y_open(own[:, 0:128], d) for d in range(1, SIDE)]
    kept = attend(spots, own, others)
    lanes = lax.broadcasted_iota(jnp.int32, kept.shape, 1)
    mixed = jnp.where(lanes < HEAD_DIM, 0.0, kept).astype(LOW)
    rows = mixed.shape[0] // SIDE
    mixed_rows = jnp.concatenate(
        [mixed[0:rows]] + [move_x(mixed[d * rows : (d + 1) * rows], d) for d in range(1, SIDE)], axis=1
    )
    hidden = residual + (scatter_z(local_dot(mixed_rows, w_back).astype(LOW)) + b_out)
    return hidden, (residual, normed_all, own, others, kept, mixed_rows)


def forward_hidden_units(hidden, vectors, b_up, w_up, w_down):
    gain_two, bias_two, b_down = vectors[3:6]
    normed_two_all = gather_z(layer_norm(hidden, gain_two, bias_two).astype(LOW))
    up_value = nt_dot(normed_two_all, w_up) + b_up
    activated = jax.nn.gelu(up_value).astype(LOW)
    result = hidden + (scatter_z(local_dot(activated, w_down).astype(LOW)) + b_down)
    return result, (hidden, normed_two_all, up_value, activated)


def backward_hidden_units(grad_out, grad_down_all, stored, vectors, w_up, w_down):
    hidden, normed_two_all, up_value, activated = stored
    gain_two = vectors[3]
    grad_down = grad_out.astype(LOW)
    g_b_down = jnp.sum(grad_down.astype(FULL), axis=0)
    _, gelu_pull = jax.vjp(jax.nn.gelu, up_value)
    (grad_up,) = gelu_pull(nt_dot(grad_down_all, w_down))
    grad_up = grad_up.astype(LOW)
    grad_normed_two = scatter_z(local_dot(grad_up, w_up).astype(LOW))
    g_w_down = tn_dot(activated, grad_down_all).astype(LOW)
    g_b_up = jnp.sum(grad_up.astype(FULL), axis=0)
    g_w_up = tn_dot(grad_up, normed_two_all).astype(LOW)
    grad_hidden_part, g_gain_two, g_bias_two = layer_norm_back(grad_normed_two, hidden, gain_two)
    grad_hidden = grad_out + grad_hidden_part
    return grad_hidden, (g_gain_two, g_bias_two, g_b_down), g_b_up, g_w_up, g_w_down


def backward_mixed(grad_hidden, stored, w_back, spots):
    mixed_rows = stored[5]
    grad_attn = grad_hidden.astype(LOW)
    g_b_out = jnp.sum(grad_attn.astype(FULL), axis=0)
    grad_attn_all = gather_z(grad_attn)
    grad_mixed = (nt_dot(grad_attn_all, w_back) * spots["upper"]).astype(LOW)
    pieces = [grad_mixed[:, d * 128 : (d + 1) * 128] for d in range(SIDE)]
    grad_own = jnp.concatenate(
        [pieces[0]] + [move_x(pieces[d], -d) for d in range(1, SIDE)], axis=0
    )
    g_w_out = tn_dot(mixed_rows, grad_attn_all).astype(LOW)
    return grad_own, g_b_out, g_w_out


def backward_heads(parts):
    dq, dkv0, dkv1, dkv2, dkv3 = parts
    dkv = dkv0.astype(FULL)
    for d, part in enumerate((dkv1, dkv2, dkv3), 1):
        dkv = dkv + move_y_open(part, -d).astype(FULL)
    grad_own = jnp.concatenate([dkv.astype(LOW), dq], axis=1)
    rows = grad_own.shape[0] // SIDE
    return jnp.concatenate(
        [grad_own[0:rows]] + [move_x(grad_own[d * rows : (d + 1) * rows], d) for d in range(1, SIDE)],
        axis=1,
    )


def backward_entry(grad_qkv, grad_hidden, stored, vectors, w_heads):
    residual, normed_all = stored[0:2]
    gain_one = vectors[0]
    grad_normed = scatter_z(local_dot(grad_qkv, w_heads).astype(LOW))
    g_w_heads = tn_dot(grad_qkv, normed_all).astype(LOW)
    g_b_qkv = jnp.sum(grad_qkv.astype(FULL), axis=0)
    grad_residual_part, g_gain_one, g_bias_one = layer_norm_back(grad_normed, residual, gain_one)
    return grad_hidden + grad_residual_part, (g_gain_one, g_bias_one), g_b_qkv, g_w_heads


def per_device(
    inputs,
    segments,
    gain_one,
    bias_one,
    w_qkv,
    b_qv,
    w_out,
    b_out,
    gain_two,
    bias_two,
    w_up,
    b_up,
    w_down,
    b_down,
    cotangent,
):
    here = lax.axis_index("section")
    block = lax.axis_index("ctx")
    spot = lax.axis_index("tensor")
    x_here, z_here = spot // SIDE, spot % SIDE
    row_count, model_width = inputs.shape[2], inputs.shape[3]

    def owner(layer, yes, no):
        return jnp.where(here == layer, yes, no)

    sequence = lax.dynamic_index_in_dim(inputs, here, 0, False)[0].astype(FULL)
    grad_last = lax.dynamic_index_in_dim(cotangent, here, 0, False)[0].astype(FULL)
    grad_last_all = lax.dynamic_index_in_dim(cotangent, here, 0, False)[0]

    gap = jnp.zeros((HEAD_DIM,), LOW)
    biases = jnp.concatenate(
        [b_up[0], gap, b_qv[0, 1], b_qv[0, 0], gap, jnp.zeros((model_width - 512,), LOW)]
    )[None]
    heads_kv = jnp.concatenate(
        [w_qkv[0, :, 1].T, w_qkv[0, :, 2].T, biases, jnp.zeros((15, model_width), LOW)], axis=0
    )
    heads_qo = jnp.concatenate(
        [w_qkv[0, :, 0].T, w_out[0], jnp.zeros((16, model_width), LOW)], axis=0
    )
    heads_qo_other = swap(heads_qo)
    small = jnp.concatenate(
        [gain_one, bias_one, b_out, gain_two, bias_two, b_down, jnp.zeros((2, model_width), LOW)],
        axis=0,
    )
    small_other = swap(small)
    up_own, down_other = w_up[0].T, swap(w_down[0])
    downward = [(x_here - d) % SIDE for d in range(SIDE)]

    def reorder(pieces):
        return [lax.dynamic_index_in_dim(pieces, place, 0, False) for place in downward]

    def half_heads(layer):
        return owner(layer, heads_kv, heads_qo_other)

    def join_heads(layer, mine, theirs):
        key_value, query_out = owner(layer, mine, theirs), owner(layer, theirs, mine)
        whole = jnp.concatenate([key_value[:, :128], query_out[:, :128]], axis=1)
        back = query_out[:, :128].reshape(SIDE * 128, model_width)
        rows = key_value[:, 128, :512].astype(FULL)
        bias_heads = rows[:, 256:].reshape(1, SIDE * TILE)
        bias_up = jnp.concatenate(reorder(rows[:, :256])).reshape(1, SIDE * TILE)
        return (whole.reshape(SIDE * TILE, model_width), back), bias_heads, bias_up

    def gather_whole(half):
        return lax.all_gather(half, "tensor", axis=0, tiled=True, axis_index_groups=X_GROUPS)

    def join_units(layer, mine):
        theirs = swap(mine)
        return owner(layer, mine, theirs), owner(layer, theirs, mine)

    smalls = (owner(0, small, small_other), owner(0, small_other, small))
    vectors = [
        tuple(smalls[layer][row : row + 1].astype(FULL) for row in range(6)) for layer in range(2)
    ]
    normed = layer_norm(sequence, *vectors[0][0:2]).astype(LOW)
    half, normed = tie(half_heads(0), normed)
    mine = jnp.stack([half] + [move_x(half, d) for d in range(1, SIDE)])
    half = owner(0, up_own, down_other)
    normed_all, mine, half, grad_last_all = tie(gather_z(normed), mine, half, gather_z(grad_last_all))
    heads_first, bias_heads_first, bias_up_first = join_heads(0, mine, swap(mine))
    units_first = gather_whole(half)
    heads_last = gather_whole(half_heads(1)).reshape(SIDE, -1, model_width)
    units_last = gather_whole(owner(1, up_own, down_other))
    normed_all, segments = tie(normed_all, segments)
    segment_ids = lax.dynamic_index_in_dim(segments, here, 0, False)
    start_one = jnp.sum((segment_ids < 1).astype(jnp.int32))
    start_two = jnp.sum((segment_ids < 2).astype(jnp.int32))

    lane = jnp.arange(SIDE * TILE) % TILE
    spots = {
        "scalars": jnp.stack([block, x_here, z_here, start_one, start_two]).astype(jnp.int32),
        "scale": jnp.where(lane < 128, 1.0, jnp.where(lane < 192, BASE_TWO_SCALE, 0.0)).astype(FULL),
        "upper": (jnp.arange(SIDE * 128) % 128 >= HEAD_DIM).astype(FULL),
    }

    hidden, kept_heads_first = forward_attention(
        sequence, normed_all, spots, vectors[0], bias_heads_first, *heads_first
    )
    units_first = join_units(0, units_first)
    middle, kept_units_first = forward_hidden_units(hidden, vectors[0], bias_up_first, *units_first)
    mine = jnp.stack(reorder(heads_last))
    middle, mine, theirs = tie(middle, mine, swap(mine))
    heads_last, bias_heads_last, bias_up_last = join_heads(1, mine, theirs)
    middle = middle.astype(LOW).astype(FULL)
    normed_all = gather_z(layer_norm(middle, *vectors[1][0:2]).astype(LOW))
    hidden, kept_heads_last = forward_attention(
        middle, normed_all, spots, vectors[1], bias_heads_last, *heads_last
    )
    units_last = join_units(1, units_last)
    result, kept_units_last = forward_hidden_units(hidden, vectors[1], bias_up_last, *units_last)

    def swap_grads(layer, first, second):
        return owner(layer, first, second), swap(owner(layer, second, first))

    def add_grads(kept, arrived):
        return (kept.astype(FULL) + arrived.astype(FULL)).astype(LOW)

    def scatter_whole(grads):
        return lax.psum_scatter(
            grads, "tensor", scatter_dimension=0, tiled=True, axis_index_groups=X_GROUPS
        )

    def split_heads(g_w_heads, g_w_out):
        heads = g_w_heads.reshape(SIDE, TILE, model_width)
        return heads[:, 0:128], heads[:, 128:256] + g_w_out.reshape(SIDE, 128, model_width)

    turn = jnp.stack(downward)[None, :] == jnp.arange(SIDE)[:, None]

    def pack_vectors(heads, units, g_b_out, g_b_up, g_b_qkv):
        by_turn = jnp.sum(
            jnp.where(turn[:, :, None], g_b_up.reshape(SIDE, 1, TILE), 0.0), axis=0
        )
        return jnp.concatenate(
            [
                jnp.stack([*heads, g_b_out, *units]),
                jnp.concatenate([by_turn, g_b_qkv.reshape(SIDE, TILE)], axis=1).reshape(2, -1),
            ],
            axis=0,
        )

    grad_hidden, vec_units_last, g_b_up_last, g_up, g_down = backward_hidden_units(
        grad_last, grad_last_all, kept_units_last, vectors[1], *units_last
    )
    grad_hidden, units_kept, units_arrived = tie(grad_hidden, *swap_grads(1, g_up, g_down))
    units_sum_last = scatter_whole(add_grads(units_kept, units_arrived))
    grad_mixed, g_b_out_last, g_out = backward_mixed(grad_hidden, kept_heads_last, heads_last[1], spots)
    grad_qkv = backward_heads(attend_back(spots, *kept_heads_last[2:5], grad_mixed))
    grad_middle, vec_heads_last, g_b_qkv_last, g_heads = backward_entry(
        grad_qkv, grad_hidden, kept_heads_last, vectors[1], heads_last[0]
    )
    heads_kept, heads_arrived = swap_grads(1, *split_heads(g_heads, g_out))

    grad_middle = grad_middle.astype(LOW).astype(FULL)
    grad_down_all, heads_kept, heads_arrived = tie(
        gather_z(grad_middle.astype(LOW)), heads_kept, heads_arrived
    )
    heads_sum_last = scatter_whole(
        jnp.concatenate(reorder(add_grads(heads_kept, heads_arrived)), axis=0)
    )
    grad_hidden, vec_units_first, g_b_up_first, g_up, g_down = backward_hidden_units(
        grad_middle, grad_down_all, kept_units_first, vectors[0], *units_first
    )
    grad_hidden, units_kept, units_arrived, units_sum_last = tie(
        grad_hidden, *swap_grads(0, g_up, g_down), units_sum_last
    )
    units_sum_first = scatter_whole(add_grads(units_kept, units_arrived))
    grad_mixed, g_b_out_first, g_out = backward_mixed(grad_hidden, kept_heads_first, heads_first[1], spots)
    parts = attend_back(spots, *kept_heads_first[2:5], grad_mixed)
    parts, units_sum_first, heads_sum_last = tie(parts, units_sum_first, heads_sum_last)
    units_sum_first, units_sum_last, heads_sum_last = lax.psum(
        (units_sum_first, units_sum_last, heads_sum_last), "ctx"
    )
    grad_qkv = backward_heads(parts)

    gain_one, bias_one = vectors[0][0:2]
    residual, normed_all = kept_heads_first[0:2]
    grad_normed = local_dot(grad_qkv, heads_first[0])
    g_bias_one = jnp.sum(grad_normed, axis=0)
    g_gain_one = jnp.sum(grad_normed * ((normed_all.astype(FULL) - bias_one) / gain_one), axis=0)
    g_b_qkv_first = jnp.sum(grad_qkv.astype(FULL), axis=0)
    sums_first = pack_vectors(
        (g_gain_one, g_bias_one), vec_units_first, g_b_out_first, g_b_up_first, g_b_qkv_first
    )
    sums_last = pack_vectors(vec_heads_last, vec_units_last, g_b_out_last, g_b_up_last, g_b_qkv_last)
    common = jnp.pad(jnp.concatenate([sums_first[:6], sums_last[:6]]), ((0, 4), (0, 0))).astype(LOW)
    chunks = grad_normed.astype(LOW).reshape(SIDE, row_count, model_width)
    chunks = even_pairs([jnp.concatenate([chunks[d], common], axis=0) for d in range(SIDE)], move_z)
    heads_kept, heads_arrived = swap_grads(0, *split_heads(tn_dot(grad_qkv, normed_all).astype(LOW), g_out))
    halves = add_grads(heads_kept, heads_arrived)
    sums_first = jnp.concatenate([chunks[row_count : row_count + 6], sums_first[6:]])
    sums_last = jnp.concatenate([chunks[row_count + 6 : row_count + 12], sums_last[6:]])
    sums = owner(0, sums_first, sums_last) + swap(owner(0, sums_last, sums_first))
    common = sums[:6].astype(LOW)
    split = sums[6:].reshape(SIDE, 1, 512).astype(LOW)
    packs = [
        jnp.concatenate(
            [
                halves[d],
                common,
                jnp.pad(split[d], ((0, 0), (0, model_width - 512))),
                jnp.zeros((9, model_width), LOW),
            ],
            axis=0,
        )
        for d in range(SIDE)
    ]
    pack = even_sum(even_pairs(packs, move_x).astype(LOW), move_y)
    pack, units_sum_first, units_sum_last, heads_sum_last = tie(
        pack, units_sum_first, units_sum_last, heads_sum_last
    )
    heads_sum_first, pack = pack[:128], pack[128:]
    grad_first = grad_hidden + layer_norm_back(chunks[:row_count], residual, gain_one)[0]

    passed = swap(owner(0, result, grad_first))
    kept = owner(0, grad_first, result)
    boundary = owner(0, jnp.stack([kept, passed]), jnp.stack([passed, kept]))
    boundary = boundary.reshape(1, 2, 1, row_count, model_width)

    units_sum = owner(0, units_sum_first, units_sum_last)
    heads_sum = owner(0, heads_sum_first, heads_sum_last)
    units_theirs = swap(owner(0, units_sum_last, units_sum_first))
    heads_theirs = swap(owner(0, heads_sum_last, heads_sum_first).astype(LOW))
    g_key_value = heads_sum.astype(FULL)
    g_query_out = heads_theirs.astype(FULL)
    g_w_qkv = jnp.stack([g_query_out[0:64].T, g_key_value[0:64].T, g_key_value[64:128].T], axis=1)
    g_b_qv = jnp.stack([pack[6, 384:448], pack[6, 320:384]])
    return (
        boundary,
        pack[0:1],
        pack[1:2],
        g_w_qkv[None],
        g_b_qv[None],
        g_query_out[64:128][None],
        pack[2:3],
        pack[3:4],
        pack[4:5],
        units_sum.astype(FULL).T[None],
        pack[6:7, 0:256],
        units_theirs.astype(FULL)[None],
        pack[5:6],
    )


def solution(mesh):
    return jax.shard_map(
        per_device,
        mesh=mesh,
        in_specs=(
            P(None, "ctx", "tensor", None),
            P(),
            P("section", None),
            P("section", None),
            P("section", None, None, "tensor"),
            P("section", None, "tensor"),
            P("section", "tensor", None),
            P("section", None),
            P("section", None),
            P("section", None),
            P("section", None, "tensor"),
            P("section", "tensor"),
            P("section", "tensor", None),
            P("section", None),
            P(None, "ctx", "tensor", None),
        ),
        out_specs=(
            P("section", None, "ctx", "tensor", None),
            P("section", None),
            P("section", None),
            P("section", None, None, "tensor"),
            P("section", None, "tensor"),
            P("section", "tensor", None),
            P("section", None),
            P("section", None),
            P("section", None),
            P("section", None, "tensor"),
            P("section", "tensor"),
            P("section", "tensor", None),
            P("section", None),
        ),
        check_vma=False,
    )
```

```python
import functools
import math

import jax
import jax.numpy as jnp
from jax import lax
from jax.experimental import pallas as pl
from jax.experimental.pallas import tpu as pltpu
from jax.sharding import PartitionSpec as P

HEAD_DIM = 64
EPSILON = 1e-05
MASK_FILL = -1e30
BASE_TWO_SCALE = 0.125 * math.log2(math.e)
SIDE = 4
TILE = 256
LN_TWO = math.log(2.0)
LOW = jnp.bfloat16
FULL = jnp.float32


def move_z(block, distance):
    route = [
        (x * SIDE + z, x * SIDE + (z + distance) % SIDE) for x in range(SIDE) for z in range(SIDE)
    ]
    return lax.ppermute(block, "tensor", route)


def move_x(block, distance):
    route = [
        (x * SIDE + z, (x + distance) % SIDE * SIDE + z) for x in range(SIDE) for z in range(SIDE)
    ]
    return lax.ppermute(block, "tensor", route)


def move_y(block, distance):
    return lax.ppermute(block, "ctx", [(y, (y + distance) % SIDE) for y in range(SIDE)])


def move_y_open(block, distance):
    route = [(y, y + distance) for y in range(SIDE) if 0 <= y + distance < SIDE]
    return lax.ppermute(block, "ctx", route)


def move_x_in(block, distance, section):
    base = section * SIDE * SIDE
    route = [
        (base + x * SIDE + z, base + (x + distance) % SIDE * SIDE + z)
        for x in range(SIDE)
        for z in range(SIDE)
    ]
    return lax.ppermute(block, ("section", "tensor"), route)


def move_y_in(block, distance, section):
    base = section * SIDE
    route = [(base + y, base + (y + distance) % SIDE) for y in range(SIDE)]
    return lax.ppermute(block, ("section", "ctx"), route)


def swap(block):
    return lax.ppermute(block, "section", [(0, 1), (1, 0)])


def send_to(block, section):
    return lax.ppermute(block, "section", [(1 - section, section)])


def gather_z(rows):
    return jnp.concatenate([rows] + [move_z(rows, d) for d in range(1, SIDE)], axis=0)


def scatter_z(rows):
    chunks = rows.reshape(SIDE, rows.shape[0] // SIDE, rows.shape[1])
    total = chunks[0].astype(FULL)
    for d in range(1, SIDE):
        total = total + move_z(chunks[d], -d).astype(FULL)
    return total


def even_sum(block, move):
    low = block.astype(FULL)
    return (low + move(block, 2).astype(FULL)) + (
        move(block, 1).astype(FULL) + move(block, 3).astype(FULL)
    )


def even_pairs(blocks, move):
    return (blocks[0].astype(FULL) + move(blocks[2], -2).astype(FULL)) + (
        move(blocks[1], -1).astype(FULL) + move(blocks[3], -3).astype(FULL)
    )


def layer_norm(values, gain, bias):
    center = values - jnp.mean(values, axis=-1, keepdims=True)
    spread = jnp.mean(center * center, axis=-1, keepdims=True)
    return center * lax.rsqrt(spread + EPSILON) * gain + bias


def layer_norm_back(grad, values, gain):
    center = values - jnp.mean(values, axis=-1, keepdims=True)
    scale = lax.rsqrt(jnp.mean(center * center, axis=-1, keepdims=True) + EPSILON)
    unit = center * scale
    part = grad * gain
    back = scale * (
        part
        - jnp.mean(part, axis=-1, keepdims=True)
        - unit * jnp.mean(part * unit, axis=-1, keepdims=True)
    )
    return back, jnp.sum(grad * unit, axis=0), jnp.sum(grad, axis=0)


def local_dot(left, right):
    return jnp.dot(left, right, preferred_element_type=FULL)


def back_dot(left, right):
    return jnp.einsum("rf,df->rd", left, right, preferred_element_type=FULL)


def outer_sum(left, right):
    return jnp.einsum("rd,rf->df", left, right, preferred_element_type=FULL)


def nt_dot(left, right):
    return lax.dot_general(left, right, (((1,), (1,)), ((), ())), preferred_element_type=FULL)


def tn_dot(left, right):
    return lax.dot_general(left, right, (((0,), (0,)), ((), ())), preferred_element_type=FULL)


def place_in_block(order, x_here, z_here):
    from_x = (x_here + (order >> 8)) & 3
    from_z = (z_here - ((order >> 6) & 3)) & 3
    return (from_x << 8) + (from_z << 6) + (order & 63)


def first_of_document(place, start_one, start_two):
    return jnp.where(place >= start_two, start_two, jnp.where(place >= start_one, start_one, 0))


def tile_bounds(scalar_ref, indices, rows_all):
    block, x_here, _, start_one, start_two = [scalar_ref[i] for i in range(5)]
    least, most = [], []
    for index in indices:
        place = block * rows_all + ((x_here + index) & 3) * TILE
        least.append(first_of_document(place, start_one, start_two))
        most.append(first_of_document(place + TILE - 1, start_one, start_two))
    return functools.reduce(jnp.minimum, least), functools.reduce(jnp.maximum, most)


def tile_limits(scalar_ref, index, rows_all):
    block, x_here, z_here, start_one, start_two = [scalar_ref[i] for i in range(5)]
    order = lax.broadcasted_iota(jnp.int32, (1, TILE), 1) + index * TILE
    high = block * rows_all + place_in_block(order, x_here, z_here)
    return first_of_document(high, start_one, start_two), high


def attend_kernel(
    scalar_ref, own_ref, kv1_ref, kv2_ref, kv3_ref, out_ref, peak, mixed, held, keys, arrived
):
    block = scalar_ref[0]
    rows_all = own_ref.shape[0]
    tiles = rows_all // TILE
    copies = [
        pltpu.make_async_copy(ref, held.at[d], arrived.at[d])
        for d, ref in enumerate((kv1_ref, kv2_ref, kv3_ref))
    ]
    for copy in copies:
        copy.start()
    peak[...] = jnp.full_like(peak, MASK_FILL)
    mixed[...] = jnp.zeros_like(mixed)
    keys[...] = place_in_block(
        lax.broadcasted_iota(jnp.int32, keys.shape, 0), scalar_ref[1], scalar_ref[2]
    )
    for d in range(SIDE):
        if d > 0:
            copies[d - 1].wait()
        start = (block - d) * rows_all

        @pl.loop(0, tiles // 2)
        def _(pair, d=d, start=start):
            indices = [pair * 2, pair * 2 + 1]
            least, most = tile_bounds(scalar_ref, indices, rows_all)

            def step(masked):
                key_values = own_ref[:, 0:128] if d == 0 else held[d - 1]
                lanes = lax.broadcasted_iota(jnp.int32, key_values.shape, 1)
                ones_values = jnp.where(lanes < HEAD_DIM, jnp.ones_like(key_values), key_values)
                raws = []
                for index in indices:
                    rows = pl.ds(pl.multiple_of(index * TILE, TILE), TILE)
                    raws.append(nt_dot(key_values, own_ref[rows, 128:256]))
                for index, raw in zip(indices, raws):
                    if masked:
                        low, high = tile_limits(scalar_ref, index, rows_all)
                        allowed = keys[...] >= low - start
                        if d == 0:
                            allowed = allowed & (keys[...] <= high - start)
                        raw = jnp.where(allowed, raw, MASK_FILL)
                    old = peak[index]
                    top = jnp.maximum(old, jnp.max(raw, axis=0, keepdims=True))
                    weight = jnp.exp2(raw - top).astype(LOW)
                    peak[index] = top
                    mixed[index] = mixed[index] * jnp.exp2(old - top) + tn_dot(ones_values, weight)

            if d == 0:
                step(True)
            else:
                reached = (block >= d) & (least < start + rows_all)
                pl.when(reached & (most <= start))(lambda: step(False))
                pl.when(reached & (most > start))(lambda: step(True))

    @pl.loop(0, tiles)
    def _(index):
        rows = pl.ds(pl.multiple_of(index * TILE, TILE), TILE)
        sums = mixed[index]
        count = sums[0:1, :]
        level = peak[index] + jnp.log2(count)
        lines = lax.broadcasted_iota(jnp.int32, sums.shape, 0)
        out_ref[rows, :] = jnp.where(lines < HEAD_DIM, level, sums / count).T


def attend_back_kernel(
    scalar_ref, own_ref, kv1_ref, kv2_ref, kv3_ref, kept_ref, grad_ref,
    dq_ref, d0_ref, d1_ref, d2_ref, d3_ref,
    query_sum, key_sum, held, keys, stats, arrived,
):
    block = scalar_ref[0]
    rows_all = own_ref.shape[0]
    tiles = rows_all // TILE
    copies = [
        pltpu.make_async_copy(ref, held.at[d], arrived.at[d])
        for d, ref in enumerate((kv1_ref, kv2_ref, kv3_ref))
    ]
    for copy in copies:
        copy.start()
    query_sum[...] = jnp.zeros_like(query_sum)
    keys[...] = place_in_block(
        lax.broadcasted_iota(jnp.int32, keys.shape, 0), scalar_ref[1], scalar_ref[2]
    )

    @pl.loop(0, tiles)
    def _(index):
        rows = pl.ds(pl.multiple_of(index * TILE, TILE), TILE)
        kept = kept_ref[rows, :]
        stats[index, 0:1, :] = kept.T[0:1, :]
        stats[index, 1:2, :] = jnp.sum((kept * grad_ref[rows, :].astype(FULL)).T, axis=0, keepdims=True)

    for d, out_ref in enumerate((d0_ref, d1_ref, d2_ref, d3_ref)):
        if d > 0:
            copies[d - 1].wait()

        @pl.when(block >= d)
        def _(d=d, out_ref=out_ref):
            start = (block - d) * rows_all
            key_sum[...] = jnp.zeros_like(key_sum)

            @pl.loop(0, tiles)
            def _(index):
                indices = [index]
                least, most = tile_bounds(scalar_ref, indices, rows_all)

                def step(masked):
                    key_values = own_ref[:, 0:128] if d == 0 else held[d - 1]
                    spans = [pl.ds(pl.multiple_of(index * TILE, TILE), TILE) for index in indices]
                    raws = [nt_dot(key_values, own_ref[rows, 128:256]) for rows in spans]
                    meets = [nt_dot(key_values, grad_ref[rows, :]) for rows in spans]
                    for index, rows, raw, meet in zip(indices, spans, raws, meets):
                        probs = jnp.exp2(raw - stats[index, 0:1, :])
                        if masked:
                            low, high = tile_limits(scalar_ref, index, rows_all)
                            allowed = keys[...] >= low - start
                            if d == 0:
                                allowed = allowed & (keys[...] <= high - start)
                            probs = jnp.where(allowed, probs, 0.0)
                        grad_scores = (probs * (meet - stats[index, 1:2, :])).astype(LOW)
                        key_sum[...] += local_dot(grad_scores, own_ref[rows, 128:256]) * LN_TWO + local_dot(
                            probs.astype(LOW), grad_ref[rows, :]
                        )
                        query_sum[rows, :] += tn_dot(grad_scores, key_values)

                if d == 0:
                    step(True)
                else:
                    pl.when(most <= start)(lambda: step(False))
                    pl.when((most > start) & (least < start + rows_all))(lambda: step(True))

            out_ref[...] = key_sum[...].astype(LOW)

        if d > 0:

            @pl.when(block < d)
            def _(out_ref=out_ref):
                out_ref[...] = jnp.zeros_like(out_ref)

    lanes = lax.broadcasted_iota(jnp.int32, dq_ref.shape, 1)
    dq_ref[...] = jnp.where(lanes < HEAD_DIM, query_sum[...] * 0.125, 0.0).astype(LOW)


VMEM_SPEC = pl.BlockSpec(memory_space=pltpu.VMEM)
SMEM_SPEC = pl.BlockSpec(memory_space=pltpu.SMEM)
FAR_SPEC = pl.BlockSpec(memory_space=pltpu.HBM)


def attend(spots, own, others):
    rows = own.shape[0]
    return pl.pallas_call(
        attend_kernel,
        out_shape=jax.ShapeDtypeStruct((rows, 128), FULL),
        in_specs=[SMEM_SPEC, VMEM_SPEC] + [FAR_SPEC] * 3,
        out_specs=VMEM_SPEC,
        scratch_shapes=[
            pltpu.VMEM((rows // TILE, 1, TILE), FULL),
            pltpu.VMEM((rows // TILE, 128, TILE), FULL),
            pltpu.VMEM((3, rows, 128), LOW),
            pltpu.VMEM((rows, 1), jnp.int32),
            pltpu.SemaphoreType.DMA((3,)),
        ],
        compiler_params=pltpu.CompilerParams(vmem_limit_bytes=40 << 20),
        cost_estimate=pl.CostEstimate(
            flops=4 * rows * 2 * rows * 128, bytes_accessed=4 << 20, transcendentals=rows * 2 * rows
        ),
        name="attend",
    )(spots["scalars"], own, *others)


def attend_back(spots, own, others, kept, grad):
    rows = own.shape[0]
    return pl.pallas_call(
        attend_back_kernel,
        out_shape=[jax.ShapeDtypeStruct((rows, 128), LOW)] * 5,
        in_specs=[SMEM_SPEC, VMEM_SPEC] + [FAR_SPEC] * 3 + [VMEM_SPEC] * 2,
        out_specs=[VMEM_SPEC] * 5,
        scratch_shapes=[
            pltpu.VMEM((rows, 128), FULL),
            pltpu.VMEM((rows, 128), FULL),
            pltpu.VMEM((3, rows, 128), LOW),
            pltpu.VMEM((rows, 1), jnp.int32),
            pltpu.VMEM((rows // TILE, 8, TILE), FULL),
            pltpu.SemaphoreType.DMA((3,)),
        ],
        compiler_params=pltpu.CompilerParams(vmem_limit_bytes=40 << 20),
        cost_estimate=pl.CostEstimate(
            flops=10 * rows * 2 * rows * 128, bytes_accessed=6 << 20, transcendentals=rows * 2 * rows
        ),
        name="attend_back",
    )(spots["scalars"], own, *others, kept, grad)


def tie(first, *rest):
    return lax.optimization_barrier((first, *rest))


X_GROUPS = [[x * SIDE + z for x in range(SIDE)] for z in range(SIDE)]


def forward_attention(residual, normed_all, spots, vectors, bias_qkv, w_heads, w_back):
    b_out = vectors[2]
    projected = ((nt_dot(normed_all, w_heads) + bias_qkv) * spots["scale"]).astype(LOW)
    width = projected.shape[1] // SIDE
    pieces = [projected[:, d * width : (d + 1) * width] for d in range(SIDE)]
    own = jnp.concatenate([pieces[0]] + [move_x(pieces[d], -d) for d in range(1, SIDE)], axis=0)
    others = [move_y_open(own[:, 0:128], d) for d in range(1, SIDE)]
    kept = attend(spots, own, others)
    lanes = lax.broadcasted_iota(jnp.int32, kept.shape, 1)
    mixed = jnp.where(lanes < HEAD_DIM, 0.0, kept).astype(LOW)
    rows = mixed.shape[0] // SIDE
    mixed_rows = jnp.concatenate(
        [mixed[0:rows]] + [move_x(mixed[d * rows : (d + 1) * rows], d) for d in range(1, SIDE)], axis=1
    )
    hidden = residual + (scatter_z(local_dot(mixed_rows, w_back).astype(LOW)) + b_out)
    return hidden, (residual, normed_all, own, others, kept, mixed_rows)


def forward_hidden_units(hidden, vectors, b_up, w_up, w_down):
    gain_two, bias_two, b_down = vectors[3:6]
    normed_two_all = gather_z(layer_norm(hidden, gain_two, bias_two).astype(LOW))
    up_value = nt_dot(normed_two_all, w_up) + b_up
    activated = jax.nn.gelu(up_value).astype(LOW)
    result = hidden + (scatter_z(local_dot(activated, w_down).astype(LOW)) + b_down)
    return result, (hidden, normed_two_all, up_value, activated)


def backward_hidden_units(grad_out, grad_down_all, stored, vectors, w_up, w_down):
    hidden, normed_two_all, up_value, activated = stored
    gain_two = vectors[3]
    grad_down = grad_out.astype(LOW)
    g_b_down = jnp.sum(grad_down.astype(FULL), axis=0)
    _, gelu_pull = jax.vjp(jax.nn.gelu, up_value)
    (grad_up,) = gelu_pull(nt_dot(grad_down_all, w_down))
    grad_up = grad_up.astype(LOW)
    grad_normed_two = scatter_z(local_dot(grad_up, w_up).astype(LOW))
    g_w_down = tn_dot(activated, grad_down_all).astype(LOW)
    g_b_up = jnp.sum(grad_up.astype(FULL), axis=0)
    g_w_up = tn_dot(grad_up, normed_two_all).astype(LOW)
    grad_hidden_part, g_gain_two, g_bias_two = layer_norm_back(grad_normed_two, hidden, gain_two)
    grad_hidden = grad_out + grad_hidden_part
    return grad_hidden, (g_gain_two, g_bias_two, g_b_down), g_b_up, g_w_up, g_w_down


def backward_mixed(grad_hidden, stored, w_back, spots):
    mixed_rows = stored[5]
    grad_attn = grad_hidden.astype(LOW)
    g_b_out = jnp.sum(grad_attn.astype(FULL), axis=0)
    grad_attn_all = gather_z(grad_attn)
    grad_mixed = (nt_dot(grad_attn_all, w_back) * spots["upper"]).astype(LOW)
    pieces = [grad_mixed[:, d * 128 : (d + 1) * 128] for d in range(SIDE)]
    grad_own = jnp.concatenate(
        [pieces[0]] + [move_x(pieces[d], -d) for d in range(1, SIDE)], axis=0
    )
    g_w_out = tn_dot(mixed_rows, grad_attn_all).astype(LOW)
    return grad_own, g_b_out, g_w_out


def backward_heads(parts):
    dq, dkv0, dkv1, dkv2, dkv3 = parts
    dkv = dkv0.astype(FULL)
    for d, part in enumerate((dkv1, dkv2, dkv3), 1):
        dkv = dkv + move_y_open(part, -d).astype(FULL)
    return jnp.concatenate([dkv.astype(LOW), dq], axis=1)


def spread_heads(grad_own):
    rows = grad_own.shape[0] // SIDE
    return jnp.concatenate(
        [grad_own[0:rows]] + [move_x(grad_own[d * rows : (d + 1) * rows], d) for d in range(1, SIDE)],
        axis=1,
    )


def backward_entry(grad_qkv, grad_hidden, stored, vectors, w_heads):
    residual, normed_all = stored[0:2]
    gain_one = vectors[0]
    grad_normed = scatter_z(local_dot(grad_qkv, w_heads).astype(LOW))
    g_w_heads = tn_dot(grad_qkv, normed_all).astype(LOW)
    g_b_qkv = jnp.sum(grad_qkv.astype(FULL), axis=0)
    grad_residual_part, g_gain_one, g_bias_one = layer_norm_back(grad_normed, residual, gain_one)
    return grad_hidden + grad_residual_part, (g_gain_one, g_bias_one), g_b_qkv, g_w_heads


def per_device(
    inputs,
    segments,
    gain_one,
    bias_one,
    w_qkv,
    b_qv,
    w_out,
    b_out,
    gain_two,
    bias_two,
    w_up,
    b_up,
    w_down,
    b_down,
    cotangent,
):
    here = lax.axis_index("section")
    block = lax.axis_index("ctx")
    spot = lax.axis_index("tensor")
    x_here, z_here = spot // SIDE, spot % SIDE
    row_count, model_width = inputs.shape[2], inputs.shape[3]

    def owner(layer, yes, no):
        return jnp.where(here == layer, yes, no)

    sequence = lax.dynamic_index_in_dim(inputs, here, 0, False)[0].astype(FULL)
    grad_last = lax.dynamic_index_in_dim(cotangent, here, 0, False)[0].astype(FULL)
    grad_last_all = lax.dynamic_index_in_dim(cotangent, here, 0, False)[0]

    gap = jnp.zeros((HEAD_DIM,), LOW)
    biases = jnp.concatenate(
        [b_up[0], gap, b_qv[0, 1], b_qv[0, 0], gap, jnp.zeros((model_width - 512,), LOW)]
    )[None]
    heads_kv = jnp.concatenate(
        [w_qkv[0, :, 1].T, w_qkv[0, :, 2].T, biases, jnp.zeros((15, model_width), LOW)], axis=0
    )
    heads_qo = jnp.concatenate(
        [w_qkv[0, :, 0].T, w_out[0], jnp.zeros((16, model_width), LOW)], axis=0
    )
    heads_qo_other = swap(heads_qo)
    small = jnp.concatenate(
        [gain_one, bias_one, b_out, gain_two, bias_two, b_down, jnp.zeros((2, model_width), LOW)],
        axis=0,
    )
    small_other = swap(small)
    up_own, down_other = w_up[0].T, swap(w_down[0])
    downward = [(x_here - d) % SIDE for d in range(SIDE)]

    def reorder(pieces):
        return [lax.dynamic_index_in_dim(pieces, place, 0, False) for place in downward]

    def half_heads(layer):
        return owner(layer, heads_kv, heads_qo_other)

    def join_heads(layer, mine, theirs):
        key_value, query_out = owner(layer, mine, theirs), owner(layer, theirs, mine)
        whole = jnp.concatenate([key_value[:, :128], query_out[:, :128]], axis=1)
        back = query_out[:, :128].reshape(SIDE * 128, model_width)
        rows = key_value[:, 128, :512].astype(FULL)
        bias_heads = rows[:, 256:].reshape(1, SIDE * TILE)
        bias_up = jnp.concatenate(reorder(rows[:, :256])).reshape(1, SIDE * TILE)
        return (whole.reshape(SIDE * TILE, model_width), back), bias_heads, bias_up

    def gather_whole(half):
        return lax.all_gather(half, "tensor", axis=0, tiled=True, axis_index_groups=X_GROUPS)

    def join_units(layer, mine):
        theirs = swap(mine)
        return owner(layer, mine, theirs), owner(layer, theirs, mine)

    smalls = (owner(0, small, small_other), owner(0, small_other, small))
    vectors = [
        tuple(smalls[layer][row : row + 1].astype(FULL) for row in range(6)) for layer in range(2)
    ]
    normed = layer_norm(sequence, *vectors[0][0:2]).astype(LOW)
    half, normed = tie(half_heads(0), normed)
    mine = jnp.stack([half] + [move_x(half, d) for d in range(1, SIDE)])
    half = owner(0, up_own, down_other)
    normed_all, mine, half, grad_last_all = tie(gather_z(normed), mine, half, gather_z(grad_last_all))
    heads_first, bias_heads_first, bias_up_first = join_heads(0, mine, swap(mine))
    units_first = gather_whole(half)
    heads_last = gather_whole(half_heads(1)).reshape(SIDE, -1, model_width)
    units_last = gather_whole(owner(1, up_own, down_other))
    normed_all, segments = tie(normed_all, segments)
    segment_ids = lax.dynamic_index_in_dim(segments, here, 0, False)
    start_one = jnp.sum((segment_ids < 1).astype(jnp.int32))
    start_two = jnp.sum((segment_ids < 2).astype(jnp.int32))

    lane = jnp.arange(SIDE * TILE) % TILE
    spots = {
        "scalars": jnp.stack([block, x_here, z_here, start_one, start_two]).astype(jnp.int32),
        "scale": jnp.where(lane < 128, 1.0, jnp.where(lane < 192, BASE_TWO_SCALE, 0.0)).astype(FULL),
        "upper": (jnp.arange(SIDE * 128) % 128 >= HEAD_DIM).astype(FULL),
    }

    hidden, kept_heads_first = forward_attention(
        sequence, normed_all, spots, vectors[0], bias_heads_first, *heads_first
    )
    units_first = join_units(0, units_first)
    middle, kept_units_first = forward_hidden_units(hidden, vectors[0], bias_up_first, *units_first)
    mine = jnp.stack(reorder(heads_last))
    middle, mine, theirs = tie(middle, mine, swap(mine))
    heads_last, bias_heads_last, bias_up_last = join_heads(1, mine, theirs)
    middle = middle.astype(LOW).astype(FULL)
    normed_all = gather_z(layer_norm(middle, *vectors[1][0:2]).astype(LOW))
    hidden, kept_heads_last = forward_attention(
        middle, normed_all, spots, vectors[1], bias_heads_last, *heads_last
    )
    units_last = join_units(1, units_last)
    result, kept_units_last = forward_hidden_units(hidden, vectors[1], bias_up_last, *units_last)

    def swap_grads(layer, first, second):
        return owner(layer, first, second), swap(owner(layer, second, first))

    def add_grads(kept, arrived):
        return (kept.astype(FULL) + arrived.astype(FULL)).astype(LOW)

    def scatter_whole(grads):
        return lax.psum_scatter(
            grads, "tensor", scatter_dimension=0, tiled=True, axis_index_groups=X_GROUPS
        )

    def split_heads(g_w_heads, g_w_out):
        heads = g_w_heads.reshape(SIDE, TILE, model_width)
        return heads[:, 0:128], heads[:, 128:256] + g_w_out.reshape(SIDE, 128, model_width)

    turn = jnp.stack(downward)[None, :] == jnp.arange(SIDE)[:, None]

    def pack_vectors(heads, units, g_b_out, g_b_up, g_b_qkv):
        by_turn = jnp.sum(
            jnp.where(turn[:, :, None], g_b_up.reshape(SIDE, 1, TILE), 0.0), axis=0
        )
        return jnp.concatenate(
            [
                jnp.stack([*heads, g_b_out, *units]),
                jnp.concatenate([by_turn, g_b_qkv.reshape(SIDE, TILE)], axis=1).reshape(2, -1),
            ],
            axis=0,
        )

    grad_hidden, vec_units_last, g_b_up_last, g_up, g_down = backward_hidden_units(
        grad_last, grad_last_all, kept_units_last, vectors[1], *units_last
    )
    grad_hidden, units_kept, units_arrived = tie(grad_hidden, *swap_grads(1, g_up, g_down))
    units_sum_last = scatter_whole(add_grads(units_kept, units_arrived))
    grad_mixed, g_b_out_last, g_out = backward_mixed(grad_hidden, kept_heads_last, heads_last[1], spots)
    grad_qkv = spread_heads(backward_heads(attend_back(spots, *kept_heads_last[2:5], grad_mixed)))
    grad_middle, vec_heads_last, g_b_qkv_last, g_heads = backward_entry(
        grad_qkv, grad_hidden, kept_heads_last, vectors[1], heads_last[0]
    )
    heads_kept, heads_arrived = swap_grads(1, *split_heads(g_heads, g_out))

    grad_middle = grad_middle.astype(LOW).astype(FULL)
    grad_down_all, heads_kept, heads_arrived = tie(
        gather_z(grad_middle.astype(LOW)), heads_kept, heads_arrived
    )
    heads_sum_last = scatter_whole(
        jnp.concatenate(reorder(add_grads(heads_kept, heads_arrived)), axis=0)
    )
    grad_hidden, vec_units_first, g_b_up_first, g_up, g_down = backward_hidden_units(
        grad_middle, grad_down_all, kept_units_first, vectors[0], *units_first
    )
    grad_hidden, units_kept, units_arrived, units_sum_last = tie(
        grad_hidden, *swap_grads(0, g_up, g_down), units_sum_last
    )
    units_sum_first = scatter_whole(add_grads(units_kept, units_arrived))
    grad_mixed, g_b_out_first, g_out = backward_mixed(grad_hidden, kept_heads_first, heads_first[1], spots)
    parts = attend_back(spots, *kept_heads_first[2:5], grad_mixed)
    grad_own = backward_heads(parts)
    grad_own, units_sum_first, heads_sum_last = tie(grad_own, units_sum_first, heads_sum_last)
    units_sum_first, units_sum_last, heads_sum_last = lax.psum(
        (units_sum_first, units_sum_last, heads_sum_last), "ctx"
    )
    grad_qkv = spread_heads(grad_own)

    gain_one, bias_one = vectors[0][0:2]
    residual, normed_all = kept_heads_first[0:2]
    grad_normed = local_dot(grad_qkv, heads_first[0])
    g_bias_one = jnp.sum(grad_normed, axis=0)
    g_gain_one = jnp.sum(grad_normed * ((normed_all.astype(FULL) - bias_one) / gain_one), axis=0)
    g_b_qkv_first = jnp.sum(grad_qkv.astype(FULL), axis=0)
    sums_first = pack_vectors(
        (g_gain_one, g_bias_one), vec_units_first, g_b_out_first, g_b_up_first, g_b_qkv_first
    )
    sums_last = pack_vectors(vec_heads_last, vec_units_last, g_b_out_last, g_b_up_last, g_b_qkv_last)
    common = jnp.pad(jnp.concatenate([sums_first[:6], sums_last[:6]]), ((0, 4), (0, 0))).astype(LOW)
    chunks = grad_normed.astype(LOW).reshape(SIDE, row_count, model_width)
    chunks = even_pairs([jnp.concatenate([chunks[d], common], axis=0) for d in range(SIDE)], move_z)
    heads_kept, heads_arrived = swap_grads(0, *split_heads(tn_dot(grad_qkv, normed_all).astype(LOW), g_out))
    halves = add_grads(heads_kept, heads_arrived)
    sums_first = jnp.concatenate([chunks[row_count : row_count + 6], sums_first[6:]])
    sums_last = jnp.concatenate([chunks[row_count + 6 : row_count + 12], sums_last[6:]])
    sums = owner(0, sums_first, sums_last) + swap(owner(0, sums_last, sums_first))
    common = sums[:6].astype(LOW)
    split = sums[6:].reshape(SIDE, 1, 512).astype(LOW)
    packs = [
        jnp.concatenate(
            [
                halves[d],
                common,
                jnp.pad(split[d], ((0, 0), (0, model_width - 512))),
                jnp.zeros((9, model_width), LOW),
            ],
            axis=0,
        )
        for d in range(SIDE)
    ]
    pack = even_sum(even_pairs(packs, move_x).astype(LOW), move_y)
    pack, units_sum_first, units_sum_last, heads_sum_last = tie(
        pack, units_sum_first, units_sum_last, heads_sum_last
    )
    heads_sum_first, pack = pack[:128], pack[128:]
    grad_first = grad_hidden + layer_norm_back(chunks[:row_count], residual, gain_one)[0]

    passed = swap(owner(0, result, grad_first))
    kept = owner(0, grad_first, result)
    boundary = owner(0, jnp.stack([kept, passed]), jnp.stack([passed, kept]))
    boundary = boundary.reshape(1, 2, 1, row_count, model_width)

    units_sum = owner(0, units_sum_first, units_sum_last)
    heads_sum = owner(0, heads_sum_first, heads_sum_last)
    units_theirs = swap(owner(0, units_sum_last, units_sum_first))
    heads_theirs = swap(owner(0, heads_sum_last, heads_sum_first).astype(LOW))
    g_key_value = heads_sum.astype(FULL)
    g_query_out = heads_theirs.astype(FULL)
    g_w_qkv = jnp.stack([g_query_out[0:64].T, g_key_value[0:64].T, g_key_value[64:128].T], axis=1)
    g_b_qv = jnp.stack([pack[6, 384:448], pack[6, 320:384]])
    return (
        boundary,
        pack[0:1],
        pack[1:2],
        g_w_qkv[None],
        g_b_qv[None],
        g_query_out[64:128][None],
        pack[2:3],
        pack[3:4],
        pack[4:5],
        units_sum.astype(FULL).T[None],
        pack[6:7, 0:256],
        units_theirs.astype(FULL)[None],
        pack[5:6],
    )


def solution(mesh):
    return jax.shard_map(
        per_device,
        mesh=mesh,
        in_specs=(
            P(None, "ctx", "tensor", None),
            P(),
            P("section", None),
            P("section", None),
            P("section", None, None, "tensor"),
            P("section", None, "tensor"),
            P("section", "tensor", None),
            P("section", None),
            P("section", None),
            P("section", None),
            P("section", None, "tensor"),
            P("section", "tensor"),
            P("section", "tensor", None),
            P("section", None),
            P(None, "ctx", "tensor", None),
        ),
        out_specs=(
            P("section", None, "ctx", "tensor", None),
            P("section", None),
            P("section", None),
            P("section", None, None, "tensor"),
            P("section", None, "tensor"),
            P("section", "tensor", None),
            P("section", None),
            P("section", None),
            P("section", None),
            P("section", None, "tensor"),
            P("section", "tensor"),
            P("section", "tensor", None),
            P("section", None),
        ),
        check_vma=False,
    )
```
